512 devices in a mesh: dp: 32 (over x, z_lo, core), sample: 4 (over z_hi), mp: 4 (over y).
Axes of the slice: x: 4, y: 4, z: 16 (z_hi: 4, z_lo: 4; z = z_hi * 4 + z_lo), core: 2. Of those that a mesh axis runs over, the one named last changes fastest.
Arguments:
- prefix_hidden: bfloat16 [32, 832, 2048], P('dp', 'sample')
- prefix_kv_weight: bfloat16 [2048, 512], P(None, 'mp'), may hold values from -0.125 to 0.125
- action_hidden: bfloat16 [32, 1200, 1024], P('dp', 'sample'), may hold values from -6 to 6
- query_weight: bfloat16 [1024, 2048], P(None, 'mp'), may hold values from -0.1875 to 0.1875
- action_kv_weight: bfloat16 [1024, 512], replicated, may hold values from -0.1875 to 0.1875
- out_cotangent: bfloat16 [32, 1200, 2048], P('dp', 'sample', 'mp'), may hold values from -96 to 96
- prompt_len: int32 [32], P('dp'), may hold values from 1 to 64, as said below
- view_valid: int32 [32, 3], P('dp'), may hold values from 0 to 1, as said below
Outputs:
- prefix_grad: bfloat16 [32, 832, 2048], P('dp', ('sample', 'mp'))
- kv_weight_update: bfloat16 [2048, 512], P(None, 'mp')
The draws below stay inside these ranges and needn't reach their ends.
Inputs may be any that keep to these rules, and one draw needn't show every extreme that they name: `prompt_len`: observation 0 uses all 64 prompt positions. `view_valid`: the first view of every observation is present.
All inputs are finite; a program needn't handle non-finite values.
Results may differ from the reference program's by a relative error of at most 0.012.
The reference program's roundings to bfloat16 on the way count: a program that leaves them out, or rounds other values in their place, can miss the bound.
Values may be sent and summed in bfloat16 or wider, within the bound.
A program may use at most 64 MiB of HBM per device.

```python
import jax
import jax.numpy as jnp
from jax import lax

D = 2048
HD = 256
DA = 1024
HEADS = 8
VIEWS = 3
VIEW_TOK = 256
PROMPT = 64
HORIZON = 50
PREFIX = 832
ACTIONS = 1200
OBS = 32
N_SAMPLE = 4


def draw_prefix_hidden(key, part):
    key = jax.random.fold_in(key, 11)
    base_key, feature_key, row_key, pair_key = jax.random.split(key, 4)
    full_shape = (OBS, PREFIX, D)
    noise = jax.random.normal(base_key, full_shape, jnp.float32)
    position_ramp = jnp.arange(D, dtype=jnp.float32) / D
    feature_scale = 10.0 ** (0.5 * position_ramp + 0.5 * jax.random.uniform(feature_key, (D,), jnp.float32))
    row_scale = 10.0 ** (0.5 * jax.random.uniform(row_key, (OBS, PREFIX, 1), jnp.float32))
    groups_all = OBS * N_SAMPLE
    pairing = jax.random.permutation(pair_key, groups_all).astype(jnp.int32).reshape(OBS, N_SAMPLE)
    block_of_row = jnp.arange(PREFIX, dtype=jnp.int32) // (PREFIX // N_SAMPLE)
    target = pairing[:, block_of_row]
    feature_block = jnp.arange(D, dtype=jnp.int32) * groups_all // D
    boost = jnp.where(feature_block[None, None, :] == target[:, :, None], 8.0, 1.0)
    result = 0.3 * noise * feature_scale * row_scale * boost
    return result.astype(jnp.bfloat16)


def draw_prompt_len(key, part):
    key = jax.random.fold_in(key, 12)
    lengths = jax.random.randint(key, (OBS,), 1, PROMPT + 1)
    return lengths.at[0].set(PROMPT).astype(jnp.int32)


def draw_view_valid(key, part):
    key = jax.random.fold_in(key, 37)
    flag_key, obs_key, view_key = jax.random.split(key, 3)
    view_flags = jax.random.randint(flag_key, (OBS, VIEWS), 0, 2).astype(jnp.int32)
    missing_obs = jax.random.randint(obs_key, (), 0, OBS)
    missing_view = jax.random.randint(view_key, (), 1, VIEWS)
    obs_range = jnp.arange(OBS, dtype=jnp.int32)[:, None]
    view_range = jnp.arange(VIEWS, dtype=jnp.int32)[None, :]
    hit = (obs_range == missing_obs) & (view_range == missing_view)
    view_flags = jnp.where(hit, 0, view_flags)
    view_flags = jnp.where(view_range == 0, 1, view_flags)
    return view_flags.astype(jnp.int32)


def block_scale(stream_key, extent, pieces, low, largest):
    level = 1.0
    for dim, parts in pieces:
        steps = jax.random.uniform(jax.random.fold_in(jax.random.fold_in(stream_key, 6), dim), (parts,), jnp.float32, low / len(pieces), largest / len(pieces))
        level = level * jnp.repeat(jnp.exp(steps), extent[dim] // parts).reshape((-1,) + (1,) * (len(extent) - 1 - dim))
    return level


def bell_draw(key, extent, scale, bound, cuts=(), kind=jnp.bfloat16):
    values = scale * jax.random.normal(key, extent, jnp.float32)
    if cuts:
        values = values * block_scale(key, extent, cuts, -0.22, 0.18)
    return jnp.clip(values, -bound, bound).astype(kind)


def setup_inputs(seed: int = 0) -> dict:
    splits = jax.random.split(jax.random.key(seed), 9)
    return {
        "prefix_hidden": draw_prefix_hidden(jax.random.fold_in(splits[8], 71), 0),
        "prefix_kv_weight": bell_draw(splits[1], (D, 2 * HD), D ** -0.5, 0.125, ((1, 4),)),
        "action_hidden": bell_draw(splits[2], (OBS, ACTIONS, DA), 1.0, 6.0, ((0, 32), (1, 4))),
        "query_weight": bell_draw(splits[3], (DA, HEADS * HD), DA ** -0.5, 0.1875, ((1, 4),)),
        "action_kv_weight": bell_draw(splits[4], (DA, 2 * HD), DA ** -0.5, 0.1875),
        "out_cotangent": bell_draw(splits[5], (OBS, ACTIONS, HEADS * HD), 16.0, 96.0, ((0, 32), (1, 4), (2, 4))),
        "prompt_len": draw_prompt_len(jax.random.fold_in(splits[8], 71), 0),
        "view_valid": draw_view_valid(jax.random.fold_in(splits[8], 71), 0),
    }


def prefix_valid(length, view_flags, total_rows):
    position = jnp.arange(total_rows, dtype=jnp.int32)
    image_end = view_flags.shape[0] * VIEW_TOK
    view_id = position // VIEW_TOK
    view_range = jnp.arange(view_flags.shape[0], dtype=jnp.int32)
    flag_of = lax.optimization_barrier(jnp.sum(jnp.where(view_id[:, None] == view_range[None, :], view_flags[None, :], 0), axis=1))
    return jnp.where(position < image_end, flag_of == 1, position - image_end < length)

def attention_grads(queries, all_keys, all_values, grad_out, usable):
    row_total = queries.shape[0]
    prefix_rows = usable.shape[0]
    same_draw = jnp.arange(row_total, dtype=jnp.int32) // HORIZON
    allowed = jnp.concatenate([jnp.broadcast_to(usable[None, :], (row_total, prefix_rows)), same_draw[:, None] == same_draw[None, :]], axis=1)
    scaling = HD ** (-0.5)
    scores = jnp.einsum('qhd,kd->hqk', queries.astype(jnp.float32), all_keys.astype(jnp.float32)) * scaling
    row_max = lax.optimization_barrier(jnp.max(jnp.where(allowed[None], scores, -jnp.inf), axis=-1, keepdims=True))
    exponent = jnp.where(allowed[None], jnp.exp(scores - row_max), 0.0)
    softmax = exponent / lax.optimization_barrier(jnp.sum(exponent, axis=-1, keepdims=True))
    d_probs = jnp.einsum('qhd,kd->hqk', grad_out.astype(jnp.float32), all_values.astype(jnp.float32))
    row_dot = lax.optimization_barrier(jnp.sum(softmax * d_probs, axis=-1, keepdims=True))
    d_scores = (softmax * (d_probs - row_dot) * scaling).astype(jnp.bfloat16)
    probs_low = softmax.astype(jnp.bfloat16)
    d_keys = jnp.einsum('hqk,qhd->kd', d_scores[:, :, :prefix_rows].astype(jnp.float32), queries.astype(jnp.float32))
    d_values = jnp.einsum('hqk,qhd->kd', probs_low[:, :, :prefix_rows].astype(jnp.float32), grad_out.astype(jnp.float32))
    return jnp.concatenate([d_keys, d_values], axis=1)

def reference(prefix_hidden, prefix_kv_weight, action_hidden, query_weight, action_kv_weight, out_cotangent, prompt_len, view_valid):

    def one_observation(inputs):
        hidden, actions, cotangent, length, view_flags = inputs
        prefix_kv = jnp.dot(hidden, prefix_kv_weight, preferred_element_type=jnp.float32).astype(jnp.bfloat16)
        queries = jnp.dot(actions, query_weight, preferred_element_type=jnp.float32).astype(jnp.bfloat16)
        queries = queries.reshape(actions.shape[0], HEADS, HD)
        action_kv = jnp.dot(actions, action_kv_weight, preferred_element_type=jnp.float32).astype(jnp.bfloat16)
        all_keys = jnp.concatenate([prefix_kv[:, :HD], action_kv[:, :HD]], axis=0)
        all_values = jnp.concatenate([prefix_kv[:, HD:], action_kv[:, HD:]], axis=0)
        usable = prefix_valid(length, view_flags, PREFIX)
        grad_out = cotangent.reshape(actions.shape[0], HEADS, HD)
        d_prefix = attention_grads(queries, all_keys, all_values, grad_out, usable).astype(jnp.bfloat16)
        input_grad = jnp.dot(d_prefix, prefix_kv_weight.T, preferred_element_type=jnp.float32).astype(jnp.bfloat16)
        weight_term = jnp.dot(hidden.T, d_prefix, preferred_element_type=jnp.float32)
        return (input_grad, weight_term)
    input_grads, weight_terms = lax.map(one_observation, (prefix_hidden, action_hidden, out_cotangent, prompt_len, view_valid))
    weight_grad = lax.optimization_barrier(jnp.sum(weight_terms, axis=0))
    scaling = lax.rsqrt(jnp.mean(weight_grad * weight_grad) + 1e-06)
    return (input_grads, (weight_grad * scaling).astype(jnp.bfloat16))
```

```python
import jax
import jax.numpy as jnp
from jax import lax
from jax.experimental import pallas as pl
from jax.experimental.pallas import tpu as pltpu
from jax.sharding import PartitionSpec as P

BF = jnp.bfloat16
F32 = jnp.float32
D = 2048
HD = 256
ROWS = 208
COLS = 128
ACT = 300
ACTP = 304
QR = 2 * ACTP
VIEW_TOK = 256
VIEWS = 3
HORIZON = 50
NEG = -3.0e38
HALF = ((0, 112), (112, 96))
N_SEMS = 160


def dot(a, b):
    return jnp.dot(a, b, preferred_element_type=F32)


def dot_nt(a, b):
    return lax.dot_general(a, b, (((1,), (1,)), ((), ())), preferred_element_type=F32)


def kernel(
    len_ref, view_ref, hid_h, w_h, act_h, wq_h, wakv_h, cot_h,
    o_grad, o_upd, o_sq,
    hid_v, wg, act_v, wq_v, wakv_v, cot_v, kv, akv, qs, gs, e_s, d_s, ea_s, da_s,
    dkv, st, yb,
    rr, zst, za0, za1, zb0, zb1, zc0, zc1, zsc0, zsc1,
    dres, gbuf, hx, hxt, tf, ts, zr, upd,
    sq, ysq, xs, xsq, ds, dr,
    lsem, ssem, rsem,
):
    dp = lax.axis_index("dp")
    s = lax.axis_index("sample")
    m = lax.axis_index("mp")
    x = dp // 8
    zl = lax.rem(dp, 8) // 2
    c = lax.rem(dp, 2)

    def at(a, k):
        return lax.rem(a + k, 4)

    z = s * 4 + zl

    def dev(kx=0, kz=0, ks=0, km=0, kc=0):
        cc = 1 - c if kc else c
        d = at(x, kx) * 8 + at(zl, kz) * 2 + cc
        return {"dp": d, "sample": at(s, ks), "mp": at(m, km)}

    along_z = [(ks, kz) for ks in (2, 1, 3, 0) for kz in (1, 2, 3, 0) if ks or kz]
    yp, ym = dev(km=1), dev(km=3)
    zp, zm = dev(ks=1), dev(ks=3)
    xp, xm = dev(kx=1), dev(kx=3)
    other = dev(kc=1)

    index = {}
    sent = []

    def number(name):
        return index.setdefault(name, len(index))

    def send(name, src, dst, device):
        i = number(name)
        copy = pltpu.make_async_remote_copy(
            src_ref=src, dst_ref=dst, send_sem=ssem.at[i], recv_sem=rsem.at[i],
            device_id=device, device_id_type=pl.DeviceIdType.MESH,
        )
        copy.start()
        sent.append(copy)

    def recv(name, dst, device=None):
        i = number(name)
        pltpu.make_async_remote_copy(
            src_ref=dst, dst_ref=dst, send_sem=ssem.at[i], recv_sem=rsem.at[i],
            device_id=other if device is None else device,
            device_id_type=pl.DeviceIdType.MESH,
        ).wait_recv()

    def drain(n):
        for copy in sent[:n]:
            copy.wait_send()
        del sent[:n]

    def col(k):
        return pl.ds(pl.multiple_of(at(m, k) * COLS, COLS), COLS)

    loads = [
        pltpu.make_async_copy(hid_h.at[0, 0:112], hid_v.at[0:112], lsem.at[0]),
        pltpu.make_async_copy(w_h, wg.at[:, col(0)], lsem.at[1]),
        pltpu.make_async_copy(act_h.at[0], act_v, lsem.at[2]),
        pltpu.make_async_copy(wq_h, wq_v, lsem.at[3]),
        pltpu.make_async_copy(wakv_h, wakv_v, lsem.at[4]),
        pltpu.make_async_copy(cot_h.at[0], cot_v, lsem.at[5]),
        pltpu.make_async_copy(hid_h.at[0, 112:208], hid_v.at[112:208], lsem.at[6]),
    ]
    for i in (1, 0, 6):
        loads[i].start()

    barrier = pltpu.get_barrier_semaphore()
    peers = [dev(km=k) for k in (1, 2, 3)] + [dev(ks=ks, kz=kz) for ks, kz in along_z] + [other]
    peers += [dev(kx=k, kc=kc) for k in (1, 2, 3) for kc in (0, 1)]
    for peer in peers:
        pl.semaphore_signal(
            barrier, inc=1, device_id=peer, device_id_type=pl.DeviceIdType.MESH
        )

    def kvh(r, h, k):
        r0, n = HALF[h]
        return kv.at[r, pl.ds(r0, n), col(k)]

    def ysend(r):
        block = kv.at[r, :, col(0)]
        for k in (2, 1, 3):
            send(f"y{r}{k}", block, block, dev(km=k))

    def ywait(r):
        for k in (1, 3, 2):
            recv(f"y{r}{k}", kv.at[r, :, col(4 - k)])

    loads[1].wait()
    loads[0].wait()
    for i in (2, 3, 5, 4):
        loads[i].start()
    kv[0, 0:112, col(0)] = dot(hid_v[0:112], wg[:, col(0)]).astype(BF)
    pl.semaphore_wait(barrier, len(peers))
    send("zp0", kvh(0, 0, 0), kvh(3, 0, 0), zp)
    loads[6].wait()
    kv[0, 112:208, col(0)] = dot(hid_v[112:208], wg[:, col(0)]).astype(BF)
    send("zm1", kvh(0, 1, 0), kvh(1, 1, 0), zm)
    send("zp1", kvh(0, 1, 0), kvh(3, 1, 0), zp)
    send("zm0", kvh(0, 0, 0), kvh(1, 0, 0), zm)
    ysend(0)

    def slot(rx, rc):
        return pl.ds((rx * 2 + rc) * ROWS, ROWS)

    def hidden_columns(kx, kc):
        j = at(x, kx) * 2 + (1 - c if kc else c)
        return pl.ds(pl.multiple_of(j * 256, 256), 256)

    def send_hidden(kx):
        for kc in (0, 1):
            send(f"hx{kx}{kc}", hid_v.at[:, hidden_columns(kx, kc)],
                 hx.at[slot(4 - kx, kc)], dev(kx=kx, kc=kc))

    send_hidden(1)
    send_hidden(3)
    send("hx01", hid_v.at[:, hidden_columns(0, 1)], hx.at[slot(0, 1)], other)
    hx[slot(0, 0), :] = hid_v[:, hidden_columns(0, 0)]

    for ref in (qs, gs):
        ref[288:304, :] = jnp.zeros((16, HD), BF)
        ref[592:608, :] = jnp.zeros((16, HD), BF)
    akv[288:304, :] = jnp.zeros((16, 2 * HD), BF)
    loads[2].wait()
    loads[3].wait()
    queries = (dot(act_v[...], wq_v[...]).astype(BF).astype(F32) * (HD**-0.5)).astype(BF)
    qs[0:ACT, :] = queries[:, :HD]
    qs[ACTP : ACTP + ACT, :] = queries[:, HD:]
    loads[4].wait()
    akv[0:ACT, :] = dot(act_v[...], wakv_v[...]).astype(BF)
    loads[5].wait()
    gs[0:ACT, :] = cot_v[:, :HD]
    gs[ACTP : ACTP + ACT, :] = cot_v[:, HD:]

    block_max, block_sum, block_dot = {}, {}, {}

    def attend(r, keys, values, mask, e_ref, d_ref):
        scores = mask(dot_nt(keys, qs[...]))
        top = jnp.max(scores, axis=0, keepdims=True)
        e = jnp.exp(scores - top)
        d = dot_nt(values, gs[...])
        if e_ref is not None:
            e_ref[...] = e
            d_ref[...] = d
        block_max[r] = top
        block_sum[r] = jnp.sum(e, axis=0, keepdims=True)
        block_dot[r] = jnp.sum(e * d, axis=0, keepdims=True)

    def draw(i):
        total = jnp.zeros_like(i)
        for t in range(1, ACTP // HORIZON + 1):
            total = total + jnp.where(i >= t * HORIZON, 1, 0)
        return total

    key_draw = draw(lax.broadcasted_iota(jnp.int32, (ACTP, 1), 0))
    query_index = lax.broadcasted_iota(jnp.int32, (1, QR), 1)
    query_draw = draw(query_index - jnp.where(query_index >= ACTP, ACTP, 0))
    attend(
        "a", akv[:, :HD], akv[:, HD:],
        lambda scores: jnp.where(key_draw == query_draw, scores, NEG), None, None,
    )

    def attend_prefix(r):
        p = at(s, r) * ROWS + lax.broadcasted_iota(jnp.int32, (ROWS, 1), 0)
        usable = jnp.where(p >= VIEWS * VIEW_TOK, jnp.where(p - VIEWS * VIEW_TOK < len_ref[0], 1, 0), 0)
        for v in range(VIEWS):
            inside = jnp.where(p >= v * VIEW_TOK, 1, 0) * jnp.where(p < (v + 1) * VIEW_TOK, 1, 0)
            usable = usable + inside * jnp.where(view_ref[0, v] == 1, 1, 0)
        ceiling = jnp.where(usable > 0, -NEG, NEG)
        attend(
            r, kv[r, :, :HD], kv[r, :, HD:],
            lambda scores: jnp.minimum(scores, ceiling), e_s.at[r], d_s.at[r],
        )

    recv("zp0", kvh(3, 0, 0))
    send("zfp", kvh(3, 0, 0), kvh(2, 0, 0), zp)
    recv("zm1", kvh(1, 1, 0))
    send("zfm", kvh(1, 1, 0), kvh(2, 1, 0), zm)
    recv("zp1", kvh(3, 1, 0))
    ysend(3)
    recv("zm0", kvh(1, 0, 0))
    ysend(1)
    ywait(0)
    attend_prefix(0)
    recv("zfp", kvh(2, 0, 0))
    recv("zfm", kvh(2, 1, 0))
    ysend(2)
    send_hidden(2)
    ywait(3)
    attend_prefix(3)
    ywait(1)
    attend_prefix(1)
    ywait(2)
    attend_prefix(2)

    blocks = ("a", 0, 1, 2, 3)
    top = block_max["a"]
    for r in (0, 1, 2, 3):
        top = jnp.maximum(top, block_max[r])
    factor = {r: jnp.exp(block_max[r] - top) for r in blocks}
    total = sum(factor[r] * block_sum[r] for r in blocks)
    inverse = 1.0 / total
    row_dot = sum(factor[r] * block_dot[r] for r in blocks) * inverse

    def half(h):
        r0, n = HALF[h]
        return pl.ds(r0, n)

    def gradients(r):
        p = e_s[r] * (factor[r] * inverse)
        d = p * (d_s[r] - row_dot)
        dk = dot(d.astype(BF), qs[...])
        dv = dot(p.astype(BF), gs[...])
        dkv[r, :, :HD] = dk
        dkv[r, :, HD:] = dv
        st[r, :, :HD] = dk.astype(BF)
        st[r, :, HD:] = dv.astype(BF)
        for k in (2, 1, 3):
            send(f"r{r}{k}", st.at[r, :, col(k)], yb.at[r, 3 - k], dev(km=k))

    def finish(r):
        piece = dkv[r, :, col(0)]
        for k in (1, 3, 2):
            recv(f"r{r}{k}", yb.at[r, 3 - k])
            piece = piece + yb[r, 3 - k].astype(F32)
        rr[r] = piece
        if r:
            zst[r] = piece.astype(BF)

    gradients(2)
    gradients(1)
    gradients(3)
    gradients(0)
    finish(2)
    send("zap", zst.at[2, half(0)], za0, zp)
    send("zam", zst.at[2, half(1)], za1, zm)
    finish(1)
    send("zbp", zst.at[1, half(1)], zb1, zp)
    finish(3)
    send("zbm", zst.at[3, half(0)], zb0, zm)
    early = len(sent)
    recv("zap", za0)
    zsc0[...] = (rr[1, half(0), :] + za0[...].astype(F32)).astype(BF)
    send("zcp", zsc0, zc0, zp)
    recv("zam", za1)
    zsc1[...] = (rr[3, half(1), :] + za1[...].astype(F32)).astype(BF)
    send("zcm", zsc1, zc1, zm)

    def wpart(q, k):
        return wg.at[pl.ds(pl.multiple_of(c * 1024 + q * 512, 512), 512), col(k)]

    send("wp0", wpart(0, 0), wpart(0, 0), yp)
    send("wm1", wpart(1, 0), wpart(1, 0), ym)
    send("wp1", wpart(1, 0), wpart(1, 0), yp)
    send("wm0", wpart(0, 0), wpart(0, 0), ym)

    finish(0)
    for kx in (1, 3, 2):
        for kc in (0, 1):
            recv(f"hx{kx}{kc}", hx.at[slot(4 - kx, kc)])
    recv("hx01", hx.at[slot(0, 1)])
    hxt[...] = hx[...].T
    drain(early)

    def gh(rx, rc, h):
        r0, n = HALF[h]
        return gbuf.at[pl.ds((rx * 2 + rc) * ROWS + r0, n)]

    recv("zbm", zb0)
    recv("zcp", zc0)
    dres[half(0), :] = rr[0, half(0), :] + zb0[...].astype(F32) + zc0[...].astype(F32)
    gbuf[half(0), :] = dres[half(0), :].astype(BF)
    for kx in (2, 1, 3):
        send(f"g{kx}0", gh(0, 0, 0), gh(4 - kx, 0, 0), dev(kx=kx))
    send("gc00", gh(0, 0, 0), gh(0, 1, 0), other)
    recv("zbp", zb1)
    recv("zcm", zc1)
    dres[half(1), :] = rr[0, half(1), :] + zb1[...].astype(F32) + zc1[...].astype(F32)
    gbuf[half(1), :] = dres[half(1), :].astype(BF)
    for kx in (2, 1, 3):
        send(f"g{kx}1", gh(0, 0, 1), gh(4 - kx, 0, 1), dev(kx=kx))
    send("gc01", gh(0, 0, 1), gh(0, 1, 1), other)

    for k in range(4):
        ds[k, 0:52, :] = dres[52 * k : 52 * k + 52, :].astype(BF)
        ds[k, 48:64, :] = jnp.where(
            lax.broadcasted_iota(jnp.int32, (16, COLS), 0) < 4, ds[k, 48:64, :].astype(F32), 0.0
        ).astype(BF)
    for k in (1, 3, 2):
        send(f"dy{k}", ds.at[at(m, k)], dr.at[:, col(0)], dev(km=k))
    dr[:, col(0)] = ds[m]

    for h in (0, 1):
        for kx in (1, 3, 2):
            recv(f"g{kx}{h}", gh(4 - kx, 0, h))
            send(f"gc{kx}{h}", gh(4 - kx, 0, h), gh(4 - kx, 1, h), other)
    recv("wp0", wpart(0, 3))
    send("wfp", wpart(0, 3), wpart(0, 3), yp)
    recv("wm1", wpart(1, 1))
    send("wfm", wpart(1, 1), wpart(1, 1), ym)
    recv("gc00", gh(0, 1, 0))
    recv("gc01", gh(0, 1, 1))
    for h in (0, 1):
        for kx in (1, 3, 2):
            recv(f"gc{kx}{h}", gh(4 - kx, 1, h))

    tf[...] = dot(hxt[...], gbuf[...])
    ts[...] = tf[...].astype(BF)

    def rows(start, n):
        return pl.ds(pl.multiple_of(start, n), n)

    def place(ks, kz):
        return (at(s, ks) * 4 + at(zl, kz)) * 16

    for i, (ks, kz) in enumerate(along_z):
        send(f"t{ks}{kz}", ts.at[rows(place(ks, kz), 16)], zr.at[i], dev(ks=ks, kz=kz))
    recv("wp1", wpart(1, 3))
    recv("wm0", wpart(0, 1))
    recv("wfp", wpart(0, 2))
    recv("wfm", wpart(1, 2))
    for k in (1, 2, 3):
        piece = wg.at[pl.ds(pl.multiple_of(c * 1024, 1024), 1024), col(k)]
        send(f"wc{k}", piece, piece, other)

    late = len(sent)
    base = (x * 2 + c) * 256
    piece = tf[rows(z * 16, 16), :]
    for i, (ks, kz) in reversed(list(enumerate(along_z))):
        recv(f"t{ks}{kz}", zr.at[i])
        piece = piece + zr[i].astype(F32)
    mine = upd.at[rows(base + z * 16, 16)]
    mine[...] = piece.astype(BF)
    for ks, kz in along_z:
        send(f"u{ks}{kz}", mine, mine, dev(ks=ks, kz=kz))
    drain(late)

    def u64(kx, ks):
        return upd.at[rows(at(x, kx) * 512 + c * 256 + at(s, ks) * 64, 64)]

    def u256(kx, kc):
        return upd.at[rows(at(x, kx) * 512 + (1 - c if kc else c) * 256, 256)]

    for ks in (0, 1, 3, 2):
        for kz in (1, 2, 3, 0):
            if ks or kz:
                source = rows(base + place(4 - ks, 4 - kz), 16)
                recv(f"u{ks}{kz}", upd.at[source])
        for kx in (2, 1, 3):
            send(f"ux{kx}{ks}", u64(0, 4 - ks), u64(0, 4 - ks), dev(kx=kx))
    send("uc0", u256(0, 0), u256(0, 0), other)
    own = upd[rows(base, 256), :].astype(F32)
    sq[...] = jnp.sum((own * own).reshape(32, 8, COLS), axis=0)
    for k in (1, 3, 2):
        send(f"sy{k}", sq, ysq.at[3 - k], dev(km=k))

    for k in (1, 2, 3):
        piece = wg.at[pl.ds(pl.multiple_of((1 - c) * 1024, 1024), 1024), col(k)]
        recv(f"wc{k}", piece)
    for k in (1, 3, 2):
        recv(f"dy{k}", dr.at[:, col(4 - k)])
    for j in range(4):
        part = dot_nt(dr[...], wg[512 * j : 512 * j + 512, :])
        o_grad[0, :, 512 * j : 512 * j + 512] = part[:52].astype(BF)

    for k in (1, 3, 2):
        recv(f"sy{k}", ysq.at[3 - k])
    xs[...] = sq[...] + ysq[0] + ysq[1] + ysq[2]
    across = [(kx, kc) for kx in (2, 1, 3, 0) for kc in (1, 0) if kx or kc]
    for i, (kx, kc) in enumerate(across):
        send(f"sx{kx}{kc}", xs, xsq.at[i], dev(kx=kx, kc=kc))
    for kx in (1, 3, 2):
        for ks in (0, 1, 3, 2):
            recv(f"ux{kx}{ks}", u64(4 - kx, 4 - ks))
        send(f"uc{kx}", u256(4 - kx, 0), u256(4 - kx, 0), other)
    everything = xs[...]
    for i, (kx, kc) in enumerate(across):
        recv(f"sx{kx}{kc}", xsq.at[i])
        everything = everything + xsq[i]
    o_sq[...] = everything
    recv("uc0", u256(0, 1))
    for kx in (1, 3, 2):
        recv(f"uc{kx}", u256(4 - kx, 1))
    o_upd[...] = upd[...]
    drain(len(sent))


def write_results(grad_ref, raw_ref, sq_ref, o_grad, o_upd):
    o_grad[...] = grad_ref[...]
    scale = lax.rsqrt(jnp.sum(sq_ref[...]) / (D * 2 * HD) + 1e-06)
    o_upd[...] = (raw_ref[...].astype(F32) * scale).astype(BF)


def per_device(
    prefix_hidden, prefix_kv_weight, action_hidden, query_weight, action_kv_weight,
    out_cotangent, prompt_len, view_valid,
):
    vm = pltpu.VMEM
    scratch = [
        vm((ROWS, D), BF), vm((D, 512), BF), vm((ACT, 1024), BF), vm((1024, 512), BF),
        vm((1024, 512), BF), vm((ACT, 512), BF), vm((4, ROWS, 512), BF), vm((ACTP, 512), BF),
        vm((QR, HD), BF), vm((QR, HD), BF), vm((4, ROWS, QR), F32), vm((4, ROWS, QR), F32),
        vm((8, 128), F32), vm((8, 128), F32),
        vm((4, ROWS, 512), F32), vm((4, ROWS, 512), BF),
        vm((4, 3, ROWS, COLS), BF),
        vm((4, ROWS, COLS), F32), vm((4, ROWS, COLS), BF),
        vm((112, COLS), BF), vm((96, COLS), BF), vm((112, COLS), BF), vm((96, COLS), BF),
        vm((112, COLS), BF), vm((96, COLS), BF), vm((112, COLS), BF), vm((96, COLS), BF),
        vm((ROWS, COLS), F32), vm((8 * ROWS, COLS), BF), vm((8 * ROWS, 256), BF),
        vm((256, 8 * ROWS), BF), vm((256, COLS), F32), vm((256, COLS), BF),
        vm((15, 16, COLS), BF), vm((D, COLS), BF),
        vm((8, 128), F32), vm((3, 8, 128), F32), vm((8, 128), F32), vm((7, 8, 128), F32),
        vm((4, 64, COLS), BF), vm((64, 512), BF),
        pltpu.SemaphoreType.DMA((7,)),
        pltpu.SemaphoreType.DMA((N_SEMS,)), pltpu.SemaphoreType.DMA((N_SEMS,)),
    ]
    smem = pl.BlockSpec(memory_space=pltpu.SMEM)
    hbm = pl.BlockSpec(memory_space=pltpu.HBM)
    grad, raw, squares = pl.pallas_call(
        kernel,
        out_shape=(
            jax.ShapeDtypeStruct((1, 52, D), BF),
            jax.ShapeDtypeStruct((D, COLS), BF),
            jax.ShapeDtypeStruct((8, 128), F32),
        ),
        in_specs=[smem, smem] + [hbm] * 6,
        out_specs=(pl.BlockSpec(memory_space=pltpu.VMEM),) * 3,
        scratch_shapes=scratch,
        compiler_params=pltpu.CompilerParams(
            collective_id=0, has_side_effects=True, vmem_limit_bytes=40 * 1024 * 1024
        ),
    )(
        prompt_len, view_valid, *[pltpu.with_memory_space_constraint(v, pltpu.HBM) for v in (prefix_hidden, prefix_kv_weight, action_hidden, query_weight, action_kv_weight, out_cotangent)])
    return pl.pallas_call(
        write_results,
        out_shape=(
            jax.ShapeDtypeStruct((1, 52, D), BF),
            jax.ShapeDtypeStruct((D, COLS), BF),
        ),
        in_specs=[pl.BlockSpec(memory_space=pltpu.VMEM)] * 3,
        out_specs=(pl.BlockSpec(memory_space=pltpu.VMEM),) * 2,
        compiler_params=pltpu.CompilerParams(vmem_limit_bytes=40 * 1024 * 1024),
    )(grad, raw, squares)


def solution(mesh):
    return jax.shard_map(
        per_device,
        mesh=mesh,
        in_specs=(
            P("dp", "sample", None),
            P(None, "mp"),
            P("dp", "sample", None),
            P(None, "mp"),
            P(),
            P("dp", "sample", "mp"),
            P("dp"),
            P("dp", None),
        ),
        out_specs=(P("dp", ("sample", "mp"), None), P(None, "mp")),
        check_vma=False,
    )
```

```python
import jax
import jax.numpy as jnp
from jax import lax
from jax.experimental import pallas as pl
from jax.experimental.pallas import tpu as pltpu
from jax.sharding import PartitionSpec as P

BF = jnp.bfloat16
F32 = jnp.float32
D = 2048
HD = 256
ROWS = 208
COLS = 128
ACT = 300
ACTP = 304
QR = 2 * ACTP
VIEW_TOK = 256
VIEWS = 3
HORIZON = 50
NEG = -3.0e38
HALF = ((0, 112), (112, 96))
PART = ((0, 64), (64, 48), (112, 48), (160, 48))
N_SEMS = 160


def dot(a, b):
    return jnp.dot(a, b, preferred_element_type=F32)


def wide(*pieces):
    return jnp.concatenate(pieces, axis=1)


def dot_nt(a, b):
    return lax.dot_general(a, b, (((1,), (1,)), ((), ())), preferred_element_type=F32)


def kernel(
    len_ref, view_ref, hid_h, w_h, act_h, wq_h, wakv_h, cot_h,
    o_grad, o_upd, o_sq,
    hid_v, wg, act_v, wq_v, wakv_v, cot_v, kv, akv, qs, gs, e_s, d_s,
    dkv, st, yb,
    rr, zst, za0, za1, zb0, zb1, zc0, zc1, zsc0, zsc1,
    dres, gbuf, hx, hxt, tf, ts, zr, upd,
    sq, ysq, xs, xsq, ds, dr,
    lsem, ssem, rsem,
):
    dp = lax.axis_index("dp")
    s = lax.axis_index("sample")
    m = lax.axis_index("mp")
    x = dp // 8
    zl = lax.rem(dp, 8) // 2
    c = lax.rem(dp, 2)

    def at(a, k):
        return lax.rem(a + k, 4)

    z = s * 4 + zl

    def dev(kx=0, kz=0, ks=0, km=0, kc=0):
        cc = 1 - c if kc else c
        d = at(x, kx) * 8 + at(zl, kz) * 2 + cc
        return {"dp": d, "sample": at(s, ks), "mp": at(m, km)}

    along_z = [(ks, kz) for ks in (2, 1, 3, 0) for kz in (1, 2, 3, 0) if ks or kz]
    yp, ym = dev(km=1), dev(km=3)
    zp, zm = dev(ks=1), dev(ks=3)
    xp, xm = dev(kx=1), dev(kx=3)
    other = dev(kc=1)

    index = {}
    sent = []

    def number(name):
        return index.setdefault(name, len(index))

    def send(name, src, dst, device):
        i = number(name)
        copy = pltpu.make_async_remote_copy(
            src_ref=src, dst_ref=dst, send_sem=ssem.at[i], recv_sem=rsem.at[i],
            device_id=device, device_id_type=pl.DeviceIdType.MESH,
        )
        copy.start()
        sent.append(copy)

    def recv(name, dst, device=None):
        i = number(name)
        pltpu.make_async_remote_copy(
            src_ref=dst, dst_ref=dst, send_sem=ssem.at[i], recv_sem=rsem.at[i],
            device_id=other if device is None else device,
            device_id_type=pl.DeviceIdType.MESH,
        ).wait_recv()

    def drain(n):
        for copy in sent[:n]:
            copy.wait_send()
        del sent[:n]

    loads = [
        pltpu.make_async_copy(hid_h.at[0, 0:112], hid_v.at[0:112], lsem.at[0]),
        pltpu.make_async_copy(w_h, wg.at[m], lsem.at[1]),
        pltpu.make_async_copy(act_h.at[0], act_v, lsem.at[2]),
        pltpu.make_async_copy(wq_h, wq_v, lsem.at[3]),
        pltpu.make_async_copy(wakv_h, wakv_v, lsem.at[4]),
        pltpu.make_async_copy(cot_h.at[0], cot_v, lsem.at[5]),
        pltpu.make_async_copy(hid_h.at[0, 112:208], hid_v.at[112:208], lsem.at[6]),
    ]
    for i in (1, 0, 6):
        loads[i].start()

    barrier = pltpu.get_barrier_semaphore()
    peers = [dev(km=k) for k in (1, 2, 3)] + [dev(ks=ks, kz=kz) for ks, kz in along_z] + [other]
    peers += [dev(kx=k, kc=kc) for k in (1, 2, 3) for kc in (0, 1)]
    for peer in peers:
        pl.semaphore_signal(
            barrier, inc=1, device_id=peer, device_id_type=pl.DeviceIdType.MESH
        )

    def kvp(r, i):
        r0, n = PART[i]
        return kv.at[r, m, pl.ds(r0, n)]

    def ysend(r):
        block = kv.at[r, m]
        for k in (2, 1, 3):
            send(f"y{r}{k}", block, block, dev(km=k))

    def ywait(r):
        for k in (1, 3, 2):
            recv(f"y{r}{k}", kv.at[r, at(m, 4 - k)])

    loads[1].wait()
    loads[0].wait()
    for i in (2, 3, 5, 4):
        loads[i].start()
    kv[0, m, 0:112, :] = dot(hid_v[0:112], wg[m]).astype(BF)
    pl.semaphore_wait(barrier, len(peers))
    for i in (0, 1):
        send(f"zp{i}", kvp(0, i), kvp(3, i), zp)
    loads[6].wait()
    kv[0, m, 112:208, :] = dot(hid_v[112:208], wg[m]).astype(BF)
    for i in (2, 3):
        send(f"zm{i}", kvp(0, i), kvp(1, i), zm)
    for i, j in ((2, 0), (3, 1)):
        send(f"zp{i}", kvp(0, i), kvp(3, i), zp)
        send(f"zm{j}", kvp(0, j), kvp(1, j), zm)
    ysend(0)

    def slot(rx, rc):
        return pl.ds((rx * 2 + rc) * ROWS, ROWS)

    def hidden_columns(kx, kc):
        j = at(x, kx) * 2 + (1 - c if kc else c)
        return pl.ds(pl.multiple_of(j * 256, 256), 256)

    def send_hidden(kx):
        for kc in (0, 1):
            send(f"hx{kx}{kc}", hid_v.at[:, hidden_columns(kx, kc)],
                 hx.at[slot(4 - kx, kc)], dev(kx=kx, kc=kc))

    send_hidden(1)
    send_hidden(3)
    send("hx01", hid_v.at[:, hidden_columns(0, 1)], hx.at[slot(0, 1)], other)
    hx[slot(0, 0), :] = hid_v[:, hidden_columns(0, 0)]

    for ref in (qs, gs):
        ref[288:304, :] = jnp.zeros((16, HD), BF)
        ref[592:608, :] = jnp.zeros((16, HD), BF)
    akv[288:304, :] = jnp.zeros((16, 2 * HD), BF)
    loads[2].wait()
    loads[3].wait()
    queries = (dot(act_v[...], wq_v[...]).astype(BF).astype(F32) * (HD**-0.5)).astype(BF)
    qs[0:ACT, :] = queries[:, :HD]
    qs[ACTP : ACTP + ACT, :] = queries[:, HD:]
    loads[4].wait()
    akv[0:ACT, :] = dot(act_v[...], wakv_v[...]).astype(BF)
    loads[5].wait()
    gs[0:ACT, :] = cot_v[:, :HD]
    gs[ACTP : ACTP + ACT, :] = cot_v[:, HD:]

    block_max, block_sum, block_dot = {}, {}, {}

    def attend(r, keys, values, mask, e_ref, d_ref):
        scores = mask(dot_nt(keys, qs[...]))
        top = jnp.max(scores, axis=0, keepdims=True)
        e = jnp.exp(scores - top)
        d = dot_nt(values, gs[...])
        if e_ref is not None:
            e_ref[...] = e
            d_ref[...] = d
        block_max[r] = top
        block_sum[r] = jnp.sum(e, axis=0, keepdims=True)
        block_dot[r] = jnp.sum(e * d, axis=0, keepdims=True)

    def draw(i):
        total = jnp.zeros_like(i)
        for t in range(1, ACTP // HORIZON + 1):
            total = total + jnp.where(i >= t * HORIZON, 1, 0)
        return total

    key_draw = draw(lax.broadcasted_iota(jnp.int32, (ACTP, 1), 0))
    query_index = lax.broadcasted_iota(jnp.int32, (1, QR), 1)
    query_draw = draw(query_index - jnp.where(query_index >= ACTP, ACTP, 0))
    attend(
        "a", akv[:, :HD], akv[:, HD:],
        lambda scores: jnp.where(key_draw == query_draw, scores, NEG), None, None,
    )

    def attend_prefix(r):
        p = at(s, r) * ROWS + lax.broadcasted_iota(jnp.int32, (ROWS, 1), 0)
        usable = jnp.where(p >= VIEWS * VIEW_TOK, jnp.where(p - VIEWS * VIEW_TOK < len_ref[0], 1, 0), 0)
        for v in range(VIEWS):
            inside = jnp.where(p >= v * VIEW_TOK, 1, 0) * jnp.where(p < (v + 1) * VIEW_TOK, 1, 0)
            usable = usable + inside * jnp.where(view_ref[0, v] == 1, 1, 0)
        ceiling = jnp.where(usable > 0, -NEG, NEG)
        attend(
            r, wide(kv[r, 0], kv[r, 1]), wide(kv[r, 2], kv[r, 3]),
            lambda scores: jnp.minimum(scores, ceiling), e_s.at[r], d_s.at[r],
        )

    for i, j in ((0, 2), (1, 3)):
        recv(f"zp{i}", kvp(3, i))
        send(f"zf{i}", kvp(3, i), kvp(2, i), zp)
        recv(f"zm{j}", kvp(1, j))
        send(f"zf{j}", kvp(1, j), kvp(2, j), zm)
    for i in (2, 3):
        recv(f"zp{i}", kvp(3, i))
    ysend(3)
    for i in (0, 1):
        recv(f"zm{i}", kvp(1, i))
    ysend(1)
    ywait(0)
    attend_prefix(0)
    for i in (0, 2, 1, 3):
        recv(f"zf{i}", kvp(2, i))
    ysend(2)
    send_hidden(2)
    ywait(3)
    attend_prefix(3)
    ywait(1)
    attend_prefix(1)
    ywait(2)
    attend_prefix(2)

    blocks = ("a", 0, 1, 2, 3)
    top = block_max["a"]
    for r in (0, 1, 2, 3):
        top = jnp.maximum(top, block_max[r])
    factor = {r: jnp.exp(block_max[r] - top) for r in blocks}
    total = sum(factor[r] * block_sum[r] for r in blocks)
    inverse = 1.0 / total
    row_dot = sum(factor[r] * block_dot[r] for r in blocks) * inverse

    def half(h):
        r0, n = HALF[h]
        return pl.ds(r0, n)

    def gradients(r):
        p = e_s[r] * (factor[r] * inverse)
        d = p * (d_s[r] - row_dot)
        dk = dot(d.astype(BF), qs[...])
        dv = dot(p.astype(BF), gs[...])
        for k in range(4):
            half_block = (dk, dv)[k // 2][:, (k % 2) * COLS : (k % 2 + 1) * COLS]
            dkv[r, k] = half_block
            st[r, k] = half_block.astype(BF)
        for k in (2, 1, 3):
            send(f"r{r}{k}", st.at[r, at(m, k)], yb.at[r, 3 - k], dev(km=k))

    def finish(r):
        piece = dkv[r, m]
        for k in (1, 3, 2):
            recv(f"r{r}{k}", yb.at[r, 3 - k])
            piece = piece + yb[r, 3 - k].astype(F32)
        rr[r] = piece
        if r:
            zst[r] = piece.astype(BF)

    gradients(2)
    gradients(1)
    gradients(3)
    gradients(0)
    finish(2)
    send("zap", zst.at[2, half(0)], za0, zp)
    send("zam", zst.at[2, half(1)], za1, zm)
    finish(1)
    send("zbp", zst.at[1, half(1)], zb1, zp)
    finish(3)
    send("zbm", zst.at[3, half(0)], zb0, zm)
    early = len(sent)
    recv("zap", za0)
    zsc0[...] = (rr[1, half(0), :] + za0[...].astype(F32)).astype(BF)
    send("zcp", zsc0, zc0, zp)
    recv("zam", za1)
    zsc1[...] = (rr[3, half(1), :] + za1[...].astype(F32)).astype(BF)
    send("zcm", zsc1, zc1, zm)

    def wpart(q, k):
        return wg.at[at(m, k), pl.ds(pl.multiple_of(c * 1024 + q * 512, 512), 512)]

    send("wp0", wpart(0, 0), wpart(0, 0), yp)
    send("wm1", wpart(1, 0), wpart(1, 0), ym)
    send("wp1", wpart(1, 0), wpart(1, 0), yp)
    send("wm0", wpart(0, 0), wpart(0, 0), ym)

    finish(0)
    for kx in (1, 3, 2):
        for kc in (0, 1):
            recv(f"hx{kx}{kc}", hx.at[slot(4 - kx, kc)])
    recv("hx01", hx.at[slot(0, 1)])
    hxt[...] = hx[...].T
    drain(early)

    def gh(rx, rc, h):
        r0, n = HALF[h]
        return gbuf.at[pl.ds((rx * 2 + rc) * ROWS + r0, n)]

    recv("zbm", zb0)
    recv("zcp", zc0)
    dres[half(0), :] = rr[0, half(0), :] + zb0[...].astype(F32) + zc0[...].astype(F32)
    gbuf[half(0), :] = dres[half(0), :].astype(BF)
    for kx in (2, 1, 3):
        send(f"g{kx}0", gh(0, 0, 0), gh(4 - kx, 0, 0), dev(kx=kx))
    send("gc00", gh(0, 0, 0), gh(0, 1, 0), other)
    recv("zbp", zb1)
    recv("zcm", zc1)
    dres[half(1), :] = rr[0, half(1), :] + zb1[...].astype(F32) + zc1[...].astype(F32)
    gbuf[half(1), :] = dres[half(1), :].astype(BF)
    for kx in (2, 1, 3):
        send(f"g{kx}1", gh(0, 0, 1), gh(4 - kx, 0, 1), dev(kx=kx))
    send("gc01", gh(0, 0, 1), gh(0, 1, 1), other)

    for k in range(4):
        ds[k, 0:52, :] = dres[52 * k : 52 * k + 52, :].astype(BF)
        ds[k, 48:64, :] = jnp.where(
            lax.broadcasted_iota(jnp.int32, (16, COLS), 0) < 4, ds[k, 48:64, :].astype(F32), 0.0
        ).astype(BF)
    for k in (1, 3, 2):
        send(f"dy{k}", ds.at[at(m, k)], dr.at[m], dev(km=k))
    dr[m] = ds[m]

    for h in (0, 1):
        for kx in (1, 3, 2):
            recv(f"g{kx}{h}", gh(4 - kx, 0, h))
            send(f"gc{kx}{h}", gh(4 - kx, 0, h), gh(4 - kx, 1, h), other)
    recv("wp0", wpart(0, 3))
    send("wfp", wpart(0, 3), wpart(0, 3), yp)
    recv("wm1", wpart(1, 1))
    send("wfm", wpart(1, 1), wpart(1, 1), ym)
    recv("gc00", gh(0, 1, 0))
    recv("gc01", gh(0, 1, 1))
    for h in (0, 1):
        for kx in (1, 3, 2):
            recv(f"gc{kx}{h}", gh(4 - kx, 1, h))

    tf[...] = dot(hxt[...], gbuf[...])
    ts[...] = tf[...].astype(BF)

    def rows(start, n):
        return pl.ds(pl.multiple_of(start, n), n)

    def place(ks, kz):
        return (at(s, ks) * 4 + at(zl, kz)) * 16

    for i, (ks, kz) in enumerate(along_z):
        send(f"t{ks}{kz}", ts.at[rows(place(ks, kz), 16)], zr.at[i], dev(ks=ks, kz=kz))
    recv("wp1", wpart(1, 3))
    recv("wm0", wpart(0, 1))
    recv("wfp", wpart(0, 2))
    recv("wfm", wpart(1, 2))
    for k in (1, 2, 3):
        piece = wg.at[at(m, k), pl.ds(pl.multiple_of(c * 1024, 1024), 1024)]
        send(f"wc{k}", piece, piece, other)

    late = len(sent)
    base = (x * 2 + c) * 256
    piece = tf[rows(z * 16, 16), :]
    for i, (ks, kz) in reversed(list(enumerate(along_z))):
        recv(f"t{ks}{kz}", zr.at[i])
        piece = piece + zr[i].astype(F32)
    mine = upd.at[rows(base + z * 16, 16)]
    mine[...] = piece.astype(BF)
    for ks, kz in along_z:
        send(f"u{ks}{kz}", mine, mine, dev(ks=ks, kz=kz))
    drain(late)

    def u64(kx, ks):
        return upd.at[rows(at(x, kx) * 512 + c * 256 + at(s, ks) * 64, 64)]

    def u256(kx, kc):
        return upd.at[rows(at(x, kx) * 512 + (1 - c if kc else c) * 256, 256)]

    for ks in (0, 1, 3, 2):
        for kz in (1, 2, 3, 0):
            if ks or kz:
                source = rows(base + place(4 - ks, 4 - kz), 16)
                recv(f"u{ks}{kz}", upd.at[source])
        for kx in (2, 1, 3):
            send(f"ux{kx}{ks}", u64(0, 4 - ks), u64(0, 4 - ks), dev(kx=kx))
    send("uc0", u256(0, 0), u256(0, 0), other)
    own = upd[rows(base, 256), :].astype(F32)
    sq[...] = jnp.sum((own * own).reshape(32, 8, COLS), axis=0)
    for k in (1, 3, 2):
        send(f"sy{k}", sq, ysq.at[3 - k], dev(km=k))

    for k in (1, 2, 3):
        piece = wg.at[at(m, k), pl.ds(pl.multiple_of((1 - c) * 1024, 1024), 1024)]
        recv(f"wc{k}", piece)
    for k in (1, 3, 2):
        recv(f"dy{k}", dr.at[at(m, 4 - k)])
    for j in range(4):
        weight = wide(*[wg[k, 512 * j : 512 * j + 512, :] for k in range(4)])
        part = dot_nt(wide(dr[0], dr[1], dr[2], dr[3]), weight)
        o_grad[0, :, 512 * j : 512 * j + 512] = part[:52].astype(BF)

    for k in (1, 3, 2):
        recv(f"sy{k}", ysq.at[3 - k])
    xs[...] = sq[...] + ysq[0] + ysq[1] + ysq[2]
    across = [(kx, kc) for kx in (2, 1, 3, 0) for kc in (1, 0) if kx or kc]
    for i, (kx, kc) in enumerate(across):
        send(f"sx{kx}{kc}", xs, xsq.at[i], dev(kx=kx, kc=kc))
    for kx in (1, 3, 2):
        for ks in (0, 1, 3, 2):
            recv(f"ux{kx}{ks}", u64(4 - kx, 4 - ks))
        send(f"uc{kx}", u256(4 - kx, 0), u256(4 - kx, 0), other)
    everything = xs[...]
    for i, (kx, kc) in enumerate(across):
        recv(f"sx{kx}{kc}", xsq.at[i])
        everything = everything + xsq[i]
    o_sq[...] = everything
    recv("uc0", u256(0, 1))
    for kx in (1, 3, 2):
        recv(f"uc{kx}", u256(4 - kx, 1))
    o_upd[...] = upd[...]
    drain(len(sent))


def write_results(grad_ref, raw_ref, sq_ref, o_grad, o_upd):
    o_grad[...] = grad_ref[...]
    scale = lax.rsqrt(jnp.sum(sq_ref[...]) / (D * 2 * HD) + 1e-06)
    o_upd[...] = (raw_ref[...].astype(F32) * scale).astype(BF)


def per_device(
    prefix_hidden, prefix_kv_weight, action_hidden, query_weight, action_kv_weight,
    out_cotangent, prompt_len, view_valid,
):
    vm = pltpu.VMEM
    scratch = [
        vm((ROWS, D), BF), vm((4, D, COLS), BF), vm((ACT, 1024), BF), vm((1024, 512), BF),
        vm((1024, 512), BF), vm((ACT, 512), BF), vm((4, 4, ROWS, COLS), BF), vm((ACTP, 512), BF),
        vm((QR, HD), BF), vm((QR, HD), BF), vm((4, ROWS, QR), F32), vm((4, ROWS, QR), F32),
        vm((4, 4, ROWS, COLS), F32), vm((4, 4, ROWS, COLS), BF),
        vm((4, 3, ROWS, COLS), BF),
        vm((4, ROWS, COLS), F32), vm((4, ROWS, COLS), BF),
        vm((112, COLS), BF), vm((96, COLS), BF), vm((112, COLS), BF), vm((96, COLS), BF),
        vm((112, COLS), BF), vm((96, COLS), BF), vm((112, COLS), BF), vm((96, COLS), BF),
        vm((ROWS, COLS), F32), vm((8 * ROWS, COLS), BF), vm((8 * ROWS, 256), BF),
        vm((256, 8 * ROWS), BF), vm((256, COLS), F32), vm((256, COLS), BF),
        vm((15, 16, COLS), BF), vm((D, COLS), BF),
        vm((8, 128), F32), vm((3, 8, 128), F32), vm((8, 128), F32), vm((7, 8, 128), F32),
        vm((4, 64, COLS), BF), vm((4, 64, COLS), BF),
        pltpu.SemaphoreType.DMA((7,)),
        pltpu.SemaphoreType.DMA((N_SEMS,)), pltpu.SemaphoreType.DMA((N_SEMS,)),
    ]
    smem = pl.BlockSpec(memory_space=pltpu.SMEM)
    hbm = pl.BlockSpec(memory_space=pltpu.HBM)
    grad, raw, squares = pl.pallas_call(
        kernel,
        out_shape=(
            jax.ShapeDtypeStruct((1, 52, D), BF),
            jax.ShapeDtypeStruct((D, COLS), BF),
            jax.ShapeDtypeStruct((8, 128), F32),
        ),
        in_specs=[smem, smem] + [hbm] * 6,
        out_specs=(pl.BlockSpec(memory_space=pltpu.VMEM),) * 3,
        scratch_shapes=scratch,
        compiler_params=pltpu.CompilerParams(
            collective_id=0, has_side_effects=True, vmem_limit_bytes=40 * 1024 * 1024
        ),
    )(
        prompt_len, view_valid, *[pltpu.with_memory_space_constraint(v, pltpu.HBM) for v in (prefix_hidden, prefix_kv_weight, action_hidden, query_weight, action_kv_weight, out_cotangent)])
    return pl.pallas_call(
        write_results,
        out_shape=(
            jax.ShapeDtypeStruct((1, 52, D), BF),
            jax.ShapeDtypeStruct((D, COLS), BF),
        ),
        in_specs=[pl.BlockSpec(memory_space=pltpu.VMEM)] * 3,
        out_specs=(pl.BlockSpec(memory_space=pltpu.VMEM),) * 2,
        compiler_params=pltpu.CompilerParams(vmem_limit_bytes=40 * 1024 * 1024),
    )(grad, raw, squares)


def solution(mesh):
    return jax.shard_map(
        per_device,
        mesh=mesh,
        in_specs=(
            P("dp", "sample", None),
            P(None, "mp"),
            P("dp", "sample", None),
            P(None, "mp"),
            P(),
            P("dp", "sample", "mp"),
            P("dp"),
            P("dp", None),
        ),
        out_specs=(P("dp", ("sample", "mp"), None), P(None, "mp")),
        check_vma=False,
    )
```

```python
import jax
import jax.numpy as jnp
from jax import lax
from jax.experimental import pallas as pl
from jax.experimental.pallas import tpu as pltpu
from jax.sharding import PartitionSpec as P

BF = jnp.bfloat16
F32 = jnp.float32
D = 2048
HD = 256
ROWS = 208
COLS = 128
ACT = 300
ACTP = 304
QR = 2 * ACTP
VIEW_TOK = 256
VIEWS = 3
HORIZON = 50
NEG = -3.0e38
HALF = ((0, 112), (112, 96))
PART = ((0, 64), (64, 48), (112, 48), (160, 48))
N_SEMS = 160


def dot(a, b):
    return jnp.dot(a, b, preferred_element_type=F32)


def wide(*pieces):
    return jnp.concatenate(pieces, axis=1)


def dot_nt(a, b):
    return lax.dot_general(a, b, (((1,), (1,)), ((), ())), preferred_element_type=F32)


def kernel(
    len_ref, view_ref, hid_h, w_h, act_h, wq_h, wakv_h, cot_h,
    o_grad, o_upd, o_sq,
    hid_v, wg, act_v, wq_v, wakv_v, cot_v, kv, akv, qs, gs, qt, gt, e_s, d_s,
    dkv, st, yb,
    rr, zst, za0, za1, zb0, zb1, zc0, zc1, zsc0, zsc1,
    dres, gbuf, hx, hxt, tf, ts, zr, upd,
    sq, ysq, xs, xsq, ds, dr,
    lsem, ssem, rsem,
):
    dp = lax.axis_index("dp")
    s = lax.axis_index("sample")
    m = lax.axis_index("mp")
    x = dp // 8
    zl = lax.rem(dp, 8) // 2
    c = lax.rem(dp, 2)

    def at(a, k):
        return lax.rem(a + k, 4)

    z = s * 4 + zl

    def dev(kx=0, kz=0, ks=0, km=0, kc=0):
        cc = 1 - c if kc else c
        d = at(x, kx) * 8 + at(zl, kz) * 2 + cc
        return {"dp": d, "sample": at(s, ks), "mp": at(m, km)}

    along_z = [(ks, kz) for ks in (2, 1, 3, 0) for kz in (1, 2, 3, 0) if ks or kz]
    yp, ym = dev(km=1), dev(km=3)
    zp, zm = dev(ks=1), dev(ks=3)
    xp, xm = dev(kx=1), dev(kx=3)
    other = dev(kc=1)

    index = {}
    sent = []

    def number(name):
        return index.setdefault(name, len(index))

    def send(name, src, dst, device):
        i = number(name)
        copy = pltpu.make_async_remote_copy(
            src_ref=src, dst_ref=dst, send_sem=ssem.at[i], recv_sem=rsem.at[i],
            device_id=device, device_id_type=pl.DeviceIdType.MESH,
        )
        copy.start()
        sent.append(copy)

    def recv(name, dst, device=None):
        i = number(name)
        pltpu.make_async_remote_copy(
            src_ref=dst, dst_ref=dst, send_sem=ssem.at[i], recv_sem=rsem.at[i],
            device_id=other if device is None else device,
            device_id_type=pl.DeviceIdType.MESH,
        ).wait_recv()

    def drain(n):
        for copy in sent[:n]:
            copy.wait_send()
        del sent[:n]

    loads = [
        pltpu.make_async_copy(hid_h.at[0, 0:112], hid_v.at[0:112], lsem.at[0]),
        pltpu.make_async_copy(w_h, wg.at[m], lsem.at[1]),
        pltpu.make_async_copy(act_h.at[0], act_v, lsem.at[2]),
        pltpu.make_async_copy(wq_h, wq_v, lsem.at[3]),
        pltpu.make_async_copy(wakv_h, wakv_v, lsem.at[4]),
        pltpu.make_async_copy(cot_h.at[0], cot_v, lsem.at[5]),
        pltpu.make_async_copy(hid_h.at[0, 112:208], hid_v.at[112:208], lsem.at[6]),
    ]
    for i in (1, 0, 6):
        loads[i].start()

    barrier = pltpu.get_barrier_semaphore()
    peers = [dev(km=k) for k in (1, 2, 3)] + [dev(ks=ks, kz=kz) for ks, kz in along_z] + [other]
    peers += [dev(kx=k, kc=kc) for k in (1, 2, 3) for kc in (0, 1)]
    for peer in peers:
        pl.semaphore_signal(
            barrier, inc=1, device_id=peer, device_id_type=pl.DeviceIdType.MESH
        )

    def kvp(r, i):
        r0, n = PART[i]
        return kv.at[r, m, pl.ds(r0, n)]

    def ysend(r):
        block = kv.at[r, m]
        for k in (2, 1, 3):
            send(f"y{r}{k}", block, block, dev(km=k))

    def ywait(r):
        for k in (1, 3, 2):
            recv(f"y{r}{k}", kv.at[r, at(m, 4 - k)])

    loads[1].wait()
    loads[0].wait()
    for i in (2, 3, 5, 4):
        loads[i].start()
    kv[0, m, 0:112, :] = dot(hid_v[0:112], wg[m]).astype(BF)
    pl.semaphore_wait(barrier, len(peers))
    for i in (0, 1):
        send(f"zp{i}", kvp(0, i), kvp(3, i), zp)
    loads[6].wait()
    kv[0, m, 112:208, :] = dot(hid_v[112:208], wg[m]).astype(BF)
    for i in (2, 3):
        send(f"zm{i}", kvp(0, i), kvp(1, i), zm)
    for i, j in ((2, 0), (3, 1)):
        send(f"zp{i}", kvp(0, i), kvp(3, i), zp)
        send(f"zm{j}", kvp(0, j), kvp(1, j), zm)
    ysend(0)

    def slot(rx, rc):
        return pl.ds((rx * 2 + rc) * ROWS, ROWS)

    def hidden_columns(kx, kc):
        j = at(x, kx) * 2 + (1 - c if kc else c)
        return pl.ds(pl.multiple_of(j * 256, 256), 256)

    def send_hidden(kx):
        for kc in (0, 1):
            send(f"hx{kx}{kc}", hid_v.at[:, hidden_columns(kx, kc)],
                 hx.at[slot(4 - kx, kc)], dev(kx=kx, kc=kc))

    send_hidden(1)
    send_hidden(3)
    send("hx01", hid_v.at[:, hidden_columns(0, 1)], hx.at[slot(0, 1)], other)
    hx[slot(0, 0), :] = hid_v[:, hidden_columns(0, 0)]

    for ref in (qs, gs):
        ref[288:304, :] = jnp.zeros((16, HD), BF)
        ref[592:608, :] = jnp.zeros((16, HD), BF)
    akv[288:304, :] = jnp.zeros((16, 2 * HD), BF)
    loads[2].wait()
    loads[3].wait()
    queries = (dot(act_v[...], wq_v[...]).astype(BF).astype(F32) * (HD**-0.5)).astype(BF)
    qs[0:ACT, :] = queries[:, :HD]
    qs[ACTP : ACTP + ACT, :] = queries[:, HD:]
    loads[4].wait()
    akv[0:ACT, :] = dot(act_v[...], wakv_v[...]).astype(BF)
    loads[5].wait()
    gs[0:ACT, :] = cot_v[:, :HD]
    gs[ACTP : ACTP + ACT, :] = cot_v[:, HD:]

    qt[...] = qs[...].T
    gt[...] = gs[...].T

    block_max, block_sum, block_dot = {}, {}, {}

    def attend(r, keys, values, mask, e_ref, d_ref):
        scores = mask(dot(keys, qt[...]))
        top = jnp.max(scores, axis=0, keepdims=True)
        e = jnp.exp(scores - top)
        d = dot(values, gt[...])
        if e_ref is not None:
            e_ref[...] = e
            d_ref[...] = d
        block_max[r] = top
        block_sum[r] = jnp.sum(e, axis=0, keepdims=True)
        block_dot[r] = jnp.sum(e * d, axis=0, keepdims=True)

    def draw(i):
        total = jnp.zeros_like(i)
        for t in range(1, ACTP // HORIZON + 1):
            total = total + jnp.where(i >= t * HORIZON, 1, 0)
        return total

    for i, j in ((0, 2), (1, 3)):
        recv(f"zp{i}", kvp(3, i))
        send(f"zf{i}", kvp(3, i), kvp(2, i), zp)
        recv(f"zm{j}", kvp(1, j))
        send(f"zf{j}", kvp(1, j), kvp(2, j), zm)

    key_draw = draw(lax.broadcasted_iota(jnp.int32, (ACTP, 1), 0))
    query_index = lax.broadcasted_iota(jnp.int32, (1, QR), 1)
    query_draw = draw(query_index - jnp.where(query_index >= ACTP, ACTP, 0))
    attend(
        "a", akv[:, :HD], akv[:, HD:],
        lambda scores: jnp.where(key_draw == query_draw, scores, NEG), None, None,
    )

    def attend_prefix(r):
        p = at(s, r) * ROWS + lax.broadcasted_iota(jnp.int32, (ROWS, 1), 0)
        usable = jnp.where(p >= VIEWS * VIEW_TOK, jnp.where(p - VIEWS * VIEW_TOK < len_ref[0], 1, 0), 0)
        for v in range(VIEWS):
            inside = jnp.where(p >= v * VIEW_TOK, 1, 0) * jnp.where(p < (v + 1) * VIEW_TOK, 1, 0)
            usable = usable + inside * jnp.where(view_ref[0, v] == 1, 1, 0)
        ceiling = jnp.where(usable > 0, -NEG, NEG)
        attend(
            r, wide(kv[r, 0], kv[r, 1]), wide(kv[r, 2], kv[r, 3]),
            lambda scores: jnp.minimum(scores, ceiling), e_s.at[r], d_s.at[r],
        )

    for i in (2, 3):
        recv(f"zp{i}", kvp(3, i))
    ysend(3)
    for i in (0, 1):
        recv(f"zm{i}", kvp(1, i))
    ysend(1)
    ywait(0)
    attend_prefix(0)
    for i in (0, 2, 1, 3):
        recv(f"zf{i}", kvp(2, i))
    ysend(2)
    send_hidden(2)
    ywait(3)
    attend_prefix(3)
    ywait(1)
    attend_prefix(1)
    ywait(2)
    attend_prefix(2)

    blocks = ("a", 0, 1, 2, 3)
    top = block_max["a"]
    for r in (0, 1, 2, 3):
        top = jnp.maximum(top, block_max[r])
    factor = {r: jnp.exp(block_max[r] - top) for r in blocks}
    total = sum(factor[r] * block_sum[r] for r in blocks)
    inverse = 1.0 / total
    row_dot = sum(factor[r] * block_dot[r] for r in blocks) * inverse

    def half(h):
        r0, n = HALF[h]
        return pl.ds(r0, n)

    def gradients(r):
        p = e_s[r] * (factor[r] * inverse)
        d = p * (d_s[r] - row_dot)
        dk = dot(d.astype(BF), qs[...])
        dv = dot(p.astype(BF), gs[...])
        for k in range(4):
            half_block = (dk, dv)[k // 2][:, (k % 2) * COLS : (k % 2 + 1) * COLS]
            dkv[r, k] = half_block
            st[r, k] = half_block.astype(BF)
        for k in (2, 1, 3):
            send(f"r{r}{k}", st.at[r, at(m, k)], yb.at[r, 3 - k], dev(km=k))

    def finish(r):
        piece = dkv[r, m]
        for k in (1, 3, 2):
            recv(f"r{r}{k}", yb.at[r, 3 - k])
            piece = piece + yb[r, 3 - k].astype(F32)
        rr[r] = piece
        if r:
            zst[r] = piece.astype(BF)

    gradients(2)
    gradients(1)
    gradients(3)
    gradients(0)
    finish(2)
    send("zap", zst.at[2, half(0)], za0, zp)
    send("zam", zst.at[2, half(1)], za1, zm)
    finish(1)
    send("zbp", zst.at[1, half(1)], zb1, zp)
    finish(3)
    send("zbm", zst.at[3, half(0)], zb0, zm)
    early = len(sent)
    recv("zap", za0)
    zsc0[...] = (rr[1, half(0), :] + za0[...].astype(F32)).astype(BF)
    send("zcp", zsc0, zc0, zp)
    recv("zam", za1)
    zsc1[...] = (rr[3, half(1), :] + za1[...].astype(F32)).astype(BF)
    send("zcm", zsc1, zc1, zm)

    def wpart(q, k):
        return wg.at[at(m, k), pl.ds(pl.multiple_of(c * 1024 + q * 512, 512), 512)]

    send("wp0", wpart(0, 0), wpart(0, 0), yp)
    send("wm1", wpart(1, 0), wpart(1, 0), ym)
    send("wp1", wpart(1, 0), wpart(1, 0), yp)
    send("wm0", wpart(0, 0), wpart(0, 0), ym)

    finish(0)
    for kx in (1, 3, 2):
        for kc in (0, 1):
            recv(f"hx{kx}{kc}", hx.at[slot(4 - kx, kc)])
    recv("hx01", hx.at[slot(0, 1)])
    hxt[...] = hx[...].T
    drain(early)

    def gh(rx, rc, h):
        r0, n = HALF[h]
        return gbuf.at[pl.ds((rx * 2 + rc) * ROWS + r0, n)]

    recv("zbm", zb0)
    recv("zcp", zc0)
    dres[half(0), :] = rr[0, half(0), :] + zb0[...].astype(F32) + zc0[...].astype(F32)
    gbuf[half(0), :] = dres[half(0), :].astype(BF)
    for kx in (2, 1, 3):
        send(f"g{kx}0", gh(0, 0, 0), gh(4 - kx, 0, 0), dev(kx=kx))
    send("gc00", gh(0, 0, 0), gh(0, 1, 0), other)
    recv("zbp", zb1)
    recv("zcm", zc1)
    dres[half(1), :] = rr[0, half(1), :] + zb1[...].astype(F32) + zc1[...].astype(F32)
    gbuf[half(1), :] = dres[half(1), :].astype(BF)
    for kx in (2, 1, 3):
        send(f"g{kx}1", gh(0, 0, 1), gh(4 - kx, 0, 1), dev(kx=kx))
    send("gc01", gh(0, 0, 1), gh(0, 1, 1), other)

    for k in range(4):
        ds[k, 0:52, :] = dres[52 * k : 52 * k + 52, :].astype(BF)
        ds[k, 48:64, :] = jnp.where(
            lax.broadcasted_iota(jnp.int32, (16, COLS), 0) < 4, ds[k, 48:64, :].astype(F32), 0.0
        ).astype(BF)
    for k in (1, 3, 2):
        send(f"dy{k}", ds.at[at(m, k)], dr.at[m], dev(km=k))
    dr[m] = ds[m]

    for h in (0, 1):
        for kx in (1, 3, 2):
            recv(f"g{kx}{h}", gh(4 - kx, 0, h))
            send(f"gc{kx}{h}", gh(4 - kx, 0, h), gh(4 - kx, 1, h), other)
    recv("wp0", wpart(0, 3))
    send("wfp", wpart(0, 3), wpart(0, 3), yp)
    recv("wm1", wpart(1, 1))
    send("wfm", wpart(1, 1), wpart(1, 1), ym)
    recv("gc00", gh(0, 1, 0))
    recv("gc01", gh(0, 1, 1))
    for h in (0, 1):
        for kx in (1, 3, 2):
            recv(f"gc{kx}{h}", gh(4 - kx, 1, h))

    tf[...] = dot(hxt[...], gbuf[...])
    ts[...] = tf[...].astype(BF)

    def rows(start, n):
        return pl.ds(pl.multiple_of(start, n), n)

    def place(ks, kz):
        return (at(s, ks) * 4 + at(zl, kz)) * 16

    for i, (ks, kz) in enumerate(along_z):
        send(f"t{ks}{kz}", ts.at[rows(place(ks, kz), 16)], zr.at[i], dev(ks=ks, kz=kz))
    recv("wp1", wpart(1, 3))
    recv("wm0", wpart(0, 1))
    recv("wfp", wpart(0, 2))
    recv("wfm", wpart(1, 2))
    for k in (1, 2, 3):
        piece = wg.at[at(m, k), pl.ds(pl.multiple_of(c * 1024, 1024), 1024)]
        send(f"wc{k}", piece, piece, other)

    late = len(sent)
    base = (x * 2 + c) * 256
    piece = tf[rows(z * 16, 16), :]
    for i, (ks, kz) in reversed(list(enumerate(along_z))):
        recv(f"t{ks}{kz}", zr.at[i])
        piece = piece + zr[i].astype(F32)
    mine = upd.at[rows(base + z * 16, 16)]
    mine[...] = piece.astype(BF)
    for ks, kz in along_z:
        send(f"u{ks}{kz}", mine, mine, dev(ks=ks, kz=kz))
    drain(late)

    for k in (1, 2, 3):
        piece = wg.at[at(m, k), pl.ds(pl.multiple_of((1 - c) * 1024, 1024), 1024)]
        recv(f"wc{k}", piece)
    for k in (1, 3, 2):
        recv(f"dy{k}", dr.at[at(m, 4 - k)])
    for j in range(4):
        weight = wide(*[wg[k, 512 * j : 512 * j + 512, :] for k in range(4)])
        part = dot_nt(wide(dr[0], dr[1], dr[2], dr[3]), weight)
        o_grad[0, :, 512 * j : 512 * j + 512] = part[:52].astype(BF)

    def u64(kx, ks):
        return upd.at[rows(at(x, kx) * 512 + c * 256 + at(s, ks) * 64, 64)]

    def u256(kx, kc):
        return upd.at[rows(at(x, kx) * 512 + (1 - c if kc else c) * 256, 256)]

    for ks in (0, 1, 3, 2):
        for kz in (1, 2, 3, 0):
            if ks or kz:
                source = rows(base + place(4 - ks, 4 - kz), 16)
                recv(f"u{ks}{kz}", upd.at[source])
        for kx in (2, 1, 3):
            send(f"ux{kx}{ks}", u64(0, 4 - ks), u64(0, 4 - ks), dev(kx=kx))
    send("uc0", u256(0, 0), u256(0, 0), other)
    own = upd[rows(base, 256), :].astype(F32)
    sq[...] = jnp.sum((own * own).reshape(32, 8, COLS), axis=0)
    for k in (1, 3, 2):
        send(f"sy{k}", sq, ysq.at[3 - k], dev(km=k))

    for k in (1, 3, 2):
        recv(f"sy{k}", ysq.at[3 - k])
    xs[...] = sq[...] + ysq[0] + ysq[1] + ysq[2]
    across = [(kx, kc) for kx in (2, 1, 3, 0) for kc in (1, 0) if kx or kc]
    for i, (kx, kc) in enumerate(across):
        send(f"sx{kx}{kc}", xs, xsq.at[i], dev(kx=kx, kc=kc))
    for kx in (1, 3, 2):
        for ks in (0, 1, 3, 2):
            recv(f"ux{kx}{ks}", u64(4 - kx, 4 - ks))
        send(f"uc{kx}", u256(4 - kx, 0), u256(4 - kx, 0), other)
    everything = xs[...]
    for i, (kx, kc) in enumerate(across):
        recv(f"sx{kx}{kc}", xsq.at[i])
        everything = everything + xsq[i]
    o_sq[...] = everything
    drain(len(sent) - 3)
    recv("uc0", u256(0, 1))
    for kx in (1, 3, 2):
        recv(f"uc{kx}", u256(4 - kx, 1))
    o_upd[...] = upd[...]
    drain(len(sent))


def write_results(grad_ref, raw_ref, sq_ref, o_grad, o_upd):
    o_grad[...] = grad_ref[...]
    scale = lax.rsqrt(jnp.sum(sq_ref[...]) / (D * 2 * HD) + 1e-06)
    o_upd[...] = (raw_ref[...].astype(F32) * scale).astype(BF)


def per_device(
    prefix_hidden, prefix_kv_weight, action_hidden, query_weight, action_kv_weight,
    out_cotangent, prompt_len, view_valid,
):
    vm = pltpu.VMEM
    scratch = [
        vm((ROWS, D), BF), vm((4, D, COLS), BF), vm((ACT, 1024), BF), vm((1024, 512), BF),
        vm((1024, 512), BF), vm((ACT, 512), BF), vm((4, 4, ROWS, COLS), BF), vm((ACTP, 512), BF),
        vm((QR, HD), BF), vm((QR, HD), BF), vm((HD, QR), BF), vm((HD, QR), BF),
        vm((4, ROWS, QR), F32), vm((4, ROWS, QR), F32),
        vm((4, 4, ROWS, COLS), F32), vm((4, 4, ROWS, COLS), BF),
        vm((4, 3, ROWS, COLS), BF),
        vm((4, ROWS, COLS), F32), vm((4, ROWS, COLS), BF),
        vm((112, COLS), BF), vm((96, COLS), BF), vm((112, COLS), BF), vm((96, COLS), BF),
        vm((112, COLS), BF), vm((96, COLS), BF), vm((112, COLS), BF), vm((96, COLS), BF),
        vm((ROWS, COLS), F32), vm((8 * ROWS, COLS), BF), vm((8 * ROWS, 256), BF),
        vm((256, 8 * ROWS), BF), vm((256, COLS), F32), vm((256, COLS), BF),
        vm((15, 16, COLS), BF), vm((D, COLS), BF),
        vm((8, 128), F32), vm((3, 8, 128), F32), vm((8, 128), F32), vm((7, 8, 128), F32),
        vm((4, 64, COLS), BF), vm((4, 64, COLS), BF),
        pltpu.SemaphoreType.DMA((7,)),
        pltpu.SemaphoreType.DMA((N_SEMS,)), pltpu.SemaphoreType.DMA((N_SEMS,)),
    ]
    smem = pl.BlockSpec(memory_space=pltpu.SMEM)
    hbm = pl.BlockSpec(memory_space=pltpu.HBM)
    grad, raw, squares = pl.pallas_call(
        kernel,
        out_shape=(
            jax.ShapeDtypeStruct((1, 52, D), BF),
            jax.ShapeDtypeStruct((D, COLS), BF),
            jax.ShapeDtypeStruct((8, 128), F32),
        ),
        in_specs=[smem, smem] + [hbm] * 6,
        out_specs=(pl.BlockSpec(memory_space=pltpu.VMEM),) * 3,
        scratch_shapes=scratch,
        compiler_params=pltpu.CompilerParams(
            collective_id=0, has_side_effects=True, vmem_limit_bytes=40 * 1024 * 1024
        ),
    )(
        prompt_len, view_valid, *[pltpu.with_memory_space_constraint(v, pltpu.HBM) for v in (prefix_hidden, prefix_kv_weight, action_hidden, query_weight, action_kv_weight, out_cotangent)])
    return pl.pallas_call(
        write_results,
        out_shape=(
            jax.ShapeDtypeStruct((1, 52, D), BF),
            jax.ShapeDtypeStruct((D, COLS), BF),
        ),
        in_specs=[pl.BlockSpec(memory_space=pltpu.VMEM)] * 3,
        out_specs=(pl.BlockSpec(memory_space=pltpu.VMEM),) * 2,
        compiler_params=pltpu.CompilerParams(vmem_limit_bytes=40 * 1024 * 1024),
    )(grad, raw, squares)


def solution(mesh):
    return jax.shard_map(
        per_device,
        mesh=mesh,
        in_specs=(
            P("dp", "sample", None),
            P(None, "mp"),
            P("dp", "sample", None),
            P(None, "mp"),
            P(),
            P("dp", "sample", "mp"),
            P("dp"),
            P("dp", None),
        ),
        out_specs=(P("dp", ("sample", "mp"), None), P(None, "mp")),
        check_vma=False,
    )
```

```python
import jax
import jax.numpy as jnp
from jax import lax
from jax.experimental import pallas as pl
from jax.experimental.pallas import tpu as pltpu
from jax.sharding import PartitionSpec as P

BF = jnp.bfloat16
F32 = jnp.float32
D = 2048
HD = 256
ROWS = 208
COLS = 128
ACT = 300
ACTP = 304
QR = 2 * ACTP
VIEW_TOK = 256
VIEWS = 3
HORIZON = 50
NEG = -3.0e38
N_SEMS = 160


def dot(a, b):
    return jnp.dot(a, b, preferred_element_type=F32)


def wide(*pieces):
    return jnp.concatenate(pieces, axis=1)


def dot_nt(a, b):
    return lax.dot_general(a, b, (((1,), (1,)), ((), ())), preferred_element_type=F32)


def kernel(
    len_ref, view_ref, hid_h, w_h, act_h, wq_h, wakv_h, cot_h,
    o_grad, o_upd, o_sq,
    hid_v, wg, act_v, wq_v, wakv_v, cot_v, kv, akv, qs, gs, qt, gt, e_s, d_s,
    dkv, st, yb,
    rr, zst, zb,
    dres, gbuf, hx, hxt, tf, ts, zr, upd,
    sq, ysq, xs, xsq, ds, dr,
    lsem, ssem, rsem,
):
    dp = lax.axis_index("dp")
    s = lax.axis_index("sample")
    m = lax.axis_index("mp")
    x = dp // 8
    zl = lax.rem(dp, 8) // 2
    c = lax.rem(dp, 2)

    def at(a, k):
        return lax.rem(a + k, 4)

    z = s * 4 + zl

    def dev(kx=0, kz=0, ks=0, km=0, kc=0):
        cc = 1 - c if kc else c
        d = at(x, kx) * 8 + at(zl, kz) * 2 + cc
        return {"dp": d, "sample": at(s, ks), "mp": at(m, km)}

    along_z = [(ks, kz) for ks in (2, 1, 3, 0) for kz in (1, 2, 3, 0) if ks or kz]
    other = dev(kc=1)

    index = {}
    sent = []

    def number(name):
        return index.setdefault(name, len(index))

    def send(name, src, dst, device):
        i = number(name)
        copy = pltpu.make_async_remote_copy(
            src_ref=src, dst_ref=dst, send_sem=ssem.at[i], recv_sem=rsem.at[i],
            device_id=device, device_id_type=pl.DeviceIdType.MESH,
        )
        copy.start()
        sent.append(copy)

    def recv(name, dst, device=None):
        i = number(name)
        pltpu.make_async_remote_copy(
            src_ref=dst, dst_ref=dst, send_sem=ssem.at[i], recv_sem=rsem.at[i],
            device_id=other if device is None else device,
            device_id_type=pl.DeviceIdType.MESH,
        ).wait_recv()

    def drain(n):
        for copy in sent[:n]:
            copy.wait_send()
        del sent[:n]

    loads = [
        pltpu.make_async_copy(hid_h.at[0, 0:112], hid_v.at[0:112], lsem.at[0]),
        pltpu.make_async_copy(w_h, wg.at[m], lsem.at[1]),
        pltpu.make_async_copy(act_h.at[0], act_v, lsem.at[2]),
        pltpu.make_async_copy(wq_h, wq_v, lsem.at[3]),
        pltpu.make_async_copy(wakv_h, wakv_v, lsem.at[4]),
        pltpu.make_async_copy(cot_h.at[0], cot_v, lsem.at[5]),
        pltpu.make_async_copy(hid_h.at[0, 112:208], hid_v.at[112:208], lsem.at[6]),
    ]
    for i in (1, 0, 6):
        loads[i].start()

    barrier = pltpu.get_barrier_semaphore()
    peers = [dev(km=k) for k in (1, 2, 3)] + [dev(ks=ks, kz=kz) for ks, kz in along_z] + [other]
    peers += [dev(kx=k, kc=kc) for k in (1, 2, 3) for kc in (0, 1)]
    for peer in peers:
        pl.semaphore_signal(
            barrier, inc=1, device_id=peer, device_id_type=pl.DeviceIdType.MESH
        )

    def ysend(r):
        block = kv.at[r, m]
        for k in (2, 1, 3):
            send(f"y{r}{k}", block, block, dev(km=k))

    def ywait(r):
        for k in (1, 3, 2):
            recv(f"y{r}{k}", kv.at[r, at(m, 4 - k)])

    loads[1].wait()
    loads[0].wait()
    for i in (2, 3, 5, 4):
        loads[i].start()
    loads[6].wait()
    kv[0, m] = dot(hid_v[...], wg[m]).astype(BF)
    pl.semaphore_wait(barrier, len(peers))
    for k in (2, 1, 3):
        send(f"z{k}", kv.at[0, m], kv.at[4 - k, m], dev(ks=k))
    ysend(0)

    def slot(rx, rc):
        return pl.ds((rx * 2 + rc) * ROWS, ROWS)

    def hidden_columns(kx, kc):
        j = at(x, kx) * 2 + (1 - c if kc else c)
        return pl.ds(pl.multiple_of(j * 256, 256), 256)

    def send_hidden(kx):
        for kc in (0, 1):
            send(f"hx{kx}{kc}", hid_v.at[:, hidden_columns(kx, kc)],
                 hx.at[slot(4 - kx, kc)], dev(kx=kx, kc=kc))

    send_hidden(1)
    send_hidden(3)
    send("hx01", hid_v.at[:, hidden_columns(0, 1)], hx.at[slot(0, 1)], other)
    hx[slot(0, 0), :] = hid_v[:, hidden_columns(0, 0)]

    for ref in (qs, gs):
        ref[288:304, :] = jnp.zeros((16, HD), BF)
        ref[592:608, :] = jnp.zeros((16, HD), BF)
    akv[288:304, :] = jnp.zeros((16, 2 * HD), BF)
    loads[2].wait()
    loads[3].wait()
    queries = (dot(act_v[...], wq_v[...]).astype(BF).astype(F32) * (HD**-0.5)).astype(BF)
    qs[0:ACT, :] = queries[:, :HD]
    qs[ACTP : ACTP + ACT, :] = queries[:, HD:]
    loads[4].wait()
    akv[0:ACT, :] = dot(act_v[...], wakv_v[...]).astype(BF)
    loads[5].wait()
    gs[0:ACT, :] = cot_v[:, :HD]
    gs[ACTP : ACTP + ACT, :] = cot_v[:, HD:]

    qt[...] = qs[...].T
    gt[...] = gs[...].T

    block_max, block_sum, block_dot = {}, {}, {}

    def attend(r, keys, values, mask, e_ref, d_ref):
        scores = mask(dot(keys, qt[...]))
        top = jnp.max(scores, axis=0, keepdims=True)
        e = jnp.exp(scores - top)
        d = dot(values, gt[...])
        if e_ref is not None:
            e_ref[...] = e
            d_ref[...] = d
        block_max[r] = top
        block_sum[r] = jnp.sum(e, axis=0, keepdims=True)
        block_dot[r] = jnp.sum(e * d, axis=0, keepdims=True)

    def draw(i):
        total = jnp.zeros_like(i)
        for t in range(1, ACTP // HORIZON + 1):
            total = total + jnp.where(i >= t * HORIZON, 1, 0)
        return total

    key_draw = draw(lax.broadcasted_iota(jnp.int32, (ACTP, 1), 0))
    query_index = lax.broadcasted_iota(jnp.int32, (1, QR), 1)
    query_draw = draw(query_index - jnp.where(query_index >= ACTP, ACTP, 0))
    attend(
        "a", akv[:, :HD], akv[:, HD:],
        lambda scores: jnp.where(key_draw == query_draw, scores, NEG), None, None,
    )

    def attend_prefix(r):
        p = at(s, r) * ROWS + lax.broadcasted_iota(jnp.int32, (ROWS, 1), 0)
        usable = jnp.where(p >= VIEWS * VIEW_TOK, jnp.where(p - VIEWS * VIEW_TOK < len_ref[0], 1, 0), 0)
        for v in range(VIEWS):
            inside = jnp.where(p >= v * VIEW_TOK, 1, 0) * jnp.where(p < (v + 1) * VIEW_TOK, 1, 0)
            usable = usable + inside * jnp.where(view_ref[0, v] == 1, 1, 0)
        ceiling = jnp.where(usable > 0, -NEG, NEG)
        attend(
            r, wide(kv[r, 0], kv[r, 1]), wide(kv[r, 2], kv[r, 3]),
            lambda scores: jnp.minimum(scores, ceiling), e_s.at[r], d_s.at[r],
        )

    for r in (1, 3, 2):
        recv(f"z{4 - r}", kv.at[r, m])
        ysend(r)
    ywait(0)
    attend_prefix(0)
    send_hidden(2)
    for r in (1, 3, 2):
        ywait(r)
        attend_prefix(r)

    blocks = ("a", 0, 1, 2, 3)
    top = block_max["a"]
    for r in (0, 1, 2, 3):
        top = jnp.maximum(top, block_max[r])
    factor = {r: jnp.exp(block_max[r] - top) for r in blocks}
    total = sum(factor[r] * block_sum[r] for r in blocks)
    inverse = 1.0 / total
    row_dot = sum(factor[r] * block_dot[r] for r in blocks) * inverse

    def gradients(r):
        p = e_s[r] * (factor[r] * inverse)
        d = p * (d_s[r] - row_dot)
        dk = dot(d.astype(BF), qs[...])
        dv = dot(p.astype(BF), gs[...])
        for k in range(4):
            half_block = (dk, dv)[k // 2][:, (k % 2) * COLS : (k % 2 + 1) * COLS]
            dkv[r, k] = half_block
            st[r, k] = half_block.astype(BF)
        for k in (2, 1, 3):
            send(f"r{r}{k}", st.at[r, at(m, k)], yb.at[r, 3 - k], dev(km=k))

    def finish(r):
        piece = dkv[r, m]
        for k in (1, 3, 2):
            recv(f"r{r}{k}", yb.at[r, 3 - k])
            piece = piece + yb[r, 3 - k].astype(F32)
        rr[r] = piece
        if r:
            zst[r] = piece.astype(BF)

    gradients(2)
    gradients(1)
    gradients(3)
    gradients(0)
    for r in (2, 1, 3):
        finish(r)
        send(f"zr{r}", zst.at[r], zb.at[3 - r], dev(ks=r))
    early = len(sent)

    def wpart(half, k):
        return wg.at[at(m, k), pl.ds(pl.multiple_of(half * 1024, 1024), 1024)]

    for k in (2, 1, 3):
        send(f"w{k}", wpart(c, 0), wpart(c, 0), dev(km=k))

    finish(0)
    for kx in (1, 3, 2):
        for kc in (0, 1):
            recv(f"hx{kx}{kc}", hx.at[slot(4 - kx, kc)])
    recv("hx01", hx.at[slot(0, 1)])
    hxt[...] = hx[...].T
    drain(early)

    def block(rx, rc):
        return gbuf.at[slot(rx, rc)]

    total_block = rr[0]
    for r in (1, 3, 2):
        recv(f"zr{r}", zb.at[3 - r])
        total_block = total_block + zb[3 - r].astype(F32)
    dres[...] = total_block
    gbuf[slot(0, 0), :] = total_block.astype(BF)
    for kx in (2, 1, 3):
        send(f"g{kx}", block(0, 0), block(4 - kx, 0), dev(kx=kx))
    send("gc0", block(0, 0), block(0, 1), other)

    for k in range(4):
        ds[k, 0:52, :] = dres[52 * k : 52 * k + 52, :].astype(BF)
        ds[k, 48:64, :] = jnp.where(
            lax.broadcasted_iota(jnp.int32, (16, COLS), 0) < 4, ds[k, 48:64, :].astype(F32), 0.0
        ).astype(BF)
    for k in (1, 3, 2):
        send(f"dy{k}", ds.at[at(m, k)], dr.at[m], dev(km=k))
    dr[m] = ds[m]

    for kx in (1, 3, 2):
        recv(f"g{kx}", block(4 - kx, 0))
        send(f"gc{kx}", block(4 - kx, 0), block(4 - kx, 1), other)
    for kx in (0, 1, 3, 2):
        recv(f"gc{kx}", block((4 - kx) % 4, 1))

    tf[...] = dot(hxt[...], gbuf[...])
    ts[...] = tf[...].astype(BF)

    def rows(start, n):
        return pl.ds(pl.multiple_of(start, n), n)

    def place(ks, kz):
        return (at(s, ks) * 4 + at(zl, kz)) * 16

    for i, (ks, kz) in enumerate(along_z):
        send(f"t{ks}{kz}", ts.at[rows(place(ks, kz), 16)], zr.at[i], dev(ks=ks, kz=kz))
    for k in (1, 3, 2):
        recv(f"w{k}", wpart(c, 4 - k))
        send(f"wc{k}", wpart(c, 4 - k), wpart(c, 4 - k), other)
    late = len(sent)
    base = (x * 2 + c) * 256
    piece = tf[rows(z * 16, 16), :]
    for i, (ks, kz) in reversed(list(enumerate(along_z))):
        recv(f"t{ks}{kz}", zr.at[i])
        piece = piece + zr[i].astype(F32)
    mine = upd.at[rows(base + z * 16, 16)]
    mine[...] = piece.astype(BF)
    for ks, kz in along_z:
        send(f"u{ks}{kz}", mine, mine, dev(ks=ks, kz=kz))
    drain(late)

    for k in (1, 3, 2):
        recv(f"wc{k}", wpart(1 - c, 4 - k))
    for k in (1, 3, 2):
        recv(f"dy{k}", dr.at[at(m, 4 - k)])
    for j in range(4):
        weight = wide(*[wg[k, 512 * j : 512 * j + 512, :] for k in range(4)])
        part = dot_nt(wide(dr[0], dr[1], dr[2], dr[3]), weight)
        o_grad[0, :, 512 * j : 512 * j + 512] = part[:52].astype(BF)

    def u64(kx, ks):
        return upd.at[rows(at(x, kx) * 512 + c * 256 + at(s, ks) * 64, 64)]

    def u256(kx, kc):
        return upd.at[rows(at(x, kx) * 512 + (1 - c if kc else c) * 256, 256)]

    for ks in (0, 1, 3, 2):
        for kz in (1, 2, 3, 0):
            if ks or kz:
                source = rows(base + place(4 - ks, 4 - kz), 16)
                recv(f"u{ks}{kz}", upd.at[source])
        for kx in (2, 1, 3):
            send(f"ux{kx}{ks}", u64(0, 4 - ks), u64(0, 4 - ks), dev(kx=kx))
    send("uc0", u256(0, 0), u256(0, 0), other)
    own = upd[rows(base, 256), :].astype(F32)
    sq[...] = jnp.sum((own * own).reshape(32, 8, COLS), axis=0)
    for k in (1, 3, 2):
        send(f"sy{k}", sq, ysq.at[3 - k], dev(km=k))

    for k in (1, 3, 2):
        recv(f"sy{k}", ysq.at[3 - k])
    xs[...] = sq[...] + ysq[0] + ysq[1] + ysq[2]
    across = [(kx, kc) for kx in (2, 1, 3, 0) for kc in (1, 0) if kx or kc]
    for i, (kx, kc) in enumerate(across):
        send(f"sx{kx}{kc}", xs, xsq.at[i], dev(kx=kx, kc=kc))
    for kx in (1, 3, 2):
        for ks in (0, 1, 3, 2):
            recv(f"ux{kx}{ks}", u64(4 - kx, 4 - ks))
        send(f"uc{kx}", u256(4 - kx, 0), u256(4 - kx, 0), other)
    everything = xs[...]
    for i, (kx, kc) in enumerate(across):
        recv(f"sx{kx}{kc}", xsq.at[i])
        everything = everything + xsq[i]
    o_sq[...] = everything
    drain(len(sent) - 3)
    recv("uc0", u256(0, 1))
    for kx in (1, 3, 2):
        recv(f"uc{kx}", u256(4 - kx, 1))
    o_upd[...] = upd[...]
    drain(len(sent))


def write_results(grad_ref, raw_ref, sq_ref, o_grad, o_upd):
    o_grad[...] = grad_ref[...]
    scale = lax.rsqrt(jnp.sum(sq_ref[...]) / (D * 2 * HD) + 1e-06)
    o_upd[...] = (raw_ref[...].astype(F32) * scale).astype(BF)


def per_device(
    prefix_hidden, prefix_kv_weight, action_hidden, query_weight, action_kv_weight,
    out_cotangent, prompt_len, view_valid,
):
    vm = pltpu.VMEM
    scratch = [
        vm((ROWS, D), BF), vm((4, D, COLS), BF), vm((ACT, 1024), BF), vm((1024, 512), BF),
        vm((1024, 512), BF), vm((ACT, 512), BF), vm((4, 4, ROWS, COLS), BF), vm((ACTP, 512), BF),
        vm((QR, HD), BF), vm((QR, HD), BF), vm((HD, QR), BF), vm((HD, QR), BF),
        vm((4, ROWS, QR), F32), vm((4, ROWS, QR), F32),
        vm((4, 4, ROWS, COLS), F32), vm((4, 4, ROWS, COLS), BF),
        vm((4, 3, ROWS, COLS), BF),
        vm((4, ROWS, COLS), F32), vm((4, ROWS, COLS), BF),
        vm((3, ROWS, COLS), BF),
        vm((ROWS, COLS), F32), vm((8 * ROWS, COLS), BF), vm((8 * ROWS, 256), BF),
        vm((256, 8 * ROWS), BF), vm((256, COLS), F32), vm((256, COLS), BF),
        vm((15, 16, COLS), BF), vm((D, COLS), BF),
        vm((8, 128), F32), vm((3, 8, 128), F32), vm((8, 128), F32), vm((7, 8, 128), F32),
        vm((4, 64, COLS), BF), vm((4, 64, COLS), BF),
        pltpu.SemaphoreType.DMA((7,)),
        pltpu.SemaphoreType.DMA((N_SEMS,)), pltpu.SemaphoreType.DMA((N_SEMS,)),
    ]
    smem = pl.BlockSpec(memory_space=pltpu.SMEM)
    hbm = pl.BlockSpec(memory_space=pltpu.HBM)
    grad, raw, squares = pl.pallas_call(
        kernel,
        out_shape=(
            jax.ShapeDtypeStruct((1, 52, D), BF),
            jax.ShapeDtypeStruct((D, COLS), BF),
            jax.ShapeDtypeStruct((8, 128), F32),
        ),
        in_specs=[smem, smem] + [hbm] * 6,
        out_specs=(pl.BlockSpec(memory_space=pltpu.VMEM),) * 3,
        scratch_shapes=scratch,
        compiler_params=pltpu.CompilerParams(
            collective_id=0, has_side_effects=True, vmem_limit_bytes=40 * 1024 * 1024
        ),
    )(
        prompt_len, view_valid, *[pltpu.with_memory_space_constraint(v, pltpu.HBM) for v in (prefix_hidden, prefix_kv_weight, action_hidden, query_weight, action_kv_weight, out_cotangent)])
    return pl.pallas_call(
        write_results,
        out_shape=(
            jax.ShapeDtypeStruct((1, 52, D), BF),
            jax.ShapeDtypeStruct((D, COLS), BF),
        ),
        in_specs=[pl.BlockSpec(memory_space=pltpu.VMEM)] * 3,
        out_specs=(pl.BlockSpec(memory_space=pltpu.VMEM),) * 2,
        compiler_params=pltpu.CompilerParams(vmem_limit_bytes=40 * 1024 * 1024),
    )(grad, raw, squares)


def solution(mesh):
    return jax.shard_map(
        per_device,
        mesh=mesh,
        in_specs=(
            P("dp", "sample", None),
            P(None, "mp"),
            P("dp", "sample", None),
            P(None, "mp"),
            P(),
            P("dp", "sample", "mp"),
            P("dp"),
            P("dp", None),
        ),
        out_specs=(P("dp", ("sample", "mp"), None), P(None, "mp")),
        check_vma=False,
    )
```

```python
import jax
import jax.numpy as jnp
from jax import lax
from jax.experimental import pallas as pl
from jax.experimental.pallas import tpu as pltpu
from jax.sharding import PartitionSpec as P

BF = jnp.bfloat16
F32 = jnp.float32
D = 2048
HD = 256
ROWS = 208
COLS = 128
ACT = 300
ACTP = 304
QR = 2 * ACTP
VIEW_TOK = 256
VIEWS = 3
HORIZON = 50
NEG = -3.0e38
HALF = ((0, 112), (112, 96))
PART = ((0, 64), (64, 48), (112, 48), (160, 48))
N_SEMS = 160


def dot(a, b):
    return jnp.dot(a, b, preferred_element_type=F32)


def wide(*pieces):
    return jnp.concatenate(pieces, axis=1)


def dot_nt(a, b):
    return lax.dot_general(a, b, (((1,), (1,)), ((), ())), preferred_element_type=F32)


def kernel(
    len_ref, view_ref, hid_h, w_h, act_h, wq_h, wakv_h, cot_h,
    o_grad, o_upd, o_sq,
    hid_v, wg, act_v, wq_v, wakv_v, cot_v, kv, akv, qs, gs, qt, gt, e_s, d_s,
    dkv, st,
    yb, rr, zst, za0, za1, zb0, zb1, zc0, zc1,
    dres, hid_t, ps, pc, pf, px, qx, tf, ts, zr, upd,
    sq, ysq, xs, xsq, ds, dr,
    lsem, ssem, rsem,
):
    dp = lax.axis_index("dp")
    s = lax.axis_index("sample")
    m = lax.axis_index("mp")
    x = dp // 8
    zl = lax.rem(dp, 8) // 2
    c = lax.rem(dp, 2)

    def at(a, k):
        return lax.rem(a + k, 4)

    z = s * 4 + zl

    def dev(kx=0, kz=0, ks=0, km=0, kc=0):
        cc = 1 - c if kc else c
        d = at(x, kx) * 8 + at(zl, kz) * 2 + cc
        return {"dp": d, "sample": at(s, ks), "mp": at(m, km)}

    along_z = [(ks, kz) for ks in (2, 1, 3, 0) for kz in (1, 2, 3, 0) if ks or kz]
    yp, ym = dev(km=1), dev(km=3)
    zp, zm = dev(ks=1), dev(ks=3)
    xp, xm = dev(kx=1), dev(kx=3)
    other = dev(kc=1)

    index = {}
    sent = []

    def number(name):
        return index.setdefault(name, len(index))

    def send(name, src, dst, device):
        i = number(name)
        copy = pltpu.make_async_remote_copy(
            src_ref=src, dst_ref=dst, send_sem=ssem.at[i], recv_sem=rsem.at[i],
            device_id=device, device_id_type=pl.DeviceIdType.MESH,
        )
        copy.start()
        sent.append(copy)

    def recv(name, dst, device=None):
        i = number(name)
        pltpu.make_async_remote_copy(
            src_ref=dst, dst_ref=dst, send_sem=ssem.at[i], recv_sem=rsem.at[i],
            device_id=other if device is None else device,
            device_id_type=pl.DeviceIdType.MESH,
        ).wait_recv()

    def drain(n):
        for copy in sent[:n]:
            copy.wait_send()
        del sent[:n]

    loads = [
        pltpu.make_async_copy(hid_h.at[0, 0:112], hid_v.at[0:112], lsem.at[0]),
        pltpu.make_async_copy(w_h, wg.at[m], lsem.at[1]),
        pltpu.make_async_copy(act_h.at[0], act_v, lsem.at[2]),
        pltpu.make_async_copy(wq_h, wq_v, lsem.at[3]),
        pltpu.make_async_copy(wakv_h, wakv_v, lsem.at[4]),
        pltpu.make_async_copy(cot_h.at[0], cot_v, lsem.at[5]),
        pltpu.make_async_copy(hid_h.at[0, 112:208], hid_v.at[112:208], lsem.at[6]),
    ]
    for i in (1, 0, 6):
        loads[i].start()

    barrier = pltpu.get_barrier_semaphore()
    peers = [dev(km=k) for k in (1, 2, 3)] + [dev(ks=ks, kz=kz) for ks, kz in along_z] + [other]
    peers += [dev(kx=k, kc=kc) for k in (1, 2, 3) for kc in (0, 1)]
    for peer in peers:
        pl.semaphore_signal(
            barrier, inc=1, device_id=peer, device_id_type=pl.DeviceIdType.MESH
        )

    def kvp(r, i):
        r0, n = PART[i]
        return kv.at[r, m, pl.ds(r0, n)]

    def ysend(r):
        block = kv.at[r, m]
        for k in (2, 1, 3):
            send(f"y{r}{k}", block, block, dev(km=k))

    def ywait(r):
        for k in (1, 3, 2):
            recv(f"y{r}{k}", kv.at[r, at(m, 4 - k)])

    loads[1].wait()
    loads[0].wait()
    for i in (2, 3, 5, 4):
        loads[i].start()
    kv[0, m, 0:112, :] = dot(hid_v[0:112], wg[m]).astype(BF)
    pl.semaphore_wait(barrier, len(peers))
    for i in (0, 1):
        send(f"zp{i}", kvp(0, i), kvp(3, i), zp)
    loads[6].wait()
    kv[0, m, 112:208, :] = dot(hid_v[112:208], wg[m]).astype(BF)
    for i in (2, 3):
        send(f"zm{i}", kvp(0, i), kvp(1, i), zm)
    for i, j in ((2, 0), (3, 1)):
        send(f"zp{i}", kvp(0, i), kvp(3, i), zp)
        send(f"zm{j}", kvp(0, j), kvp(1, j), zm)
    ysend(0)

    for ref in (qs, gs):
        ref[288:304, :] = jnp.zeros((16, HD), BF)
        ref[592:608, :] = jnp.zeros((16, HD), BF)
    akv[288:304, :] = jnp.zeros((16, 2 * HD), BF)
    loads[2].wait()
    loads[3].wait()
    queries = (dot(act_v[...], wq_v[...]).astype(BF).astype(F32) * (HD**-0.5)).astype(BF)
    qs[0:ACT, :] = queries[:, :HD]
    qs[ACTP : ACTP + ACT, :] = queries[:, HD:]
    loads[4].wait()
    akv[0:ACT, :] = dot(act_v[...], wakv_v[...]).astype(BF)
    loads[5].wait()
    gs[0:ACT, :] = cot_v[:, :HD]
    gs[ACTP : ACTP + ACT, :] = cot_v[:, HD:]

    qt[...] = qs[...].T
    gt[...] = gs[...].T

    block_max, block_sum, block_dot = {}, {}, {}

    def attend(r, keys, values, mask, e_ref, d_ref):
        scores = mask(dot(keys, qt[...]))
        top = jnp.max(scores, axis=0, keepdims=True)
        e = jnp.exp(scores - top)
        d = dot(values, gt[...])
        if e_ref is not None:
            e_ref[...] = e
            d_ref[...] = d
        block_max[r] = top
        block_sum[r] = jnp.sum(e, axis=0, keepdims=True)
        block_dot[r] = jnp.sum(e * d, axis=0, keepdims=True)

    def draw(i):
        total = jnp.zeros_like(i)
        for t in range(1, ACTP // HORIZON + 1):
            total = total + jnp.where(i >= t * HORIZON, 1, 0)
        return total

    for i, j in ((0, 2), (1, 3)):
        recv(f"zp{i}", kvp(3, i))
        send(f"zf{i}", kvp(3, i), kvp(2, i), zp)
        recv(f"zm{j}", kvp(1, j))
        send(f"zf{j}", kvp(1, j), kvp(2, j), zm)

    key_draw = draw(lax.broadcasted_iota(jnp.int32, (ACTP, 1), 0))
    query_index = lax.broadcasted_iota(jnp.int32, (1, QR), 1)
    query_draw = draw(query_index - jnp.where(query_index >= ACTP, ACTP, 0))
    attend(
        "a", akv[:, :HD], akv[:, HD:],
        lambda scores: jnp.where(key_draw == query_draw, scores, NEG), None, None,
    )

    def attend_prefix(r):
        p = at(s, r) * ROWS + lax.broadcasted_iota(jnp.int32, (ROWS, 1), 0)
        usable = jnp.where(p >= VIEWS * VIEW_TOK, jnp.where(p - VIEWS * VIEW_TOK < len_ref[0], 1, 0), 0)
        for v in range(VIEWS):
            inside = jnp.where(p >= v * VIEW_TOK, 1, 0) * jnp.where(p < (v + 1) * VIEW_TOK, 1, 0)
            usable = usable + inside * jnp.where(view_ref[0, v] == 1, 1, 0)
        ceiling = jnp.where(usable > 0, -NEG, NEG)
        attend(
            r, wide(kv[r, 0], kv[r, 1]), wide(kv[r, 2], kv[r, 3]),
            lambda scores: jnp.minimum(scores, ceiling), e_s.at[r], d_s.at[r],
        )

    for i in (2, 3):
        recv(f"zp{i}", kvp(3, i))
    ysend(3)
    for i in (0, 1):
        recv(f"zm{i}", kvp(1, i))
    ysend(1)
    ywait(0)
    attend_prefix(0)
    for i in (0, 2, 1, 3):
        recv(f"zf{i}", kvp(2, i))
    ysend(2)
    ywait(3)
    attend_prefix(3)
    ywait(1)
    attend_prefix(1)
    ywait(2)
    attend_prefix(2)

    blocks = ("a", 0, 1, 2, 3)
    top = block_max["a"]
    for r in (0, 1, 2, 3):
        top = jnp.maximum(top, block_max[r])
    factor = {r: jnp.exp(block_max[r] - top) for r in blocks}
    total = sum(factor[r] * block_sum[r] for r in blocks)
    inverse = 1.0 / total
    row_dot = sum(factor[r] * block_dot[r] for r in blocks) * inverse

    def half(h):
        r0, n = HALF[h]
        return pl.ds(r0, n)

    def gradients(r, h):
        p = e_s[r, half(h), :] * (factor[r] * inverse)
        d = p * (d_s[r, half(h), :] - row_dot)
        dk = dot(d.astype(BF), qs[...])
        dv = dot(p.astype(BF), gs[...])
        for k in range(4):
            columns = (dk, dv)[k // 2][:, (k % 2) * COLS : (k % 2 + 1) * COLS]
            dkv[r, k, half(h), :] = columns
            st[r, k, half(h), :] = columns.astype(BF)
        for k in (2, 1, 3):
            send(f"r{r}{k}{h}", st.at[r, at(m, k), half(h)], yb.at[r, 3 - k, half(h)], dev(km=k))

    def finish(r, h):
        piece = dkv[r, m, half(h), :]
        for k in (1, 3, 2):
            recv(f"r{r}{k}{h}", yb.at[r, 3 - k, half(h)])
            piece = piece + yb[r, 3 - k, half(h), :].astype(F32)
        return piece

    order = ((2, 0), (2, 1), (1, 1), (3, 0), (1, 0), (3, 1))
    for r, h in order:
        gradients(r, h)
    for i, (r, h) in enumerate(order[:4]):
        zst[r, half(h), :] = finish(r, h).astype(BF)
        target = (za0, za1, zb1, zb0)[i]
        send(f"z{i}", zst.at[r, half(h)], target, zm if i % 2 else zp)
        if i < 2:
            gradients(0, i)
    early = len(sent)
    for i, (r, h), arrived, target in ((4, order[4], za0, zc0), (5, order[5], za1, zc1)):
        piece = finish(r, h)
        recv(f"z{i - 4}", arrived)
        zst[r, half(h), :] = (piece + arrived[...].astype(F32)).astype(BF)
        send(f"z{i}", zst.at[r, half(h)], target, zm if i % 2 else zp)

    def wpart(half, k):
        return wg.at[at(m, k), pl.ds(pl.multiple_of(half * 1024, 1024), 1024)]

    for k in (2, 1, 3):
        send(f"w{k}", wpart(c, 0), wpart(c, 0), dev(km=k))

    for h in (0, 1):
        rr[half(h), :] = finish(0, h)
    hid_t[...] = hid_v[...].T
    drain(early)

    recv("z3", zb0)
    recv("z4", zc0)
    dres[half(0), :] = rr[half(0), :] + zb0[...].astype(F32) + zc0[...].astype(F32)
    recv("z2", zb1)
    recv("z5", zc1)
    dres[half(1), :] = rr[half(1), :] + zb1[...].astype(F32) + zc1[...].astype(F32)
    own_grad = dres[...].astype(BF)

    def rows(start, n):
        return pl.ds(pl.multiple_of(start, n), n)

    def place256(kx, kc):
        return rows((1 - c if kc else c) * 1024 + at(x, kx) * 256, 256)

    for kx in (2, 1, 3, 0):
        ps[kx] = dot(hid_t[place256(kx, 1), :], own_grad).astype(BF)
        send(f"p{kx}", ps.at[kx], pc.at[kx], other)
    for kx in (2, 1, 3, 0):
        pf[kx] = dot(hid_t[place256(kx, 0), :], own_grad)
    for kx in (2, 1, 3):
        recv(f"p{kx}", pc.at[kx])
        px[kx] = (pf[kx] + pc[kx].astype(F32)).astype(BF)
        send(f"q{kx}", px.at[kx], qx.at[3 - kx], dev(kx=kx))

    for k in range(4):
        ds[k, 0:52, :] = dres[52 * k : 52 * k + 52, :].astype(BF)
        ds[k, 48:64, :] = jnp.where(
            lax.broadcasted_iota(jnp.int32, (16, COLS), 0) < 4, ds[k, 48:64, :].astype(F32), 0.0
        ).astype(BF)
    for k in (1, 3, 2):
        send(f"dy{k}", ds.at[at(m, k)], dr.at[m], dev(km=k))
    dr[m] = ds[m]

    recv("p0", pc.at[0])
    part = pf[0] + pc[0].astype(F32)
    for kx in (1, 3, 2):
        recv(f"q{kx}", qx.at[3 - kx])
        part = part + qx[3 - kx].astype(F32)

    tf[...] = part
    ts[...] = part.astype(BF)

    def place(ks, kz):
        return (at(s, ks) * 4 + at(zl, kz)) * 16

    for i, (ks, kz) in enumerate(along_z):
        send(f"t{ks}{kz}", ts.at[rows(place(ks, kz), 16)], zr.at[i], dev(ks=ks, kz=kz))
    for k in (1, 3, 2):
        recv(f"w{k}", wpart(c, 4 - k))
        send(f"wc{k}", wpart(c, 4 - k), wpart(c, 4 - k), other)
    late = len(sent)
    base = c * 1024 + x * 256
    piece = tf[rows(z * 16, 16), :]
    for i, (ks, kz) in reversed(list(enumerate(along_z))):
        recv(f"t{ks}{kz}", zr.at[i])
        piece = piece + zr[i].astype(F32)
    mine = upd.at[rows(base + z * 16, 16)]
    mine[...] = piece.astype(BF)
    for ks, kz in along_z:
        send(f"u{ks}{kz}", mine, mine, dev(ks=ks, kz=kz))
    drain(late)

    for k in (1, 3, 2):
        recv(f"wc{k}", wpart(1 - c, 4 - k))
    for k in (1, 3, 2):
        recv(f"dy{k}", dr.at[at(m, 4 - k)])
    for j in range(4):
        weight = wide(*[wg[k, 512 * j : 512 * j + 512, :] for k in range(4)])
        part = dot_nt(wide(dr[0], dr[1], dr[2], dr[3]), weight)
        o_grad[0, :, 512 * j : 512 * j + 512] = part[:52].astype(BF)

    def u64(kx, ks):
        return upd.at[rows(c * 1024 + at(x, kx) * 256 + at(s, ks) * 64, 64)]

    def u256(kx, kc):
        return upd.at[place256(kx, kc)]

    for ks in (0, 1, 3, 2):
        for kz in (1, 2, 3, 0):
            if ks or kz:
                source = rows(base + place(4 - ks, 4 - kz), 16)
                recv(f"u{ks}{kz}", upd.at[source])
        for kx in (2, 1, 3):
            send(f"ux{kx}{ks}", u64(0, 4 - ks), u64(0, 4 - ks), dev(kx=kx))
    send("uc0", u256(0, 0), u256(0, 0), other)
    own = upd[rows(base, 256), :].astype(F32)
    sq[...] = jnp.sum((own * own).reshape(32, 8, COLS), axis=0)
    for k in (1, 3, 2):
        send(f"sy{k}", sq, ysq.at[3 - k], dev(km=k))

    for k in (1, 3, 2):
        recv(f"sy{k}", ysq.at[3 - k])
    xs[...] = sq[...] + ysq[0] + ysq[1] + ysq[2]
    across = [(kx, kc) for kx in (2, 1, 3, 0) for kc in (1, 0) if kx or kc]
    for i, (kx, kc) in enumerate(across):
        send(f"sx{kx}{kc}", xs, xsq.at[i], dev(kx=kx, kc=kc))
    for kx in (1, 3, 2):
        for ks in (0, 1, 3, 2):
            recv(f"ux{kx}{ks}", u64(4 - kx, 4 - ks))
        send(f"uc{kx}", u256(4 - kx, 0), u256(4 - kx, 0), other)
    everything = xs[...]
    for i, (kx, kc) in enumerate(across):
        recv(f"sx{kx}{kc}", xsq.at[i])
        everything = everything + xsq[i]
    o_sq[...] = everything
    drain(len(sent) - 3)
    recv("uc0", u256(0, 1))
    for kx in (1, 3, 2):
        recv(f"uc{kx}", u256(4 - kx, 1))
    o_upd[...] = upd[...]
    drain(len(sent))


def write_results(grad_ref, raw_ref, sq_ref, o_grad, o_upd):
    o_grad[...] = grad_ref[...]
    scale = lax.rsqrt(jnp.sum(sq_ref[...]) / (D * 2 * HD) + 1e-06)
    o_upd[...] = (raw_ref[...].astype(F32) * scale).astype(BF)


def per_device(
    prefix_hidden, prefix_kv_weight, action_hidden, query_weight, action_kv_weight,
    out_cotangent, prompt_len, view_valid,
):
    vm = pltpu.VMEM
    scratch = [
        vm((ROWS, D), BF), vm((4, D, COLS), BF), vm((ACT, 1024), BF), vm((1024, 512), BF),
        vm((1024, 512), BF), vm((ACT, 512), BF), vm((4, 4, ROWS, COLS), BF), vm((ACTP, 512), BF),
        vm((QR, HD), BF), vm((QR, HD), BF), vm((HD, QR), BF), vm((HD, QR), BF),
        vm((4, ROWS, QR), F32), vm((4, ROWS, QR), F32),
        vm((4, 4, ROWS, COLS), F32), vm((4, 4, ROWS, COLS), BF),
        vm((4, 3, ROWS, COLS), BF),
        vm((ROWS, COLS), F32), vm((4, ROWS, COLS), BF),
        vm((112, COLS), BF), vm((96, COLS), BF), vm((112, COLS), BF), vm((96, COLS), BF),
        vm((112, COLS), BF), vm((96, COLS), BF),
        vm((ROWS, COLS), F32), vm((D, ROWS), BF), vm((4, 256, COLS), BF), vm((4, 256, COLS), BF),
        vm((4, 256, COLS), F32), vm((4, 256, COLS), BF), vm((3, 256, COLS), BF),
        vm((256, COLS), F32), vm((256, COLS), BF),
        vm((15, 16, COLS), BF), vm((D, COLS), BF),
        vm((8, 128), F32), vm((3, 8, 128), F32), vm((8, 128), F32), vm((7, 8, 128), F32),
        vm((4, 64, COLS), BF), vm((4, 64, COLS), BF),
        pltpu.SemaphoreType.DMA((7,)),
        pltpu.SemaphoreType.DMA((N_SEMS,)), pltpu.SemaphoreType.DMA((N_SEMS,)),
    ]
    smem = pl.BlockSpec(memory_space=pltpu.SMEM)
    hbm = pl.BlockSpec(memory_space=pltpu.HBM)
    grad, raw, squares = pl.pallas_call(
        kernel,
        out_shape=(
            jax.ShapeDtypeStruct((1, 52, D), BF),
            jax.ShapeDtypeStruct((D, COLS), BF),
            jax.ShapeDtypeStruct((8, 128), F32),
        ),
        in_specs=[smem, smem] + [hbm] * 6,
        out_specs=(pl.BlockSpec(memory_space=pltpu.VMEM),) * 3,
        scratch_shapes=scratch,
        compiler_params=pltpu.CompilerParams(
            collective_id=0, has_side_effects=True, vmem_limit_bytes=40 * 1024 * 1024
        ),
    )(
        prompt_len, view_valid, *[pltpu.with_memory_space_constraint(v, pltpu.HBM) for v in (prefix_hidden, prefix_kv_weight, action_hidden, query_weight, action_kv_weight, out_cotangent)])
    return pl.pallas_call(
        write_results,
        out_shape=(
            jax.ShapeDtypeStruct((1, 52, D), BF),
            jax.ShapeDtypeStruct((D, COLS), BF),
        ),
        in_specs=[pl.BlockSpec(memory_space=pltpu.VMEM)] * 3,
        out_specs=(pl.BlockSpec(memory_space=pltpu.VMEM),) * 2,
        compiler_params=pltpu.CompilerParams(vmem_limit_bytes=40 * 1024 * 1024),
    )(grad, raw, squares)


def solution(mesh):
    return jax.shard_map(
        per_device,
        mesh=mesh,
        in_specs=(
            P("dp", "sample", None),
            P(None, "mp"),
            P("dp", "sample", None),
            P(None, "mp"),
            P(),
            P("dp", "sample", "mp"),
            P("dp"),
            P("dp", None),
        ),
        out_specs=(P("dp", ("sample", "mp"), None), P(None, "mp")),
        check_vma=False,
    )
```

```python
import jax
import jax.numpy as jnp
from jax import lax
from jax.experimental import pallas as pl
from jax.experimental.pallas import tpu as pltpu
from jax.sharding import PartitionSpec as P

BF = jnp.bfloat16
F32 = jnp.float32
D = 2048
HD = 256
ROWS = 208
COLS = 128
ACT = 300
ACTP = 304
QR = 2 * ACTP
VIEW_TOK = 256
VIEWS = 3
HORIZON = 50
NEG = -3.0e38
HALF = ((0, 112), (112, 96))
PART = ((0, 64), (64, 48), (112, 48), (160, 48))
N_SEMS = 160


def dot(a, b):
    return jnp.dot(a, b, preferred_element_type=F32)


def wide(*pieces):
    return jnp.concatenate(pieces, axis=1)


def dot_nt(a, b):
    return lax.dot_general(a, b, (((1,), (1,)), ((), ())), preferred_element_type=F32)


def kernel(
    len_ref, view_ref, hid_h, w_h, act_h, wq_h, wakv_h, cot_h,
    o_grad, o_upd, o_sq,
    hid_v, wg, act_v, wq_v, wakv_v, cot_v, kv, akv, qs, gs, qt, gt, e_s, d_s, bmax, bsum, bdot,
    dkv, st, yb,
    rr, zst, za0, za1, zb0, zb1, zc0, zc1, zsc0, zsc1,
    dres, gbuf, hx, hxt, tf, ts, zr, upd,
    sq, ysq, xs, xsq, ds, dr,
    lsem, ssem, rsem,
):
    dp = lax.axis_index("dp")
    s = lax.axis_index("sample")
    m = lax.axis_index("mp")
    x = dp // 8
    zl = lax.rem(dp, 8) // 2
    c = lax.rem(dp, 2)

    def at(a, k):
        return lax.rem(a + k, 4)

    z = s * 4 + zl

    def dev(kx=0, kz=0, ks=0, km=0, kc=0):
        cc = 1 - c if kc else c
        d = at(x, kx) * 8 + at(zl, kz) * 2 + cc
        return {"dp": d, "sample": at(s, ks), "mp": at(m, km)}

    def far_first(i):
        return 2 - i + 3 * (i // 2) - 2 * (i // 3)

    def along_z(i):
        return far_first(i // 4), lax.rem(i + 1, 4)

    yp, ym = dev(km=1), dev(km=3)
    zp, zm = dev(ks=1), dev(ks=3)
    other = dev(kc=1)

    index = {}
    sent = []

    Y0, R0, T0, U0, FIRST = 0, 12, 24, 40, 56

    def number(name):
        if isinstance(name, str):
            return index.setdefault(name, FIRST + len(index))
        return name

    def remote(name, src, dst, device):
        i = number(name)
        return pltpu.make_async_remote_copy(
            src_ref=src, dst_ref=dst, send_sem=ssem.at[i], recv_sem=rsem.at[i],
            device_id=device, device_id_type=pl.DeviceIdType.MESH,
        )

    def send(name, src, dst, device):
        copy = remote(name, src, dst, device)
        copy.start()
        if isinstance(name, str):
            sent.append(copy)

    def recv(name, dst):
        remote(name, dst, dst, other).wait_recv()

    def sent_all(first, n, src):
        @pl.loop(0, n)
        def _(i):
            remote(first + i, src, src, other).wait_send()

    def drain(n):
        for copy in sent[:n]:
            copy.wait_send()
        del sent[:n]

    loads = [
        pltpu.make_async_copy(hid_h.at[0, 0:112], hid_v.at[0:112], lsem.at[0]),
        pltpu.make_async_copy(w_h, wg.at[m], lsem.at[1]),
        pltpu.make_async_copy(act_h.at[0], act_v, lsem.at[2]),
        pltpu.make_async_copy(wq_h, wq_v, lsem.at[3]),
        pltpu.make_async_copy(wakv_h, wakv_v, lsem.at[4]),
        pltpu.make_async_copy(cot_h.at[0], cot_v, lsem.at[5]),
        pltpu.make_async_copy(hid_h.at[0, 112:208], hid_v.at[112:208], lsem.at[6]),
    ]
    for i in (1, 0, 6):
        loads[i].start()

    barrier = pltpu.get_barrier_semaphore()
    peers = [dev(km=k) for k in (1, 2, 3)] + [dev(ks=i // 4, kz=i % 4) for i in range(1, 16)] + [other]
    peers += [dev(kx=k, kc=kc) for k in (1, 2, 3) for kc in (0, 1)]
    for peer in peers:
        pl.semaphore_signal(
            barrier, inc=1, device_id=peer, device_id_type=pl.DeviceIdType.MESH
        )

    def kvp(r, i):
        r0, n = PART[i]
        return kv.at[r, m, pl.ds(r0, n)]

    def ysend(r):
        block = kv.at[r, m]
        for k in (2, 1, 3):
            send(Y0 + 3 * r + k - 1, block, block, dev(km=k))

    def ywait(r):
        for k in (1, 3, 2):
            recv(Y0 + 3 * r + k - 1, kv.at[r, at(m, 4 - k)])

    loads[1].wait()
    loads[0].wait()
    for i in (2, 3, 5, 4):
        loads[i].start()
    kv[0, m, 0:112, :] = dot(hid_v[0:112], wg[m]).astype(BF)
    pl.semaphore_wait(barrier, len(peers))
    for i in (0, 1):
        send(f"zp{i}", kvp(0, i), kvp(3, i), zp)
    loads[6].wait()
    kv[0, m, 112:208, :] = dot(hid_v[112:208], wg[m]).astype(BF)
    for i in (2, 3):
        send(f"zm{i}", kvp(0, i), kvp(1, i), zm)
    for i, j in ((2, 0), (3, 1)):
        send(f"zp{i}", kvp(0, i), kvp(3, i), zp)
        send(f"zm{j}", kvp(0, j), kvp(1, j), zm)
    ysend(0)

    def slot(rx, rc):
        return pl.ds((rx * 2 + rc) * ROWS, ROWS)

    def hidden_columns(kx, kc):
        j = at(x, kx) * 2 + (1 - c if kc else c)
        return pl.ds(pl.multiple_of(j * 256, 256), 256)

    def send_hidden(kx):
        for kc in (0, 1):
            send(f"hx{kx}{kc}", hid_v.at[:, hidden_columns(kx, kc)],
                 hx.at[slot(4 - kx, kc)], dev(kx=kx, kc=kc))

    send_hidden(1)
    send_hidden(3)
    send("hx01", hid_v.at[:, hidden_columns(0, 1)], hx.at[slot(0, 1)], other)
    hx[slot(0, 0), :] = hid_v[:, hidden_columns(0, 0)]

    for ref in (qs, gs):
        ref[288:304, :] = jnp.zeros((16, HD), BF)
        ref[592:608, :] = jnp.zeros((16, HD), BF)
    akv[288:304, :] = jnp.zeros((16, 2 * HD), BF)
    loads[2].wait()
    loads[3].wait()
    queries = (dot(act_v[...], wq_v[...]).astype(BF).astype(F32) * (HD**-0.5)).astype(BF)
    qs[0:ACT, :] = queries[:, :HD]
    qs[ACTP : ACTP + ACT, :] = queries[:, HD:]
    loads[4].wait()
    akv[0:ACT, :] = dot(act_v[...], wakv_v[...]).astype(BF)
    loads[5].wait()
    gs[0:ACT, :] = cot_v[:, :HD]
    gs[ACTP : ACTP + ACT, :] = cot_v[:, HD:]

    qt[...] = qs[...].T
    gt[...] = gs[...].T

    def attend(r, keys, values, mask, e_ref, d_ref):
        scores = mask(dot(keys, qt[...]))
        top = jnp.max(scores, axis=0, keepdims=True)
        e = jnp.exp(scores - top)
        d = dot(values, gt[...])
        if e_ref is not None:
            e_ref[...] = e
            d_ref[...] = d
        bmax[r] = top
        bsum[r] = jnp.sum(e, axis=0, keepdims=True)
        bdot[r] = jnp.sum(e * d, axis=0, keepdims=True)

    def draw(i):
        total = jnp.zeros_like(i)
        for t in range(1, ACTP // HORIZON + 1):
            total = total + jnp.where(i >= t * HORIZON, 1, 0)
        return total

    for i, j in ((0, 2), (1, 3)):
        recv(f"zp{i}", kvp(3, i))
        send(f"zf{i}", kvp(3, i), kvp(2, i), zp)
        recv(f"zm{j}", kvp(1, j))
        send(f"zf{j}", kvp(1, j), kvp(2, j), zm)

    key_draw = draw(lax.broadcasted_iota(jnp.int32, (ACTP, 1), 0))
    query_index = lax.broadcasted_iota(jnp.int32, (1, QR), 1)
    query_draw = draw(query_index - jnp.where(query_index >= ACTP, ACTP, 0))
    attend(
        4, akv[:, :HD], akv[:, HD:],
        lambda scores: jnp.where(key_draw == query_draw, scores, NEG), None, None,
    )

    def attend_prefix(r):
        p = at(s, r) * ROWS + lax.broadcasted_iota(jnp.int32, (ROWS, 1), 0)
        usable = jnp.where(p >= VIEWS * VIEW_TOK, jnp.where(p - VIEWS * VIEW_TOK < len_ref[0], 1, 0), 0)
        for v in range(VIEWS):
            inside = jnp.where(p >= v * VIEW_TOK, 1, 0) * jnp.where(p < (v + 1) * VIEW_TOK, 1, 0)
            usable = usable + inside * jnp.where(view_ref[0, v] == 1, 1, 0)
        ceiling = jnp.where(usable > 0, -NEG, NEG)
        attend(
            r, wide(kv[r, 0], kv[r, 1]), wide(kv[r, 2], kv[r, 3]),
            lambda scores: jnp.minimum(scores, ceiling), e_s.at[r], d_s.at[r],
        )

    for i in (2, 3):
        recv(f"zp{i}", kvp(3, i))
    ysend(3)
    for i in (0, 1):
        recv(f"zm{i}", kvp(1, i))
    ysend(1)
    for i in (0, 2, 1, 3):
        recv(f"zf{i}", kvp(2, i))
    ysend(2)
    send_hidden(2)

    @pl.loop(0, 4)
    def _(i):
        r = i + i // 2 - 2 * (i // 3)
        ywait(r)
        attend_prefix(r)

    top = bmax[4]
    for r in range(4):
        top = jnp.maximum(top, bmax[r])
    total = jnp.zeros_like(top)
    weighted = jnp.zeros_like(top)
    for r in range(5):
        factor = jnp.exp(bmax[r] - top)
        total = total + factor * bsum[r]
        weighted = weighted + factor * bdot[r]
    inverse = 1.0 / total
    row_dot = weighted * inverse

    def half(h):
        r0, n = HALF[h]
        return pl.ds(r0, n)

    def gradients(r):
        p = e_s[r] * (jnp.exp(bmax[r] - top) * inverse)
        d = p * (d_s[r] - row_dot)
        dk = dot(d.astype(BF), qs[...])
        dv = dot(p.astype(BF), gs[...])
        for k in range(4):
            half_block = (dk, dv)[k // 2][:, (k % 2) * COLS : (k % 2 + 1) * COLS]
            dkv[r, k] = half_block
            st[r, k] = half_block.astype(BF)
        for k in (2, 1, 3):
            send(R0 + 3 * r + k - 1, st.at[r, at(m, k)], yb.at[r, 3 - k], dev(km=k))

    def finish(r):
        piece = dkv[r, m]
        for k in (1, 3, 2):
            recv(R0 + 3 * r + k - 1, yb.at[r, 3 - k])
            piece = piece + yb[r, 3 - k].astype(F32)
        rr[r] = piece
        if r:
            zst[r] = piece.astype(BF)

    @pl.loop(0, 4)
    def _(i):
        gradients(far_first(i))

    finish(2)
    send("zap", zst.at[2, half(0)], za0, zp)
    send("zam", zst.at[2, half(1)], za1, zm)
    finish(1)
    send("zbp", zst.at[1, half(1)], zb1, zp)
    finish(3)
    send("zbm", zst.at[3, half(0)], zb0, zm)
    early = len(sent)
    recv("zap", za0)
    zsc0[...] = (rr[1, half(0), :] + za0[...].astype(F32)).astype(BF)
    send("zcp", zsc0, zc0, zp)
    recv("zam", za1)
    zsc1[...] = (rr[3, half(1), :] + za1[...].astype(F32)).astype(BF)
    send("zcm", zsc1, zc1, zm)

    def wpart(q, k):
        return wg.at[at(m, k), pl.ds(pl.multiple_of(c * 1024 + q * 512, 512), 512)]

    send("wp0", wpart(0, 0), wpart(0, 0), yp)
    send("wm1", wpart(1, 0), wpart(1, 0), ym)
    send("wp1", wpart(1, 0), wpart(1, 0), yp)
    send("wm0", wpart(0, 0), wpart(0, 0), ym)

    finish(0)
    for kx in (1, 3, 2):
        for kc in (0, 1):
            recv(f"hx{kx}{kc}", hx.at[slot(4 - kx, kc)])
    recv("hx01", hx.at[slot(0, 1)])
    hxt[...] = hx[...].T
    sent_all(Y0, 12, kv.at[0, 0])
    sent_all(R0, 12, st.at[0, 0])
    drain(early)

    def gh(rx, rc, h):
        r0, n = HALF[h]
        return gbuf.at[pl.ds((rx * 2 + rc) * ROWS + r0, n)]

    recv("zbm", zb0)
    recv("zcp", zc0)
    dres[half(0), :] = rr[0, half(0), :] + zb0[...].astype(F32) + zc0[...].astype(F32)
    gbuf[half(0), :] = dres[half(0), :].astype(BF)
    for kx in (2, 1, 3):
        send(f"g{kx}0", gh(0, 0, 0), gh(4 - kx, 0, 0), dev(kx=kx))
    send("gc00", gh(0, 0, 0), gh(0, 1, 0), other)
    recv("zbp", zb1)
    recv("zcm", zc1)
    dres[half(1), :] = rr[0, half(1), :] + zb1[...].astype(F32) + zc1[...].astype(F32)
    gbuf[half(1), :] = dres[half(1), :].astype(BF)
    for kx in (2, 1, 3):
        send(f"g{kx}1", gh(0, 0, 1), gh(4 - kx, 0, 1), dev(kx=kx))
    send("gc01", gh(0, 0, 1), gh(0, 1, 1), other)

    for k in range(4):
        ds[k, 0:52, :] = dres[52 * k : 52 * k + 52, :].astype(BF)
        ds[k, 48:64, :] = jnp.where(
            lax.broadcasted_iota(jnp.int32, (16, COLS), 0) < 4, ds[k, 48:64, :].astype(F32), 0.0
        ).astype(BF)
    for k in (1, 3, 2):
        send(f"dy{k}", ds.at[at(m, k)], dr.at[m], dev(km=k))
    dr[m] = ds[m]

    for h in (0, 1):
        for kx in (1, 3, 2):
            recv(f"g{kx}{h}", gh(4 - kx, 0, h))
            send(f"gc{kx}{h}", gh(4 - kx, 0, h), gh(4 - kx, 1, h), other)
    recv("wp0", wpart(0, 3))
    send("wfp", wpart(0, 3), wpart(0, 3), yp)
    recv("wm1", wpart(1, 1))
    send("wfm", wpart(1, 1), wpart(1, 1), ym)
    recv("gc00", gh(0, 1, 0))
    recv("gc01", gh(0, 1, 1))
    for h in (0, 1):
        for kx in (1, 3, 2):
            recv(f"gc{kx}{h}", gh(4 - kx, 1, h))

    tf[...] = dot(hxt[...], gbuf[...])
    ts[...] = tf[...].astype(BF)

    def rows(start, n):
        return pl.ds(pl.multiple_of(start, n), n)

    def place(ks, kz):
        return (at(s, ks) * 4 + at(zl, kz)) * 16

    @pl.loop(0, 15)
    def _(i):
        ks, kz = along_z(i)
        send(T0 + i, ts.at[rows(place(ks, kz), 16)], zr.at[i], dev(ks=ks, kz=kz))

    recv("wp1", wpart(1, 3))
    recv("wm0", wpart(0, 1))
    recv("wfp", wpart(0, 2))
    recv("wfm", wpart(1, 2))
    for k in (1, 2, 3):
        piece = wg.at[at(m, k), pl.ds(pl.multiple_of(c * 1024, 1024), 1024)]
        send(f"wc{k}", piece, piece, other)

    late = len(sent)
    base = (x * 2 + c) * 256

    def add(j, piece):
        i = 14 - j
        recv(T0 + i, zr.at[i])
        return piece + zr[i].astype(F32)

    mine = upd.at[rows(base + z * 16, 16)]
    mine[...] = lax.fori_loop(0, 15, add, tf[rows(z * 16, 16), :]).astype(BF)

    @pl.loop(0, 15)
    def _(i):
        ks, kz = along_z(i)
        send(U0 + i, mine, mine, dev(ks=ks, kz=kz))

    sent_all(T0, 15, ts.at[0:16])
    drain(late)

    for k in (1, 2, 3):
        piece = wg.at[at(m, k), pl.ds(pl.multiple_of((1 - c) * 1024, 1024), 1024)]
        recv(f"wc{k}", piece)
    for k in (1, 3, 2):
        recv(f"dy{k}", dr.at[at(m, 4 - k)])
    for j in range(4):
        weight = wide(*[wg[k, 512 * j : 512 * j + 512, :] for k in range(4)])
        part = dot_nt(wide(dr[0], dr[1], dr[2], dr[3]), weight)
        o_grad[0, :, 512 * j : 512 * j + 512] = part[:52].astype(BF)

    def u64(kx, ks):
        return upd.at[rows(at(x, kx) * 512 + c * 256 + at(s, ks) * 64, 64)]

    def u256(kx, kc):
        return upd.at[rows(at(x, kx) * 512 + (1 - c if kc else c) * 256, 256)]

    for q in (3, 1, 2, 0):
        ks = far_first(q)
        for i in range(4 * q, min(4 * q + 4, 15)):
            source = rows(base + place(4 - ks, 4 - (i + 1) % 4), 16)
            recv(U0 + i, upd.at[source])
        for kx in (2, 1, 3):
            send(f"ux{kx}{ks}", u64(0, 4 - ks), u64(0, 4 - ks), dev(kx=kx))
    send("uc0", u256(0, 0), u256(0, 0), other)
    own = upd[rows(base, 256), :].astype(F32)
    sq[...] = jnp.sum((own * own).reshape(32, 8, COLS), axis=0)
    for k in (1, 3, 2):
        send(f"sy{k}", sq, ysq.at[3 - k], dev(km=k))

    for k in (1, 3, 2):
        recv(f"sy{k}", ysq.at[3 - k])
    xs[...] = sq[...] + ysq[0] + ysq[1] + ysq[2]
    across = [(kx, kc) for kx in (2, 1, 3, 0) for kc in (1, 0) if kx or kc]
    for i, (kx, kc) in enumerate(across):
        send(f"sx{kx}{kc}", xs, xsq.at[i], dev(kx=kx, kc=kc))
    for kx in (1, 3, 2):
        for ks in (0, 1, 3, 2):
            recv(f"ux{kx}{ks}", u64(4 - kx, 4 - ks))
        send(f"uc{kx}", u256(4 - kx, 0), u256(4 - kx, 0), other)
    everything = xs[...]
    for i, (kx, kc) in enumerate(across):
        recv(f"sx{kx}{kc}", xsq.at[i])
        everything = everything + xsq[i]
    o_sq[...] = everything
    sent_all(U0, 15, mine)
    drain(len(sent) - 3)
    recv("uc0", u256(0, 1))
    for kx in (1, 3, 2):
        recv(f"uc{kx}", u256(4 - kx, 1))
    o_upd[...] = upd[...]
    drain(len(sent))


def write_results(grad_ref, raw_ref, sq_ref, o_grad, o_upd):
    o_grad[...] = grad_ref[...]
    scale = lax.rsqrt(jnp.sum(sq_ref[...]) / (D * 2 * HD) + 1e-06)
    o_upd[...] = (raw_ref[...].astype(F32) * scale).astype(BF)


def per_device(
    prefix_hidden, prefix_kv_weight, action_hidden, query_weight, action_kv_weight,
    out_cotangent, prompt_len, view_valid,
):
    vm = pltpu.VMEM
    scratch = [
        vm((ROWS, D), BF), vm((4, D, COLS), BF), vm((ACT, 1024), BF), vm((1024, 512), BF),
        vm((1024, 512), BF), vm((ACT, 512), BF), vm((4, 4, ROWS, COLS), BF), vm((ACTP, 512), BF),
        vm((QR, HD), BF), vm((QR, HD), BF), vm((HD, QR), BF), vm((HD, QR), BF),
        vm((4, ROWS, QR), F32), vm((4, ROWS, QR), F32),
        vm((5, 1, QR), F32), vm((5, 1, QR), F32), vm((5, 1, QR), F32),
        vm((4, 4, ROWS, COLS), F32), vm((4, 4, ROWS, COLS), BF),
        vm((4, 3, ROWS, COLS), BF),
        vm((4, ROWS, COLS), F32), vm((4, ROWS, COLS), BF),
        vm((112, COLS), BF), vm((96, COLS), BF), vm((112, COLS), BF), vm((96, COLS), BF),
        vm((112, COLS), BF), vm((96, COLS), BF), vm((112, COLS), BF), vm((96, COLS), BF),
        vm((ROWS, COLS), F32), vm((8 * ROWS, COLS), BF), vm((8 * ROWS, 256), BF),
        vm((256, 8 * ROWS), BF), vm((256, COLS), F32), vm((256, COLS), BF),
        vm((15, 16, COLS), BF), vm((D, COLS), BF),
        vm((8, 128), F32), vm((3, 8, 128), F32), vm((8, 128), F32), vm((7, 8, 128), F32),
        vm((4, 64, COLS), BF), vm((4, 64, COLS), BF),
        pltpu.SemaphoreType.DMA((7,)),
        pltpu.SemaphoreType.DMA((N_SEMS,)), pltpu.SemaphoreType.DMA((N_SEMS,)),
    ]
    smem = pl.BlockSpec(memory_space=pltpu.SMEM)
    hbm = pl.BlockSpec(memory_space=pltpu.HBM)
    grad, raw, squares = pl.pallas_call(
        kernel,
        out_shape=(
            jax.ShapeDtypeStruct((1, 52, D), BF),
            jax.ShapeDtypeStruct((D, COLS), BF),
            jax.ShapeDtypeStruct((8, 128), F32),
        ),
        in_specs=[smem, smem] + [hbm] * 6,
        out_specs=(pl.BlockSpec(memory_space=pltpu.VMEM),) * 3,
        scratch_shapes=scratch,
        compiler_params=pltpu.CompilerParams(
            collective_id=0, has_side_effects=True, vmem_limit_bytes=40 * 1024 * 1024
        ),
    )(
        prompt_len, view_valid, *[pltpu.with_memory_space_constraint(v, pltpu.HBM) for v in (prefix_hidden, prefix_kv_weight, action_hidden, query_weight, action_kv_weight, out_cotangent)])
    return pl.pallas_call(
        write_results,
        out_shape=(
            jax.ShapeDtypeStruct((1, 52, D), BF),
            jax.ShapeDtypeStruct((D, COLS), BF),
        ),
        in_specs=[pl.BlockSpec(memory_space=pltpu.VMEM)] * 3,
        out_specs=(pl.BlockSpec(memory_space=pltpu.VMEM),) * 2,
        compiler_params=pltpu.CompilerParams(vmem_limit_bytes=40 * 1024 * 1024),
    )(grad, raw, squares)


def solution(mesh):
    return jax.shard_map(
        per_device,
        mesh=mesh,
        in_specs=(
            P("dp", "sample", None),
            P(None, "mp"),
            P("dp", "sample", None),
            P(None, "mp"),
            P(),
            P("dp", "sample", "mp"),
            P("dp"),
            P("dp", None),
        ),
        out_specs=(P("dp", ("sample", "mp"), None), P(None, "mp")),
        check_vma=False,
    )
```

```python
import jax
import jax.numpy as jnp
from jax import lax
from jax.experimental import pallas as pl
from jax.experimental.pallas import tpu as pltpu
from jax.sharding import PartitionSpec as P

BF = jnp.bfloat16
F32 = jnp.float32
D = 2048
HD = 256
ROWS = 208
COLS = 128
ACT = 300
ACTP = 304
QR = 2 * ACTP
VIEW_TOK = 256
VIEWS = 3
HORIZON = 50
NEG = -3.0e38
HALF = ((0, 112), (112, 96))
PART = ((0, 64), (64, 48), (112, 48), (160, 48))
N_SEMS = 160


def dot(a, b):
    return jnp.dot(a, b, preferred_element_type=F32)


def wide(*pieces):
    return jnp.concatenate(pieces, axis=1)


def dot_nt(a, b):
    return lax.dot_general(a, b, (((1,), (1,)), ((), ())), preferred_element_type=F32)


def kernel(
    len_ref, view_ref, hid_h, w_h, act_h, wq_h, wakv_h, cot_h,
    o_grad, o_upd, o_sq,
    hid_v, wg, act_v, wq_v, wakv_v, cot_v, kv, akv, qs, gs, qt, gt, e_s, d_s,
    dkv, st, yb,
    rr, zst, za0, za1, zb0, zb1, zc0, zc1,
    dres, gbuf, hx, hxt, tf, ts, zr, upd,
    sq, ysq, xs, xsq, ds, dr,
    lsem, ssem, rsem,
):
    dp = lax.axis_index("dp")
    s = lax.axis_index("sample")
    m = lax.axis_index("mp")
    x = dp // 8
    zl = lax.rem(dp, 8) // 2
    c = lax.rem(dp, 2)

    def at(a, k):
        return lax.rem(a + k, 4)

    z = s * 4 + zl

    def dev(kx=0, kz=0, ks=0, km=0, kc=0):
        cc = 1 - c if kc else c
        d = at(x, kx) * 8 + at(zl, kz) * 2 + cc
        return {"dp": d, "sample": at(s, ks), "mp": at(m, km)}

    along_z = [(ks, kz) for ks in (2, 1, 3, 0) for kz in (1, 2, 3, 0) if ks or kz]
    zp, zm = dev(ks=1), dev(ks=3)
    other = dev(kc=1)

    index = {}
    sent = []

    def number(name):
        return index.setdefault(name, len(index))

    def send(name, src, dst, device):
        i = number(name)
        copy = pltpu.make_async_remote_copy(
            src_ref=src, dst_ref=dst, send_sem=ssem.at[i], recv_sem=rsem.at[i],
            device_id=device, device_id_type=pl.DeviceIdType.MESH,
        )
        copy.start()
        sent.append(copy)

    def recv(name, dst, device=None):
        i = number(name)
        pltpu.make_async_remote_copy(
            src_ref=dst, dst_ref=dst, send_sem=ssem.at[i], recv_sem=rsem.at[i],
            device_id=other if device is None else device,
            device_id_type=pl.DeviceIdType.MESH,
        ).wait_recv()

    def drain(n):
        for copy in sent[:n]:
            copy.wait_send()
        del sent[:n]

    loads = [
        pltpu.make_async_copy(hid_h.at[0, 0:112], hid_v.at[0:112], lsem.at[0]),
        pltpu.make_async_copy(w_h, wg.at[m], lsem.at[1]),
        pltpu.make_async_copy(act_h.at[0], act_v, lsem.at[2]),
        pltpu.make_async_copy(wq_h, wq_v, lsem.at[3]),
        pltpu.make_async_copy(wakv_h, wakv_v, lsem.at[4]),
        pltpu.make_async_copy(cot_h.at[0], cot_v, lsem.at[5]),
        pltpu.make_async_copy(hid_h.at[0, 112:208], hid_v.at[112:208], lsem.at[6]),
    ]
    for i in (1, 0, 6):
        loads[i].start()

    barrier = pltpu.get_barrier_semaphore()
    peers = [dev(km=k) for k in (1, 2, 3)] + [dev(ks=ks, kz=kz) for ks, kz in along_z] + [other]
    peers += [dev(kx=k, kc=kc) for k in (1, 2, 3) for kc in (0, 1)]
    for peer in peers:
        pl.semaphore_signal(
            barrier, inc=1, device_id=peer, device_id_type=pl.DeviceIdType.MESH
        )

    def kvp(r, i):
        r0, n = PART[i]
        return kv.at[r, m, pl.ds(r0, n)]

    def ysend(r):
        block = kv.at[r, m]
        for k in (2, 1, 3):
            send(f"y{r}{k}", block, block, dev(km=k))

    def ywait(r):
        for k in (1, 3, 2):
            recv(f"y{r}{k}", kv.at[r, at(m, 4 - k)])

    loads[1].wait()
    loads[0].wait()
    for i in (2, 3, 5, 4):
        loads[i].start()
    kv[0, m, 0:112, :] = dot(hid_v[0:112], wg[m]).astype(BF)
    pl.semaphore_wait(barrier, len(peers))
    for i in (0, 1):
        send(f"zp{i}", kvp(0, i), kvp(3, i), zp)
    loads[6].wait()
    kv[0, m, 112:208, :] = dot(hid_v[112:208], wg[m]).astype(BF)
    for i in (2, 3):
        send(f"zm{i}", kvp(0, i), kvp(1, i), zm)
    for i, j in ((2, 0), (3, 1)):
        send(f"zp{i}", kvp(0, i), kvp(3, i), zp)
        send(f"zm{j}", kvp(0, j), kvp(1, j), zm)
    ysend(0)

    def slot(rx, rc):
        return pl.ds((rx * 2 + rc) * ROWS, ROWS)

    def hidden_columns(kx, kc):
        j = at(x, kx) * 2 + (1 - c if kc else c)
        return pl.ds(pl.multiple_of(j * 256, 256), 256)

    def send_hidden(kx):
        for kc in (0, 1):
            send(f"hx{kx}{kc}", hid_v.at[:, hidden_columns(kx, kc)],
                 hx.at[slot(4 - kx, kc)], dev(kx=kx, kc=kc))

    send_hidden(1)
    send_hidden(3)
    send("hx01", hid_v.at[:, hidden_columns(0, 1)], hx.at[slot(0, 1)], other)
    hx[slot(0, 0), :] = hid_v[:, hidden_columns(0, 0)]

    for ref in (qs, gs):
        ref[288:304, :] = jnp.zeros((16, HD), BF)
        ref[592:608, :] = jnp.zeros((16, HD), BF)
    akv[288:304, :] = jnp.zeros((16, 2 * HD), BF)
    loads[2].wait()
    loads[3].wait()
    queries = (dot(act_v[...], wq_v[...]).astype(BF).astype(F32) * (HD**-0.5)).astype(BF)
    qs[0:ACT, :] = queries[:, :HD]
    qs[ACTP : ACTP + ACT, :] = queries[:, HD:]
    loads[4].wait()
    akv[0:ACT, :] = dot(act_v[...], wakv_v[...]).astype(BF)
    loads[5].wait()
    gs[0:ACT, :] = cot_v[:, :HD]
    gs[ACTP : ACTP + ACT, :] = cot_v[:, HD:]

    qt[...] = qs[...].T
    gt[...] = gs[...].T

    block_max, block_sum, block_dot = {}, {}, {}

    def attend(r, keys, values, mask, e_ref, d_ref):
        scores = mask(dot(keys, qt[...]))
        top = jnp.max(scores, axis=0, keepdims=True)
        e = jnp.exp(scores - top)
        d = dot(values, gt[...])
        if e_ref is not None:
            e_ref[...] = e
            d_ref[...] = d
        block_max[r] = top
        block_sum[r] = jnp.sum(e, axis=0, keepdims=True)
        block_dot[r] = jnp.sum(e * d, axis=0, keepdims=True)

    def draw(i):
        total = jnp.zeros_like(i)
        for t in range(1, ACTP // HORIZON + 1):
            total = total + jnp.where(i >= t * HORIZON, 1, 0)
        return total

    for i, j in ((0, 2), (1, 3)):
        recv(f"zp{i}", kvp(3, i))
        send(f"zf{i}", kvp(3, i), kvp(2, i), zp)
        recv(f"zm{j}", kvp(1, j))
        send(f"zf{j}", kvp(1, j), kvp(2, j), zm)

    key_draw = draw(lax.broadcasted_iota(jnp.int32, (ACTP, 1), 0))
    query_index = lax.broadcasted_iota(jnp.int32, (1, QR), 1)
    query_draw = draw(query_index - jnp.where(query_index >= ACTP, ACTP, 0))
    attend(
        "a", akv[:, :HD], akv[:, HD:],
        lambda scores: jnp.where(key_draw == query_draw, scores, NEG), None, None,
    )

    def attend_prefix(r):
        p = at(s, r) * ROWS + lax.broadcasted_iota(jnp.int32, (ROWS, 1), 0)
        usable = jnp.where(p >= VIEWS * VIEW_TOK, jnp.where(p - VIEWS * VIEW_TOK < len_ref[0], 1, 0), 0)
        for v in range(VIEWS):
            inside = jnp.where(p >= v * VIEW_TOK, 1, 0) * jnp.where(p < (v + 1) * VIEW_TOK, 1, 0)
            usable = usable + inside * jnp.where(view_ref[0, v] == 1, 1, 0)
        ceiling = jnp.where(usable > 0, -NEG, NEG)
        attend(
            r, wide(kv[r, 0], kv[r, 1]), wide(kv[r, 2], kv[r, 3]),
            lambda scores: jnp.minimum(scores, ceiling), e_s.at[r], d_s.at[r],
        )

    for i in (2, 3):
        recv(f"zp{i}", kvp(3, i))
    ysend(3)
    for i in (0, 1):
        recv(f"zm{i}", kvp(1, i))
    ysend(1)
    ywait(0)
    attend_prefix(0)
    for i in (0, 2, 1, 3):
        recv(f"zf{i}", kvp(2, i))
    ysend(2)
    send_hidden(2)
    ywait(3)
    attend_prefix(3)
    ywait(1)
    attend_prefix(1)
    ywait(2)
    attend_prefix(2)

    blocks = ("a", 0, 1, 2, 3)
    top = block_max["a"]
    for r in (0, 1, 2, 3):
        top = jnp.maximum(top, block_max[r])
    factor = {r: jnp.exp(block_max[r] - top) for r in blocks}
    total = sum(factor[r] * block_sum[r] for r in blocks)
    inverse = 1.0 / total
    row_dot = sum(factor[r] * block_dot[r] for r in blocks) * inverse

    def half(h):
        r0, n = HALF[h]
        return pl.ds(r0, n)

    def gradients(r, h):
        p = e_s[r, half(h), :] * (factor[r] * inverse)
        d = p * (d_s[r, half(h), :] - row_dot)
        dk = dot(d.astype(BF), qs[...])
        dv = dot(p.astype(BF), gs[...])
        for k in range(4):
            columns = (dk, dv)[k // 2][:, (k % 2) * COLS : (k % 2 + 1) * COLS]
            dkv[r, k, half(h), :] = columns
            st[r, k, half(h), :] = columns.astype(BF)
        for k in (2, 1, 3):
            send(f"r{r}{k}{h}", st.at[r, at(m, k), half(h)], yb.at[r, 3 - k, half(h)], dev(km=k))

    def finish(r, h):
        piece = dkv[r, m, half(h), :]
        for k in (1, 3, 2):
            recv(f"r{r}{k}{h}", yb.at[r, 3 - k, half(h)])
            piece = piece + yb[r, 3 - k, half(h), :].astype(F32)
        return piece

    order = ((2, 0), (2, 1), (1, 1), (3, 0), (1, 0), (3, 1))
    for r, h in order:
        gradients(r, h)
    for i, (r, h) in enumerate(order[:4]):
        zst[r, half(h), :] = finish(r, h).astype(BF)
        target = (za0, za1, zb1, zb0)[i]
        send(f"z{i}", zst.at[r, half(h)], target, zm if i % 2 else zp)
        if i < 2:
            gradients(0, i)
    early = len(sent)
    for i, (r, h), arrived, target in ((4, order[4], za0, zc0), (5, order[5], za1, zc1)):
        piece = finish(r, h)
        recv(f"z{i - 4}", arrived)
        zst[r, half(h), :] = (piece + arrived[...].astype(F32)).astype(BF)
        send(f"z{i}", zst.at[r, half(h)], target, zm if i % 2 else zp)

    def wpart(part, k):
        return wg.at[at(m, k), pl.ds(pl.multiple_of(part * 1024, 1024), 1024)]

    for k in (2, 1, 3):
        send(f"w{k}", wpart(c, 0), wpart(c, 0), dev(km=k))

    for h in (0, 1):
        rr[half(h), :] = finish(0, h)
    for kx in (1, 3, 2):
        for kc in (0, 1):
            recv(f"hx{kx}{kc}", hx.at[slot(4 - kx, kc)])
    recv("hx01", hx.at[slot(0, 1)])
    hxt[...] = hx[...].T
    drain(early)

    def block(rx, rc):
        return gbuf.at[slot(rx, rc)]

    recv("z3", zb0)
    recv("z4", zc0)
    dres[half(0), :] = rr[half(0), :] + zb0[...].astype(F32) + zc0[...].astype(F32)
    recv("z2", zb1)
    recv("z5", zc1)
    dres[half(1), :] = rr[half(1), :] + zb1[...].astype(F32) + zc1[...].astype(F32)
    gbuf[slot(0, 0), :] = dres[...].astype(BF)
    for kx in (2, 1, 3):
        send(f"g{kx}", block(0, 0), block(4 - kx, 0), dev(kx=kx))
    send("gc0", block(0, 0), block(0, 1), other)

    for k in range(4):
        ds[k, 0:52, :] = dres[52 * k : 52 * k + 52, :].astype(BF)
        ds[k, 48:64, :] = jnp.where(
            lax.broadcasted_iota(jnp.int32, (16, COLS), 0) < 4, ds[k, 48:64, :].astype(F32), 0.0
        ).astype(BF)
    for k in (1, 3, 2):
        send(f"dy{k}", ds.at[at(m, k)], dr.at[m], dev(km=k))
    dr[m] = ds[m]

    for kx in (1, 3, 2):
        recv(f"g{kx}", block(4 - kx, 0))
        send(f"gc{kx}", block(4 - kx, 0), block(4 - kx, 1), other)
    for kx in (0, 1, 3, 2):
        recv(f"gc{kx}", block((4 - kx) % 4, 1))

    tf[...] = dot(hxt[...], gbuf[...])
    ts[...] = tf[...].astype(BF)

    def rows(start, n):
        return pl.ds(pl.multiple_of(start, n), n)

    def place(ks, kz):
        return (at(s, ks) * 4 + at(zl, kz)) * 16

    for i, (ks, kz) in enumerate(along_z):
        send(f"t{ks}{kz}", ts.at[rows(place(ks, kz), 16)], zr.at[i], dev(ks=ks, kz=kz))
    for k in (1, 3, 2):
        recv(f"w{k}", wpart(c, 4 - k))
        send(f"wc{k}", wpart(c, 4 - k), wpart(c, 4 - k), other)
    late = len(sent)
    base = (x * 2 + c) * 256
    piece = tf[rows(z * 16, 16), :]
    for i, (ks, kz) in reversed(list(enumerate(along_z))):
        recv(f"t{ks}{kz}", zr.at[i])
        piece = piece + zr[i].astype(F32)
    mine = upd.at[rows(base + z * 16, 16)]
    mine[...] = piece.astype(BF)
    for ks, kz in along_z:
        send(f"u{ks}{kz}", mine, mine, dev(ks=ks, kz=kz))
    drain(late)

    for k in (1, 3, 2):
        recv(f"wc{k}", wpart(1 - c, 4 - k))
    for k in (1, 3, 2):
        recv(f"dy{k}", dr.at[at(m, 4 - k)])
    for j in range(4):
        weight = wide(*[wg[k, 512 * j : 512 * j + 512, :] for k in range(4)])
        part = dot_nt(wide(dr[0], dr[1], dr[2], dr[3]), weight)
        o_grad[0, :, 512 * j : 512 * j + 512] = part[:52].astype(BF)

    def u64(kx, ks):
        return upd.at[rows(at(x, kx) * 512 + c * 256 + at(s, ks) * 64, 64)]

    def u256(kx, kc):
        return upd.at[rows(at(x, kx) * 512 + (1 - c if kc else c) * 256, 256)]

    for ks in (0, 1, 3, 2):
        for kz in (1, 2, 3, 0):
            if ks or kz:
                source = rows(base + place(4 - ks, 4 - kz), 16)
                recv(f"u{ks}{kz}", upd.at[source])
        for kx in (2, 1, 3):
            send(f"ux{kx}{ks}", u64(0, 4 - ks), u64(0, 4 - ks), dev(kx=kx))
    send("uc0", u256(0, 0), u256(0, 0), other)
    own = upd[rows(base, 256), :].astype(F32)
    sq[...] = jnp.sum((own * own).reshape(32, 8, COLS), axis=0)
    for k in (1, 3, 2):
        send(f"sy{k}", sq, ysq.at[3 - k], dev(km=k))

    for k in (1, 3, 2):
        recv(f"sy{k}", ysq.at[3 - k])
    xs[...] = sq[...] + ysq[0] + ysq[1] + ysq[2]
    across = [(kx, kc) for kx in (2, 1, 3, 0) for kc in (1, 0) if kx or kc]
    for i, (kx, kc) in enumerate(across):
        send(f"sx{kx}{kc}", xs, xsq.at[i], dev(kx=kx, kc=kc))
    for kx in (1, 3, 2):
        for ks in (0, 1, 3, 2):
            recv(f"ux{kx}{ks}", u64(4 - kx, 4 - ks))
        send(f"uc{kx}", u256(4 - kx, 0), u256(4 - kx, 0), other)
    everything = xs[...]
    for i, (kx, kc) in enumerate(across):
        recv(f"sx{kx}{kc}", xsq.at[i])
        everything = everything + xsq[i]
    o_sq[...] = everything
    drain(len(sent) - 3)
    recv("uc0", u256(0, 1))
    for kx in (1, 3, 2):
        recv(f"uc{kx}", u256(4 - kx, 1))
    o_upd[...] = upd[...]
    drain(len(sent))


def write_results(grad_ref, raw_ref, sq_ref, o_grad, o_upd):
    o_grad[...] = grad_ref[...]
    scale = lax.rsqrt(jnp.sum(sq_ref[...]) / (D * 2 * HD) + 1e-06)
    o_upd[...] = (raw_ref[...].astype(F32) * scale).astype(BF)


def per_device(
    prefix_hidden, prefix_kv_weight, action_hidden, query_weight, action_kv_weight,
    out_cotangent, prompt_len, view_valid,
):
    vm = pltpu.VMEM
    scratch = [
        vm((ROWS, D), BF), vm((4, D, COLS), BF), vm((ACT, 1024), BF), vm((1024, 512), BF),
        vm((1024, 512), BF), vm((ACT, 512), BF), vm((4, 4, ROWS, COLS), BF), vm((ACTP, 512), BF),
        vm((QR, HD), BF), vm((QR, HD), BF), vm((HD, QR), BF), vm((HD, QR), BF),
        vm((4, ROWS, QR), F32), vm((4, ROWS, QR), F32),
        vm((4, 4, ROWS, COLS), F32), vm((4, 4, ROWS, COLS), BF),
        vm((4, 3, ROWS, COLS), BF),
        vm((ROWS, COLS), F32), vm((4, ROWS, COLS), BF),
        vm((112, COLS), BF), vm((96, COLS), BF), vm((112, COLS), BF), vm((96, COLS), BF),
        vm((112, COLS), BF), vm((96, COLS), BF),
        vm((ROWS, COLS), F32), vm((8 * ROWS, COLS), BF), vm((8 * ROWS, 256), BF),
        vm((256, 8 * ROWS), BF), vm((256, COLS), F32), vm((256, COLS), BF),
        vm((15, 16, COLS), BF), vm((D, COLS), BF),
        vm((8, 128), F32), vm((3, 8, 128), F32), vm((8, 128), F32), vm((7, 8, 128), F32),
        vm((4, 64, COLS), BF), vm((4, 64, COLS), BF),
        pltpu.SemaphoreType.DMA((7,)),
        pltpu.SemaphoreType.DMA((N_SEMS,)), pltpu.SemaphoreType.DMA((N_SEMS,)),
    ]
    smem = pl.BlockSpec(memory_space=pltpu.SMEM)
    hbm = pl.BlockSpec(memory_space=pltpu.HBM)
    grad, raw, squares = pl.pallas_call(
        kernel,
        out_shape=(
            jax.ShapeDtypeStruct((1, 52, D), BF),
            jax.ShapeDtypeStruct((D, COLS), BF),
            jax.ShapeDtypeStruct((8, 128), F32),
        ),
        in_specs=[smem, smem] + [hbm] * 6,
        out_specs=(pl.BlockSpec(memory_space=pltpu.VMEM),) * 3,
        scratch_shapes=scratch,
        compiler_params=pltpu.CompilerParams(
            collective_id=0, has_side_effects=True, vmem_limit_bytes=40 * 1024 * 1024
        ),
    )(
        prompt_len, view_valid, *[pltpu.with_memory_space_constraint(v, pltpu.HBM) for v in (prefix_hidden, prefix_kv_weight, action_hidden, query_weight, action_kv_weight, out_cotangent)])
    return pl.pallas_call(
        write_results,
        out_shape=(
            jax.ShapeDtypeStruct((1, 52, D), BF),
            jax.ShapeDtypeStruct((D, COLS), BF),
        ),
        in_specs=[pl.BlockSpec(memory_space=pltpu.VMEM)] * 3,
        out_specs=(pl.BlockSpec(memory_space=pltpu.VMEM),) * 2,
        compiler_params=pltpu.CompilerParams(vmem_limit_bytes=40 * 1024 * 1024),
    )(grad, raw, squares)


def solution(mesh):
    return jax.shard_map(
        per_device,
        mesh=mesh,
        in_specs=(
            P("dp", "sample", None),
            P(None, "mp"),
            P("dp", "sample", None),
            P(None, "mp"),
            P(),
            P("dp", "sample", "mp"),
            P("dp"),
            P("dp", None),
        ),
        out_specs=(P("dp", ("sample", "mp"), None), P(None, "mp")),
        check_vma=False,
    )
```

```python
import jax
import jax.numpy as jnp
from jax import lax
from jax.experimental import pallas as pl
from jax.experimental.pallas import tpu as pltpu
from jax.sharding import PartitionSpec as P

BF = jnp.bfloat16
F32 = jnp.float32
D = 2048
HD = 256
ROWS = 208
COLS = 128
ACT = 300
ACTP = 304
QR = 2 * ACTP
VIEW_TOK = 256
VIEWS = 3
HORIZON = 50
NEG = -3.0e38
HALF = ((0, 112), (112, 96))
PART = ((0, 64), (64, 48), (112, 48), (160, 48))
N_SEMS = 160


def dot(a, b):
    return jnp.dot(a, b, preferred_element_type=F32)


def wide(*pieces):
    return jnp.concatenate(pieces, axis=1)


def dot_nt(a, b):
    return lax.dot_general(a, b, (((1,), (1,)), ((), ())), preferred_element_type=F32)


def kernel(
    len_ref, view_h, hid_h, w_h, act_h, wq_h, wakv_h, cot_h,
    o_grad, o_upd, o_sq,
    hid_v, wg, act_v, wq_v, wakv_v, cot_v, kv, akv, qs, gs, qt, gt, e_s, d_s,
    dkv, st, ya0, ya1, yb0, yb1, yc0, yc1, sc0, sc1,
    rr, zst, za0, za1, zb0, zb1, zc0, zc1, zsc0, zsc1,
    dres, gbuf, hx, hxt, tf, ts, zr, upd,
    sq, ysq, xs, xsq, ds, dr,
    view_ref, lsem, ssem, rsem,
):
    dp = lax.axis_index("dp")
    s = lax.axis_index("sample")
    m = lax.axis_index("mp")
    x = dp // 8
    zl = lax.rem(dp, 8) // 2
    c = lax.rem(dp, 2)

    def at(a, k):
        return lax.rem(a + k, 4)

    z = s * 4 + zl

    def dev(kx=0, kz=0, ks=0, km=0, kc=0):
        cc = 1 - c if kc else c
        d = at(x, kx) * 8 + at(zl, kz) * 2 + cc
        return {"dp": d, "sample": at(s, ks), "mp": at(m, km)}

    along_z = [(ks, kz) for ks in (2, 1, 3, 0) for kz in (1, 2, 3, 0) if ks or kz]
    yp, ym = dev(km=1), dev(km=3)
    zp, zm = dev(ks=1), dev(ks=3)
    xp, xm = dev(kx=1), dev(kx=3)
    other = dev(kc=1)

    index = {}
    sent = []

    def number(name):
        return index.setdefault(name, len(index))

    def send(name, src, dst, device):
        i = number(name)
        copy = pltpu.make_async_remote_copy(
            src_ref=src, dst_ref=dst, send_sem=ssem.at[i], recv_sem=rsem.at[i],
            device_id=device, device_id_type=pl.DeviceIdType.MESH,
        )
        copy.start()
        sent.append(copy)

    def recv(name, dst, device=None):
        i = number(name)
        pltpu.make_async_remote_copy(
            src_ref=dst, dst_ref=dst, send_sem=ssem.at[i], recv_sem=rsem.at[i],
            device_id=other if device is None else device,
            device_id_type=pl.DeviceIdType.MESH,
        ).wait_recv()

    def drain(n):
        for copy in sent[:n]:
            copy.wait_send()
        del sent[:n]

    loads = [
        pltpu.make_async_copy(hid_h.at[0, 0:112], hid_v.at[0:112], lsem.at[0]),
        pltpu.make_async_copy(w_h, wg.at[m], lsem.at[1]),
        pltpu.make_async_copy(act_h.at[0], act_v, lsem.at[2]),
        pltpu.make_async_copy(wq_h, wq_v, lsem.at[3]),
        pltpu.make_async_copy(wakv_h, wakv_v, lsem.at[4]),
        pltpu.make_async_copy(cot_h.at[0], cot_v, lsem.at[5]),
        pltpu.make_async_copy(hid_h.at[0, 112:208], hid_v.at[112:208], lsem.at[6]),
    ]
    loads.append(pltpu.make_async_copy(view_h, view_ref, lsem.at[7]))
    for i in (1, 0, 6, 7):
        loads[i].start()

    barrier = pltpu.get_barrier_semaphore()
    peers = [dev(km=k) for k in (1, 2, 3)] + [dev(ks=ks, kz=kz) for ks, kz in along_z] + [other]
    peers += [dev(kx=k, kc=kc) for k in (1, 2, 3) for kc in (0, 1)]
    for peer in peers:
        pl.semaphore_signal(
            barrier, inc=1, device_id=peer, device_id_type=pl.DeviceIdType.MESH
        )

    def kvp(r, i):
        r0, n = PART[i]
        return kv.at[r, m, pl.ds(r0, n)]

    def ysend(r):
        block = kv.at[r, m]
        for k in (2, 1, 3):
            send(f"y{r}{k}", block, block, dev(km=k))

    def ywait(r):
        for k in (1, 3, 2):
            recv(f"y{r}{k}", kv.at[r, at(m, 4 - k)])

    loads[1].wait()
    loads[0].wait()
    for i in (2, 3, 5, 4):
        loads[i].start()
    kv[0, m, 0:112, :] = dot(hid_v[0:112], wg[m]).astype(BF)
    pl.semaphore_wait(barrier, len(peers))
    for i in (0, 1):
        send(f"zp{i}", kvp(0, i), kvp(3, i), zp)
    loads[6].wait()
    kv[0, m, 112:208, :] = dot(hid_v[112:208], wg[m]).astype(BF)
    for i in (2, 3):
        send(f"zm{i}", kvp(0, i), kvp(1, i), zm)
    for i, j in ((2, 0), (3, 1)):
        send(f"zp{i}", kvp(0, i), kvp(3, i), zp)
        send(f"zm{j}", kvp(0, j), kvp(1, j), zm)
    ysend(0)

    def slot(rx, rc):
        return pl.ds((rx * 2 + rc) * ROWS, ROWS)

    def hidden_columns(kx, kc):
        j = at(x, kx) * 2 + (1 - c if kc else c)
        return pl.ds(pl.multiple_of(j * 256, 256), 256)

    def send_hidden(kx):
        for kc in (0, 1):
            send(f"hx{kx}{kc}", hid_v.at[:, hidden_columns(kx, kc)],
                 hx.at[slot(4 - kx, kc)], dev(kx=kx, kc=kc))

    send_hidden(1)
    send_hidden(3)
    send("hx01", hid_v.at[:, hidden_columns(0, 1)], hx.at[slot(0, 1)], other)
    hx[slot(0, 0), :] = hid_v[:, hidden_columns(0, 0)]

    for ref in (qs, gs):
        ref[288:304, :] = jnp.zeros((16, HD), BF)
        ref[592:608, :] = jnp.zeros((16, HD), BF)
    akv[288:304, :] = jnp.zeros((16, 2 * HD), BF)
    loads[2].wait()
    loads[3].wait()
    queries = (dot(act_v[...], wq_v[...]).astype(BF).astype(F32) * (HD**-0.5)).astype(BF)
    qs[0:ACT, :] = queries[:, :HD]
    qs[ACTP : ACTP + ACT, :] = queries[:, HD:]
    loads[4].wait()
    akv[0:ACT, :] = dot(act_v[...], wakv_v[...]).astype(BF)
    loads[5].wait()
    gs[0:ACT, :] = cot_v[:, :HD]
    gs[ACTP : ACTP + ACT, :] = cot_v[:, HD:]

    qt[...] = qs[...].T
    gt[...] = gs[...].T

    block_max, block_sum, block_dot = {}, {}, {}

    def attend(r, keys, values, mask, e_ref, d_ref):
        scores = mask(dot(keys, qt[...]))
        top = jnp.max(scores, axis=0, keepdims=True)
        e = jnp.exp(scores - top)
        d = dot(values, gt[...])
        if e_ref is not None:
            e_ref[...] = e
            d_ref[...] = d
        block_max[r] = top
        block_sum[r] = jnp.sum(e, axis=0, keepdims=True)
        block_dot[r] = jnp.sum(e * d, axis=0, keepdims=True)

    def draw(i):
        total = jnp.zeros_like(i)
        for t in range(1, ACTP // HORIZON + 1):
            total = total + jnp.where(i >= t * HORIZON, 1, 0)
        return total

    for i, j in ((0, 2), (1, 3)):
        recv(f"zp{i}", kvp(3, i))
        send(f"zf{i}", kvp(3, i), kvp(2, i), zp)
        recv(f"zm{j}", kvp(1, j))
        send(f"zf{j}", kvp(1, j), kvp(2, j), zm)

    key_draw = draw(lax.broadcasted_iota(jnp.int32, (ACTP, 1), 0))
    query_index = lax.broadcasted_iota(jnp.int32, (1, QR), 1)
    query_draw = draw(query_index - jnp.where(query_index >= ACTP, ACTP, 0))
    attend(
        "a", akv[:, :HD], akv[:, HD:],
        lambda scores: jnp.where(key_draw == query_draw, scores, NEG), None, None,
    )

    loads[7].wait()

    def attend_prefix(r):
        p = at(s, r) * ROWS + lax.broadcasted_iota(jnp.int32, (ROWS, 1), 0)
        usable = jnp.where(p >= VIEWS * VIEW_TOK, jnp.where(p - VIEWS * VIEW_TOK < len_ref[0], 1, 0), 0)
        for v in range(VIEWS):
            inside = jnp.where(p >= v * VIEW_TOK, 1, 0) * jnp.where(p < (v + 1) * VIEW_TOK, 1, 0)
            usable = usable + inside * jnp.where(view_ref[0, v] == 1, 1, 0)
        ceiling = jnp.where(usable > 0, -NEG, NEG)
        attend(
            r, wide(kv[r, 0], kv[r, 1]), wide(kv[r, 2], kv[r, 3]),
            lambda scores: jnp.minimum(scores, ceiling), e_s.at[r], d_s.at[r],
        )

    for i in (2, 3):
        recv(f"zp{i}", kvp(3, i))
    ysend(3)
    for i in (0, 1):
        recv(f"zm{i}", kvp(1, i))
    ysend(1)
    ywait(0)
    attend_prefix(0)
    for i in (0, 2, 1, 3):
        recv(f"zf{i}", kvp(2, i))
    ysend(2)
    send_hidden(2)
    ywait(3)
    attend_prefix(3)
    ywait(1)
    attend_prefix(1)
    ywait(2)
    attend_prefix(2)

    blocks = ("a", 0, 1, 2, 3)
    top = block_max["a"]
    for r in (0, 1, 2, 3):
        top = jnp.maximum(top, block_max[r])
    factor = {r: jnp.exp(block_max[r] - top) for r in blocks}
    total = sum(factor[r] * block_sum[r] for r in blocks)
    inverse = 1.0 / total
    row_dot = sum(factor[r] * block_dot[r] for r in blocks) * inverse

    def half(h):
        r0, n = HALF[h]
        return pl.ds(r0, n)

    def gradients(r):
        p = e_s[r] * (factor[r] * inverse)
        d = p * (d_s[r] - row_dot)
        dk = dot(d.astype(BF), qs[...])
        dv = dot(p.astype(BF), gs[...])
        for k in range(4):
            half_block = (dk, dv)[k // 2][:, (k % 2) * COLS : (k % 2 + 1) * COLS]
            dkv[r, k] = half_block
            st[r, k] = half_block.astype(BF)
        send(f"ra{r}p", st.at[r, at(m, 2), half(0)], ya0.at[r], yp)
        send(f"ra{r}m", st.at[r, at(m, 2), half(1)], ya1.at[r], ym)
        send(f"rb{r}p", st.at[r, at(m, 1), half(1)], yb1.at[r], yp)
        send(f"rb{r}m", st.at[r, at(m, 3), half(0)], yb0.at[r], ym)

    def combine(r):
        recv(f"ra{r}p", ya0.at[r])
        sc0[r] = (dkv[r, at(m, 1), half(0), :] + ya0[r].astype(F32)).astype(BF)
        send(f"rc{r}p", sc0.at[r], yc0.at[r], yp)
        recv(f"ra{r}m", ya1.at[r])
        sc1[r] = (dkv[r, at(m, 3), half(1), :] + ya1[r].astype(F32)).astype(BF)
        send(f"rc{r}m", sc1.at[r], yc1.at[r], ym)

    def finish(r):
        recv(f"rb{r}m", yb0.at[r])
        recv(f"rc{r}p", yc0.at[r])
        rr[r, half(0), :] = dkv[r, m, half(0), :] + yb0[r].astype(F32) + yc0[r].astype(F32)
        recv(f"rb{r}p", yb1.at[r])
        recv(f"rc{r}m", yc1.at[r])
        rr[r, half(1), :] = dkv[r, m, half(1), :] + yb1[r].astype(F32) + yc1[r].astype(F32)
        if r:
            zst[r] = rr[r].astype(BF)

    gradients(2)
    gradients(1)
    combine(2)
    gradients(3)
    combine(1)
    gradients(0)
    combine(3)
    finish(2)
    send("zap", zst.at[2, half(0)], za0, zp)
    send("zam", zst.at[2, half(1)], za1, zm)
    finish(1)
    send("zbp", zst.at[1, half(1)], zb1, zp)
    combine(0)
    finish(3)
    send("zbm", zst.at[3, half(0)], zb0, zm)
    early = len(sent)
    recv("zap", za0)
    zsc0[...] = (rr[1, half(0), :] + za0[...].astype(F32)).astype(BF)
    send("zcp", zsc0, zc0, zp)
    recv("zam", za1)
    zsc1[...] = (rr[3, half(1), :] + za1[...].astype(F32)).astype(BF)
    send("zcm", zsc1, zc1, zm)

    def wpart(q, k):
        return wg.at[at(m, k), pl.ds(pl.multiple_of(c * 1024 + q * 512, 512), 512)]

    send("wp0", wpart(0, 0), wpart(0, 0), yp)
    send("wm1", wpart(1, 0), wpart(1, 0), ym)
    send("wp1", wpart(1, 0), wpart(1, 0), yp)
    send("wm0", wpart(0, 0), wpart(0, 0), ym)

    finish(0)
    for kx in (1, 3, 2):
        for kc in (0, 1):
            recv(f"hx{kx}{kc}", hx.at[slot(4 - kx, kc)])
    recv("hx01", hx.at[slot(0, 1)])
    hxt[...] = hx[...].T
    drain(early)

    def gh(rx, rc, h):
        r0, n = HALF[h]
        return gbuf.at[pl.ds((rx * 2 + rc) * ROWS + r0, n)]

    recv("zbm", zb0)
    recv("zcp", zc0)
    dres[half(0), :] = rr[0, half(0), :] + zb0[...].astype(F32) + zc0[...].astype(F32)
    gbuf[half(0), :] = dres[half(0), :].astype(BF)
    for kx in (2, 1, 3):
        send(f"g{kx}0", gh(0, 0, 0), gh(4 - kx, 0, 0), dev(kx=kx))
    send("gc00", gh(0, 0, 0), gh(0, 1, 0), other)
    recv("zbp", zb1)
    recv("zcm", zc1)
    dres[half(1), :] = rr[0, half(1), :] + zb1[...].astype(F32) + zc1[...].astype(F32)
    gbuf[half(1), :] = dres[half(1), :].astype(BF)
    for kx in (2, 1, 3):
        send(f"g{kx}1", gh(0, 0, 1), gh(4 - kx, 0, 1), dev(kx=kx))
    send("gc01", gh(0, 0, 1), gh(0, 1, 1), other)

    for k in range(4):
        ds[k, 0:52, :] = dres[52 * k : 52 * k + 52, :].astype(BF)
        ds[k, 48:64, :] = jnp.where(
            lax.broadcasted_iota(jnp.int32, (16, COLS), 0) < 4, ds[k, 48:64, :].astype(F32), 0.0
        ).astype(BF)
    for k in (1, 3, 2):
        send(f"dy{k}", ds.at[at(m, k)], dr.at[m], dev(km=k))
    dr[m] = ds[m]

    for h in (0, 1):
        for kx in (1, 3, 2):
            recv(f"g{kx}{h}", gh(4 - kx, 0, h))
            send(f"gc{kx}{h}", gh(4 - kx, 0, h), gh(4 - kx, 1, h), other)
    recv("wp0", wpart(0, 3))
    send("wfp", wpart(0, 3), wpart(0, 3), yp)
    recv("wm1", wpart(1, 1))
    send("wfm", wpart(1, 1), wpart(1, 1), ym)
    recv("gc00", gh(0, 1, 0))
    recv("gc01", gh(0, 1, 1))
    for h in (0, 1):
        for kx in (1, 3, 2):
            recv(f"gc{kx}{h}", gh(4 - kx, 1, h))

    tf[...] = dot(hxt[...], gbuf[...])
    ts[...] = tf[...].astype(BF)

    def rows(start, n):
        return pl.ds(pl.multiple_of(start, n), n)

    def place(ks, kz):
        return (at(s, ks) * 4 + at(zl, kz)) * 16

    for i, (ks, kz) in enumerate(along_z):
        send(f"t{ks}{kz}", ts.at[rows(place(ks, kz), 16)], zr.at[i], dev(ks=ks, kz=kz))
    recv("wp1", wpart(1, 3))
    recv("wm0", wpart(0, 1))
    recv("wfp", wpart(0, 2))
    recv("wfm", wpart(1, 2))
    for k in (1, 2, 3):
        piece = wg.at[at(m, k), pl.ds(pl.multiple_of(c * 1024, 1024), 1024)]
        send(f"wc{k}", piece, piece, other)

    late = len(sent)
    base = (x * 2 + c) * 256
    piece = tf[rows(z * 16, 16), :]
    for i, (ks, kz) in reversed(list(enumerate(along_z))):
        recv(f"t{ks}{kz}", zr.at[i])
        piece = piece + zr[i].astype(F32)
    mine = upd.at[rows(base + z * 16, 16)]
    mine[...] = piece.astype(BF)
    for ks, kz in along_z:
        send(f"u{ks}{kz}", mine, mine, dev(ks=ks, kz=kz))
    drain(late)

    for k in (1, 2, 3):
        piece = wg.at[at(m, k), pl.ds(pl.multiple_of((1 - c) * 1024, 1024), 1024)]
        recv(f"wc{k}", piece)
    for k in (1, 3, 2):
        recv(f"dy{k}", dr.at[at(m, 4 - k)])
    for j in range(4):
        weight = wide(*[wg[k, 512 * j : 512 * j + 512, :] for k in range(4)])
        part = dot_nt(wide(dr[0], dr[1], dr[2], dr[3]), weight)
        o_grad[0, :, 512 * j : 512 * j + 512] = part[:52].astype(BF)

    def u64(kx, ks):
        return upd.at[rows(at(x, kx) * 512 + c * 256 + at(s, ks) * 64, 64)]

    def u256(kx, kc):
        return upd.at[rows(at(x, kx) * 512 + (1 - c if kc else c) * 256, 256)]

    for ks in (0, 1, 3, 2):
        for kz in (1, 2, 3, 0):
            if ks or kz:
                source = rows(base + place(4 - ks, 4 - kz), 16)
                recv(f"u{ks}{kz}", upd.at[source])
        for kx in (2, 1, 3):
            send(f"ux{kx}{ks}", u64(0, 4 - ks), u64(0, 4 - ks), dev(kx=kx))
    send("uc0", u256(0, 0), u256(0, 0), other)
    own = upd[rows(base, 256), :].astype(F32)
    sq[...] = jnp.sum((own * own).reshape(32, 8, COLS), axis=0)
    for k in (1, 3, 2):
        send(f"sy{k}", sq, ysq.at[3 - k], dev(km=k))

    for k in (1, 3, 2):
        recv(f"sy{k}", ysq.at[3 - k])
    xs[...] = sq[...] + ysq[0] + ysq[1] + ysq[2]
    across = [(kx, kc) for kx in (2, 1, 3, 0) for kc in (1, 0) if kx or kc]
    for i, (kx, kc) in enumerate(across):
        send(f"sx{kx}{kc}", xs, xsq.at[i], dev(kx=kx, kc=kc))
    for kx in (1, 3, 2):
        for ks in (0, 1, 3, 2):
            recv(f"ux{kx}{ks}", u64(4 - kx, 4 - ks))
        send(f"uc{kx}", u256(4 - kx, 0), u256(4 - kx, 0), other)
    everything = xs[...]
    for i, (kx, kc) in enumerate(across):
        recv(f"sx{kx}{kc}", xsq.at[i])
        everything = everything + xsq[i]
    o_sq[...] = everything
    drain(len(sent) - 3)
    recv("uc0", u256(0, 1))
    for kx in (1, 3, 2):
        recv(f"uc{kx}", u256(4 - kx, 1))
    o_upd[...] = upd[...]
    drain(len(sent))


def write_results(grad_ref, raw_ref, sq_ref, o_grad, o_upd):
    o_grad[...] = grad_ref[...]
    scale = lax.rsqrt(jnp.sum(sq_ref[...]) / (D * 2 * HD) + 1e-06)
    o_upd[...] = (raw_ref[...].astype(F32) * scale).astype(BF)


def per_device(
    prefix_hidden, prefix_kv_weight, action_hidden, query_weight, action_kv_weight,
    out_cotangent, prompt_len, view_valid,
):
    vm = pltpu.VMEM
    scratch = [
        vm((ROWS, D), BF), vm((4, D, COLS), BF), vm((ACT, 1024), BF), vm((1024, 512), BF),
        vm((1024, 512), BF), vm((ACT, 512), BF), vm((4, 4, ROWS, COLS), BF), vm((ACTP, 512), BF),
        vm((QR, HD), BF), vm((QR, HD), BF), vm((HD, QR), BF), vm((HD, QR), BF),
        vm((4, ROWS, QR), F32), vm((4, ROWS, QR), F32),
        vm((4, 4, ROWS, COLS), F32), vm((4, 4, ROWS, COLS), BF),
        vm((4, 112, COLS), BF), vm((4, 96, COLS), BF), vm((4, 112, COLS), BF),
        vm((4, 96, COLS), BF), vm((4, 112, COLS), BF), vm((4, 96, COLS), BF),
        vm((4, 112, COLS), BF), vm((4, 96, COLS), BF),
        vm((4, ROWS, COLS), F32), vm((4, ROWS, COLS), BF),
        vm((112, COLS), BF), vm((96, COLS), BF), vm((112, COLS), BF), vm((96, COLS), BF),
        vm((112, COLS), BF), vm((96, COLS), BF), vm((112, COLS), BF), vm((96, COLS), BF),
        vm((ROWS, COLS), F32), vm((8 * ROWS, COLS), BF), vm((8 * ROWS, 256), BF),
        vm((256, 8 * ROWS), BF), vm((256, COLS), F32), vm((256, COLS), BF),
        vm((15, 16, COLS), BF), vm((D, COLS), BF),
        vm((8, 128), F32), vm((3, 8, 128), F32), vm((8, 128), F32), vm((7, 8, 128), F32),
        vm((4, 64, COLS), BF), vm((4, 64, COLS), BF),
        pltpu.SMEM((1, VIEWS), jnp.int32),
        pltpu.SemaphoreType.DMA((8,)),
        pltpu.SemaphoreType.DMA((N_SEMS,)), pltpu.SemaphoreType.DMA((N_SEMS,)),
    ]
    smem = pl.BlockSpec(memory_space=pltpu.SMEM)
    hbm = pl.BlockSpec(memory_space=pltpu.HBM)
    grad, raw, squares = pl.pallas_call(
        kernel,
        out_shape=(
            jax.ShapeDtypeStruct((1, 52, D), BF),
            jax.ShapeDtypeStruct((D, COLS), BF),
            jax.ShapeDtypeStruct((8, 128), F32),
        ),
        in_specs=[smem] + [hbm] * 7,
        out_specs=(pl.BlockSpec(memory_space=pltpu.VMEM),) * 3,
        scratch_shapes=scratch,
        compiler_params=pltpu.CompilerParams(
            collective_id=0, has_side_effects=True, vmem_limit_bytes=40 * 1024 * 1024
        ),
    )(
        prompt_len, *[pltpu.with_memory_space_constraint(v, pltpu.HBM) for v in (view_valid, prefix_hidden, prefix_kv_weight, action_hidden, query_weight, action_kv_weight, out_cotangent)])
    return pl.pallas_call(
        write_results,
        out_shape=(
            jax.ShapeDtypeStruct((1, 52, D), BF),
            jax.ShapeDtypeStruct((D, COLS), BF),
        ),
        in_specs=[pl.BlockSpec(memory_space=pltpu.VMEM)] * 3,
        out_specs=(pl.BlockSpec(memory_space=pltpu.VMEM),) * 2,
        compiler_params=pltpu.CompilerParams(vmem_limit_bytes=40 * 1024 * 1024),
    )(grad, raw, squares)


def solution(mesh):
    return jax.shard_map(
        per_device,
        mesh=mesh,
        in_specs=(
            P("dp", "sample", None),
            P(None, "mp"),
            P("dp", "sample", None),
            P(None, "mp"),
            P(),
            P("dp", "sample", "mp"),
            P("dp"),
            P("dp", None),
        ),
        out_specs=(P("dp", ("sample", "mp"), None), P(None, "mp")),
        check_vma=False,
    )
```

```python
import jax
import jax.numpy as jnp
from jax import lax
from jax.experimental import pallas as pl
from jax.experimental.pallas import tpu as pltpu
from jax.sharding import PartitionSpec as P

BF = jnp.bfloat16
F32 = jnp.float32
D = 2048
HD = 256
ROWS = 208
COLS = 128
ACT = 300
ACTP = 304
QR = 2 * ACTP
VIEW_TOK = 256
VIEWS = 3
HORIZON = 50
NEG = -3.0e38
HALF = ((0, 112), (112, 96))
PART = ((0, 64), (64, 48), (112, 48), (160, 48))
N_SEMS = 160


def dot(a, b):
    return jnp.dot(a, b, preferred_element_type=F32)


def wide(*pieces):
    return jnp.concatenate(pieces, axis=1)


def dot_nt(a, b):
    return lax.dot_general(a, b, (((1,), (1,)), ((), ())), preferred_element_type=F32)


def kernel(
    len_ref, view_h, hid_h, w_h, act_h, wq_h, wakv_h, cot_h,
    o_grad, o_upd, o_sq,
    hid_v, wg, act_v, wq_v, wakv_v, cot_v, kv, akv, qs, gs, qt, gt, e_s, d_s,
    dkv, st, yb,
    rr, zst, za0, za1, zb0, zb1, zc0, zc1,
    dres, gbuf, hx, hxt, tf, ts, zr, upd,
    sq, ysq, xs, xsq, ds, dr,
    view_ref, lsem, ssem, rsem,
):
    dp = lax.axis_index("dp")
    s = lax.axis_index("sample")
    m = lax.axis_index("mp")
    x = dp // 8
    zl = lax.rem(dp, 8) // 2
    c = lax.rem(dp, 2)

    def at(a, k):
        return lax.rem(a + k, 4)

    z = s * 4 + zl

    def dev(kx=0, kz=0, ks=0, km=0, kc=0):
        cc = 1 - c if kc else c
        d = at(x, kx) * 8 + at(zl, kz) * 2 + cc
        return {"dp": d, "sample": at(s, ks), "mp": at(m, km)}

    along_z = [(ks, kz) for ks in (2, 1, 3, 0) for kz in (1, 2, 3, 0) if ks or kz]
    zp, zm = dev(ks=1), dev(ks=3)
    other = dev(kc=1)

    index = {}
    sent = []

    def number(name):
        return index.setdefault(name, len(index))

    def send(name, src, dst, device):
        i = number(name)
        copy = pltpu.make_async_remote_copy(
            src_ref=src, dst_ref=dst, send_sem=ssem.at[i], recv_sem=rsem.at[i],
            device_id=device, device_id_type=pl.DeviceIdType.MESH,
        )
        copy.start()
        sent.append(copy)

    def recv(name, dst, device=None):
        i = number(name)
        pltpu.make_async_remote_copy(
            src_ref=dst, dst_ref=dst, send_sem=ssem.at[i], recv_sem=rsem.at[i],
            device_id=other if device is None else device,
            device_id_type=pl.DeviceIdType.MESH,
        ).wait_recv()

    def drain(n):
        for copy in sent[:n]:
            copy.wait_send()
        del sent[:n]

    loads = [
        pltpu.make_async_copy(hid_h.at[0, 0:112], hid_v.at[0:112], lsem.at[0]),
        pltpu.make_async_copy(w_h, wg.at[m], lsem.at[1]),
        pltpu.make_async_copy(act_h.at[0], act_v, lsem.at[2]),
        pltpu.make_async_copy(wq_h, wq_v, lsem.at[3]),
        pltpu.make_async_copy(wakv_h, wakv_v, lsem.at[4]),
        pltpu.make_async_copy(cot_h.at[0], cot_v, lsem.at[5]),
        pltpu.make_async_copy(hid_h.at[0, 112:208], hid_v.at[112:208], lsem.at[6]),
    ]
    loads.append(pltpu.make_async_copy(view_h, view_ref, lsem.at[7]))
    for i in (1, 0, 6, 7):
        loads[i].start()

    barrier = pltpu.get_barrier_semaphore()
    peers = [dev(km=k) for k in (1, 2, 3)] + [dev(ks=ks, kz=kz) for ks, kz in along_z] + [other]
    peers += [dev(kx=k, kc=kc) for k in (1, 2, 3) for kc in (0, 1)]
    for peer in peers:
        pl.semaphore_signal(
            barrier, inc=1, device_id=peer, device_id_type=pl.DeviceIdType.MESH
        )

    def kvp(r, i):
        r0, n = PART[i]
        return kv.at[r, m, pl.ds(r0, n)]

    def ysend(r, h):
        r0, n = HALF[h]
        block = kv.at[r, m, pl.ds(r0, n)]
        for k in (2, 1, 3):
            send(f"y{r}{k}{h}", block, block, dev(km=k))

    def ywait(r):
        for h in (0, 1):
            r0, n = HALF[h]
            for k in (1, 3, 2):
                recv(f"y{r}{k}{h}", kv.at[r, at(m, 4 - k), pl.ds(r0, n)])

    loads[1].wait()
    loads[0].wait()
    for i in (2, 3, 5, 4):
        loads[i].start()
    kv[0, m, 0:112, :] = dot(hid_v[0:112], wg[m]).astype(BF)
    pl.semaphore_wait(barrier, len(peers))
    for i in (0, 1):
        send(f"zp{i}", kvp(0, i), kvp(3, i), zp)
    loads[6].wait()
    kv[0, m, 112:208, :] = dot(hid_v[112:208], wg[m]).astype(BF)
    for i in (2, 3):
        send(f"zm{i}", kvp(0, i), kvp(1, i), zm)
    for i, j in ((2, 0), (3, 1)):
        send(f"zp{i}", kvp(0, i), kvp(3, i), zp)
        send(f"zm{j}", kvp(0, j), kvp(1, j), zm)
    ysend(0, 0)
    ysend(0, 1)

    def slot(rx, rc):
        return pl.ds((rx * 2 + rc) * ROWS, ROWS)

    def hidden_columns(kx, kc):
        j = at(x, kx) * 2 + (1 - c if kc else c)
        return pl.ds(pl.multiple_of(j * 256, 256), 256)

    def send_hidden(kx):
        for kc in (0, 1):
            send(f"hx{kx}{kc}", hid_v.at[:, hidden_columns(kx, kc)],
                 hx.at[slot(4 - kx, kc)], dev(kx=kx, kc=kc))

    send_hidden(1)
    send_hidden(3)
    send("hx01", hid_v.at[:, hidden_columns(0, 1)], hx.at[slot(0, 1)], other)
    hx[slot(0, 0), :] = hid_v[:, hidden_columns(0, 0)]

    for ref in (qs, gs):
        ref[288:304, :] = jnp.zeros((16, HD), BF)
        ref[592:608, :] = jnp.zeros((16, HD), BF)
    akv[288:304, :] = jnp.zeros((16, 2 * HD), BF)
    loads[2].wait()
    loads[3].wait()
    queries = (dot(act_v[...], wq_v[...]).astype(BF).astype(F32) * (HD**-0.5)).astype(BF)
    qs[0:ACT, :] = queries[:, :HD]
    qs[ACTP : ACTP + ACT, :] = queries[:, HD:]
    loads[4].wait()
    akv[0:ACT, :] = dot(act_v[...], wakv_v[...]).astype(BF)
    loads[5].wait()
    gs[0:ACT, :] = cot_v[:, :HD]
    gs[ACTP : ACTP + ACT, :] = cot_v[:, HD:]

    qt[...] = qs[...].T
    gt[...] = gs[...].T

    block_max, block_sum, block_dot = {}, {}, {}

    def attend(r, keys, values, mask, e_ref, d_ref):
        scores = mask(dot(keys, qt[...]))
        top = jnp.max(scores, axis=0, keepdims=True)
        e = jnp.exp(scores - top)
        d = dot(values, gt[...])
        if e_ref is not None:
            e_ref[...] = e
            d_ref[...] = d
        block_max[r] = top
        block_sum[r] = jnp.sum(e, axis=0, keepdims=True)
        block_dot[r] = jnp.sum(e * d, axis=0, keepdims=True)

    def draw(i):
        total = jnp.zeros_like(i)
        for t in range(1, ACTP // HORIZON + 1):
            total = total + jnp.where(i >= t * HORIZON, 1, 0)
        return total

    for i, j in ((0, 2), (1, 3)):
        recv(f"zp{i}", kvp(3, i))
        send(f"zf{i}", kvp(3, i), kvp(2, i), zp)
        recv(f"zm{j}", kvp(1, j))
        send(f"zf{j}", kvp(1, j), kvp(2, j), zm)
    ysend(3, 0)
    ysend(1, 1)

    key_draw = draw(lax.broadcasted_iota(jnp.int32, (ACTP, 1), 0))
    query_index = lax.broadcasted_iota(jnp.int32, (1, QR), 1)
    query_draw = draw(query_index - jnp.where(query_index >= ACTP, ACTP, 0))
    attend(
        "a", akv[:, :HD], akv[:, HD:],
        lambda scores: jnp.where(key_draw == query_draw, scores, NEG), None, None,
    )

    loads[7].wait()

    def attend_prefix(r):
        p = at(s, r) * ROWS + lax.broadcasted_iota(jnp.int32, (ROWS, 1), 0)
        usable = jnp.where(p >= VIEWS * VIEW_TOK, jnp.where(p - VIEWS * VIEW_TOK < len_ref[0], 1, 0), 0)
        for v in range(VIEWS):
            inside = jnp.where(p >= v * VIEW_TOK, 1, 0) * jnp.where(p < (v + 1) * VIEW_TOK, 1, 0)
            usable = usable + inside * jnp.where(view_ref[0, v] == 1, 1, 0)
        ceiling = jnp.where(usable > 0, -NEG, NEG)
        attend(
            r, wide(kv[r, 0], kv[r, 1]), wide(kv[r, 2], kv[r, 3]),
            lambda scores: jnp.minimum(scores, ceiling), e_s.at[r], d_s.at[r],
        )

    for i in (2, 3):
        recv(f"zp{i}", kvp(3, i))
    ysend(3, 1)
    for i in (0, 1):
        recv(f"zm{i}", kvp(1, i))
    ysend(1, 0)
    ywait(0)
    attend_prefix(0)
    for i in (0, 1):
        recv(f"zf{i}", kvp(2, i))
    ysend(2, 0)
    for i in (2, 3):
        recv(f"zf{i}", kvp(2, i))
    ysend(2, 1)
    send_hidden(2)
    ywait(3)
    attend_prefix(3)
    ywait(1)
    attend_prefix(1)
    ywait(2)
    attend_prefix(2)

    blocks = ("a", 0, 1, 2, 3)
    top = block_max["a"]
    for r in (0, 1, 2, 3):
        top = jnp.maximum(top, block_max[r])
    factor = {r: jnp.exp(block_max[r] - top) for r in blocks}
    total = sum(factor[r] * block_sum[r] for r in blocks)
    inverse = 1.0 / total
    row_dot = sum(factor[r] * block_dot[r] for r in blocks) * inverse

    def half(h):
        r0, n = HALF[h]
        return pl.ds(r0, n)

    def gradients(r, h):
        p = e_s[r, half(h), :] * (factor[r] * inverse)
        d = p * (d_s[r, half(h), :] - row_dot)
        dk = dot(d.astype(BF), qs[...])
        dv = dot(p.astype(BF), gs[...])
        for k in range(4):
            columns = (dk, dv)[k // 2][:, (k % 2) * COLS : (k % 2 + 1) * COLS]
            dkv[r, k, half(h), :] = columns
            st[r, k, half(h), :] = columns.astype(BF)
        for k in (2, 1, 3):
            send(f"r{r}{k}{h}", st.at[r, at(m, k), half(h)], yb.at[r, 3 - k, half(h)], dev(km=k))

    def finish(r, h):
        piece = dkv[r, m, half(h), :]
        for k in (1, 3, 2):
            recv(f"r{r}{k}{h}", yb.at[r, 3 - k, half(h)])
            piece = piece + yb[r, 3 - k, half(h), :].astype(F32)
        return piece

    order = ((2, 0), (2, 1), (1, 1), (3, 0), (1, 0), (3, 1))
    for r, h in order:
        gradients(r, h)
    for i, (r, h) in enumerate(order[:4]):
        zst[r, half(h), :] = finish(r, h).astype(BF)
        target = (za0, za1, zb1, zb0)[i]
        send(f"z{i}", zst.at[r, half(h)], target, zm if i % 2 else zp)
        if i < 2:
            gradients(0, i)
    early = len(sent)
    for i, (r, h), arrived, target in ((4, order[4], za0, zc0), (5, order[5], za1, zc1)):
        piece = finish(r, h)
        recv(f"z{i - 4}", arrived)
        zst[r, half(h), :] = (piece + arrived[...].astype(F32)).astype(BF)
        send(f"z{i}", zst.at[r, half(h)], target, zm if i % 2 else zp)

    def wpart(part, k):
        return wg.at[at(m, k), pl.ds(pl.multiple_of(part * 1024, 1024), 1024)]

    for k in (2, 1, 3):
        send(f"w{k}", wpart(c, 0), wpart(c, 0), dev(km=k))

    for h in (0, 1):
        rr[half(h), :] = finish(0, h)
    for kx in (1, 3, 2):
        for kc in (0, 1):
            recv(f"hx{kx}{kc}", hx.at[slot(4 - kx, kc)])
    recv("hx01", hx.at[slot(0, 1)])
    hxt[...] = hx[...].T
    drain(early)

    def block(rx, rc):
        return gbuf.at[slot(rx, rc)]

    recv("z3", zb0)
    recv("z4", zc0)
    dres[half(0), :] = rr[half(0), :] + zb0[...].astype(F32) + zc0[...].astype(F32)
    recv("z2", zb1)
    recv("z5", zc1)
    dres[half(1), :] = rr[half(1), :] + zb1[...].astype(F32) + zc1[...].astype(F32)
    gbuf[slot(0, 0), :] = dres[...].astype(BF)
    for kx in (2, 1, 3):
        send(f"g{kx}", block(0, 0), block(4 - kx, 0), dev(kx=kx))
    send("gc0", block(0, 0), block(0, 1), other)

    for k in range(4):
        ds[k, 0:52, :] = dres[52 * k : 52 * k + 52, :].astype(BF)
        ds[k, 48:64, :] = jnp.where(
            lax.broadcasted_iota(jnp.int32, (16, COLS), 0) < 4, ds[k, 48:64, :].astype(F32), 0.0
        ).astype(BF)
    for k in (1, 3, 2):
        send(f"dy{k}", ds.at[at(m, k)], dr.at[m], dev(km=k))
    dr[m] = ds[m]

    for kx in (1, 3, 2):
        recv(f"g{kx}", block(4 - kx, 0))
        send(f"gc{kx}", block(4 - kx, 0), block(4 - kx, 1), other)
    for kx in (0, 1, 3, 2):
        recv(f"gc{kx}", block((4 - kx) % 4, 1))

    tf[...] = dot(hxt[...], gbuf[...])
    ts[...] = tf[...].astype(BF)

    def rows(start, n):
        return pl.ds(pl.multiple_of(start, n), n)

    def place(ks, kz):
        return (at(s, ks) * 4 + at(zl, kz)) * 16

    for i, (ks, kz) in enumerate(along_z):
        send(f"t{ks}{kz}", ts.at[rows(place(ks, kz), 16)], zr.at[i], dev(ks=ks, kz=kz))
    for k in (1, 3, 2):
        recv(f"w{k}", wpart(c, 4 - k))
        send(f"wc{k}", wpart(c, 4 - k), wpart(c, 4 - k), other)
    late = len(sent)
    base = (x * 2 + c) * 256
    piece = tf[rows(z * 16, 16), :]
    for i, (ks, kz) in reversed(list(enumerate(along_z))):
        recv(f"t{ks}{kz}", zr.at[i])
        piece = piece + zr[i].astype(F32)
    mine = upd.at[rows(base + z * 16, 16)]
    mine[...] = piece.astype(BF)
    for ks, kz in along_z:
        send(f"u{ks}{kz}", mine, mine, dev(ks=ks, kz=kz))
    drain(late)

    for k in (1, 3, 2):
        recv(f"wc{k}", wpart(1 - c, 4 - k))
    for k in (1, 3, 2):
        recv(f"dy{k}", dr.at[at(m, 4 - k)])
    for j in range(4):
        weight = wide(*[wg[k, 512 * j : 512 * j + 512, :] for k in range(4)])
        part = dot_nt(wide(dr[0], dr[1], dr[2], dr[3]), weight)
        o_grad[0, :, 512 * j : 512 * j + 512] = part[:52].astype(BF)

    def u64(kx, ks):
        return upd.at[rows(at(x, kx) * 512 + c * 256 + at(s, ks) * 64, 64)]

    def u256(kx, kc):
        return upd.at[rows(at(x, kx) * 512 + (1 - c if kc else c) * 256, 256)]

    for ks in (0, 1, 3, 2):
        for kz in (1, 2, 3, 0):
            if ks or kz:
                source = rows(base + place(4 - ks, 4 - kz), 16)
                recv(f"u{ks}{kz}", upd.at[source])
        for kx in (2, 1, 3):
            send(f"ux{kx}{ks}", u64(0, 4 - ks), u64(0, 4 - ks), dev(kx=kx))
    send("uc0", u256(0, 0), u256(0, 0), other)
    own = upd[rows(base, 256), :].astype(F32)
    sq[...] = jnp.sum((own * own).reshape(32, 8, COLS), axis=0)
    for k in (1, 3, 2):
        send(f"sy{k}", sq, ysq.at[3 - k], dev(km=k))

    for k in (1, 3, 2):
        recv(f"sy{k}", ysq.at[3 - k])
    xs[...] = sq[...] + ysq[0] + ysq[1] + ysq[2]
    across = [(kx, kc) for kx in (2, 1, 3, 0) for kc in (1, 0) if kx or kc]
    for i, (kx, kc) in enumerate(across):
        send(f"sx{kx}{kc}", xs, xsq.at[i], dev(kx=kx, kc=kc))
    for kx in (1, 3, 2):
        for ks in (0, 1, 3, 2):
            recv(f"ux{kx}{ks}", u64(4 - kx, 4 - ks))
        send(f"uc{kx}", u256(4 - kx, 0), u256(4 - kx, 0), other)
    everything = xs[...]
    for i, (kx, kc) in enumerate(across):
        recv(f"sx{kx}{kc}", xsq.at[i])
        everything = everything + xsq[i]
    o_sq[...] = everything
    drain(len(sent) - 3)
    recv("uc0", u256(0, 1))
    for kx in (1, 3, 2):
        recv(f"uc{kx}", u256(4 - kx, 1))
    o_upd[...] = upd[...]
    drain(len(sent))


def write_results(grad_ref, raw_ref, sq_ref, o_grad, o_upd):
    o_grad[...] = grad_ref[...]
    scale = lax.rsqrt(jnp.sum(sq_ref[...]) / (D * 2 * HD) + 1e-06)
    o_upd[...] = (raw_ref[...].astype(F32) * scale).astype(BF)


def per_device(
    prefix_hidden, prefix_kv_weight, action_hidden, query_weight, action_kv_weight,
    out_cotangent, prompt_len, view_valid,
):
    vm = pltpu.VMEM
    scratch = [
        vm((ROWS, D), BF), vm((4, D, COLS), BF), vm((ACT, 1024), BF), vm((1024, 512), BF),
        vm((1024, 512), BF), vm((ACT, 512), BF), vm((4, 4, ROWS, COLS), BF), vm((ACTP, 512), BF),
        vm((QR, HD), BF), vm((QR, HD), BF), vm((HD, QR), BF), vm((HD, QR), BF),
        vm((4, ROWS, QR), F32), vm((4, ROWS, QR), F32),
        vm((4, 4, ROWS, COLS), F32), vm((4, 4, ROWS, COLS), BF),
        vm((4, 3, ROWS, COLS), BF),
        vm((ROWS, COLS), F32), vm((4, ROWS, COLS), BF),
        vm((112, COLS), BF), vm((96, COLS), BF), vm((112, COLS), BF), vm((96, COLS), BF),
        vm((112, COLS), BF), vm((96, COLS), BF),
        vm((ROWS, COLS), F32), vm((8 * ROWS, COLS), BF), vm((8 * ROWS, 256), BF),
        vm((256, 8 * ROWS), BF), vm((256, COLS), F32), vm((256, COLS), BF),
        vm((15, 16, COLS), BF), vm((D, COLS), BF),
        vm((8, 128), F32), vm((3, 8, 128), F32), vm((8, 128), F32), vm((7, 8, 128), F32),
        vm((4, 64, COLS), BF), vm((4, 64, COLS), BF),
        pltpu.SMEM((1, VIEWS), jnp.int32),
        pltpu.SemaphoreType.DMA((8,)),
        pltpu.SemaphoreType.DMA((N_SEMS,)), pltpu.SemaphoreType.DMA((N_SEMS,)),
    ]
    smem = pl.BlockSpec(memory_space=pltpu.SMEM)
    hbm = pl.BlockSpec(memory_space=pltpu.HBM)
    grad, raw, squares = pl.pallas_call(
        kernel,
        out_shape=(
            jax.ShapeDtypeStruct((1, 52, D), BF),
            jax.ShapeDtypeStruct((D, COLS), BF),
            jax.ShapeDtypeStruct((8, 128), F32),
        ),
        in_specs=[smem] + [hbm] * 7,
        out_specs=(pl.BlockSpec(memory_space=pltpu.VMEM),) * 3,
        scratch_shapes=scratch,
        compiler_params=pltpu.CompilerParams(
            collective_id=0, has_side_effects=True, vmem_limit_bytes=40 * 1024 * 1024
        ),
    )(
        prompt_len, *[pltpu.with_memory_space_constraint(v, pltpu.HBM) for v in (view_valid, prefix_hidden, prefix_kv_weight, action_hidden, query_weight, action_kv_weight, out_cotangent)])
    return pl.pallas_call(
        write_results,
        out_shape=(
            jax.ShapeDtypeStruct((1, 52, D), BF),
            jax.ShapeDtypeStruct((D, COLS), BF),
        ),
        in_specs=[pl.BlockSpec(memory_space=pltpu.VMEM)] * 3,
        out_specs=(pl.BlockSpec(memory_space=pltpu.VMEM),) * 2,
        compiler_params=pltpu.CompilerParams(vmem_limit_bytes=40 * 1024 * 1024),
    )(grad, raw, squares)


def solution(mesh):
    return jax.shard_map(
        per_device,
        mesh=mesh,
        in_specs=(
            P("dp", "sample", None),
            P(None, "mp"),
            P("dp", "sample", None),
            P(None, "mp"),
            P(),
            P("dp", "sample", "mp"),
            P("dp"),
            P("dp", None),
        ),
        out_specs=(P("dp", ("sample", "mp"), None), P(None, "mp")),
        check_vma=False,
    )
```

```python
import jax
import jax.numpy as jnp
from jax import lax
from jax.experimental import pallas as pl
from jax.experimental.pallas import tpu as pltpu
from jax.sharding import PartitionSpec as P

BF = jnp.bfloat16
F32 = jnp.float32
D = 2048
HD = 256
ROWS = 208
COLS = 128
ACT = 300
ACTP = 304
QR = 2 * ACTP
VIEW_TOK = 256
VIEWS = 3
HORIZON = 50
NEG = -3.0e38
HALF = ((0, 112), (112, 96))
PART = ((0, 64), (64, 48), (112, 48), (160, 48))
N_SEMS = 200


def dot(a, b):
    return jnp.dot(a, b, preferred_element_type=F32)


def wide(*pieces):
    return jnp.concatenate(pieces, axis=1)


def dot_nt(a, b):
    return lax.dot_general(a, b, (((1,), (1,)), ((), ())), preferred_element_type=F32)


def kernel(
    len_ref, view_h, hid_h, w_h, act_h, wq_h, wakv_h, cot_h,
    o_grad, o_upd, o_sq,
    hid_v, wg, act_v, wq_v, wakv_v, cot_v, kv, akv, qs, gs, qt, gt, e_s, d_s,
    dkv, st, yb,
    rr, zst, za0, za1, zb0, zb1, zc0, zc1,
    dres, gbuf, hx, hxa, hxb, tf, ts, zr, upd,
    sq, ysq, xs, xsq, ds, dr,
    view_ref, lsem, ssem, rsem,
):
    dp = lax.axis_index("dp")
    s = lax.axis_index("sample")
    m = lax.axis_index("mp")
    x = dp // 8
    zl = lax.rem(dp, 8) // 2
    c = lax.rem(dp, 2)

    def at(a, k):
        return lax.rem(a + k, 4)

    z = s * 4 + zl

    def dev(kx=0, kz=0, ks=0, km=0, kc=0):
        cc = 1 - c if kc else c
        d = at(x, kx) * 8 + at(zl, kz) * 2 + cc
        return {"dp": d, "sample": at(s, ks), "mp": at(m, km)}

    along_z = [(ks, kz) for ks in (2, 1, 3, 0) for kz in (1, 2, 3, 0) if ks or kz]
    zp, zm = dev(ks=1), dev(ks=3)
    other = dev(kc=1)

    index = {}
    sent = []

    def number(name):
        return index.setdefault(name, len(index))

    def send(name, src, dst, device):
        i = number(name)
        copy = pltpu.make_async_remote_copy(
            src_ref=src, dst_ref=dst, send_sem=ssem.at[i], recv_sem=rsem.at[i],
            device_id=device, device_id_type=pl.DeviceIdType.MESH,
        )
        copy.start()
        sent.append(copy)

    def recv(name, dst, device=None):
        i = number(name)
        pltpu.make_async_remote_copy(
            src_ref=dst, dst_ref=dst, send_sem=ssem.at[i], recv_sem=rsem.at[i],
            device_id=other if device is None else device,
            device_id_type=pl.DeviceIdType.MESH,
        ).wait_recv()

    def drain(n):
        for copy in sent[:n]:
            copy.wait_send()
        del sent[:n]

    loads = [
        pltpu.make_async_copy(hid_h.at[0, 0:112], hid_v.at[0:112], lsem.at[0]),
        pltpu.make_async_copy(w_h, wg.at[m], lsem.at[1]),
        pltpu.make_async_copy(act_h.at[0], act_v, lsem.at[2]),
        pltpu.make_async_copy(wq_h, wq_v, lsem.at[3]),
        pltpu.make_async_copy(wakv_h, wakv_v, lsem.at[4]),
        pltpu.make_async_copy(cot_h.at[0], cot_v, lsem.at[5]),
        pltpu.make_async_copy(hid_h.at[0, 112:208], hid_v.at[112:208], lsem.at[6]),
    ]
    loads.append(pltpu.make_async_copy(view_h, view_ref, lsem.at[7]))
    for i in (1, 0, 6, 7):
        loads[i].start()

    barrier = pltpu.get_barrier_semaphore()
    peers = [dev(km=k) for k in (1, 2, 3)] + [dev(ks=ks, kz=kz) for ks, kz in along_z] + [other]
    peers += [dev(kx=k, kc=kc) for k in (1, 2, 3) for kc in (0, 1)]
    for peer in peers:
        pl.semaphore_signal(
            barrier, inc=1, device_id=peer, device_id_type=pl.DeviceIdType.MESH
        )

    def kvp(r, i):
        r0, n = PART[i]
        return kv.at[r, m, pl.ds(r0, n)]

    def ysend(r, h):
        r0, n = HALF[h]
        block = kv.at[r, m, pl.ds(r0, n)]
        for k in (2, 1, 3):
            send(f"y{r}{k}{h}", block, block, dev(km=k))

    def ywait(r):
        for h in (0, 1):
            r0, n = HALF[h]
            for k in (1, 3, 2):
                recv(f"y{r}{k}{h}", kv.at[r, at(m, 4 - k), pl.ds(r0, n)])

    loads[1].wait()
    loads[0].wait()
    for i in (2, 3, 5, 4):
        loads[i].start()
    kv[0, m, 0:112, :] = dot(hid_v[0:112], wg[m]).astype(BF)
    pl.semaphore_wait(barrier, len(peers))
    for i in (0, 1):
        send(f"zp{i}", kvp(0, i), kvp(3, i), zp)
    loads[6].wait()
    kv[0, m, 112:208, :] = dot(hid_v[112:208], wg[m]).astype(BF)
    for i in (2, 3):
        send(f"zm{i}", kvp(0, i), kvp(1, i), zm)
    for i, j in ((2, 0), (3, 1)):
        send(f"zp{i}", kvp(0, i), kvp(3, i), zp)
        send(f"zm{j}", kvp(0, j), kvp(1, j), zm)
    ysend(0, 0)
    ysend(0, 1)

    def slot(rx, rc):
        return pl.ds((rc * 4 + rx) * ROWS, ROWS)

    def hidden_columns(kx, kc):
        j = at(x, kx) * 2 + (1 - c if kc else c)
        return pl.ds(pl.multiple_of(j * 256, 256), 256)

    def send_hidden(kx):
        for kc in (0, 1):
            send(f"hx{kx}{kc}", hid_v.at[:, hidden_columns(kx, kc)],
                 hx.at[slot(4 - kx, kc)], dev(kx=kx, kc=kc))

    send_hidden(1)
    send_hidden(3)
    send("hx01", hid_v.at[:, hidden_columns(0, 1)], hx.at[slot(0, 1)], other)
    hx[slot(0, 0), :] = hid_v[:, hidden_columns(0, 0)]

    for ref in (qs, gs):
        ref[288:304, :] = jnp.zeros((16, HD), BF)
        ref[592:608, :] = jnp.zeros((16, HD), BF)
    akv[288:304, :] = jnp.zeros((16, 2 * HD), BF)
    loads[2].wait()
    loads[3].wait()
    queries = (dot(act_v[...], wq_v[...]).astype(BF).astype(F32) * (HD**-0.5)).astype(BF)
    qs[0:ACT, :] = queries[:, :HD]
    qs[ACTP : ACTP + ACT, :] = queries[:, HD:]
    loads[4].wait()
    akv[0:ACT, :] = dot(act_v[...], wakv_v[...]).astype(BF)
    loads[5].wait()
    gs[0:ACT, :] = cot_v[:, :HD]
    gs[ACTP : ACTP + ACT, :] = cot_v[:, HD:]

    qt[...] = qs[...].T
    gt[...] = gs[...].T

    block_max, block_sum, block_dot = {}, {}, {}

    def attend(r, keys, values, mask, e_ref, d_ref):
        scores = mask(dot(keys, qt[...]))
        top = jnp.max(scores, axis=0, keepdims=True)
        e = jnp.exp(scores - top)
        d = dot(values, gt[...])
        if e_ref is not None:
            e_ref[...] = e
            d_ref[...] = d
        block_max[r] = top
        block_sum[r] = jnp.sum(e, axis=0, keepdims=True)
        block_dot[r] = jnp.sum(e * d, axis=0, keepdims=True)

    def draw(i):
        total = jnp.zeros_like(i)
        for t in range(1, ACTP // HORIZON + 1):
            total = total + jnp.where(i >= t * HORIZON, 1, 0)
        return total

    for i, j in ((0, 2), (1, 3)):
        recv(f"zp{i}", kvp(3, i))
        send(f"zf{i}", kvp(3, i), kvp(2, i), zp)
        recv(f"zm{j}", kvp(1, j))
        send(f"zf{j}", kvp(1, j), kvp(2, j), zm)
    ysend(3, 0)
    ysend(1, 1)

    key_draw = draw(lax.broadcasted_iota(jnp.int32, (ACTP, 1), 0))
    query_index = lax.broadcasted_iota(jnp.int32, (1, QR), 1)
    query_draw = draw(query_index - jnp.where(query_index >= ACTP, ACTP, 0))
    attend(
        "a", akv[:, :HD], akv[:, HD:],
        lambda scores: jnp.where(key_draw == query_draw, scores, NEG), None, None,
    )

    loads[7].wait()

    def attend_prefix(r):
        p = at(s, r) * ROWS + lax.broadcasted_iota(jnp.int32, (ROWS, 1), 0)
        usable = jnp.where(p >= VIEWS * VIEW_TOK, jnp.where(p - VIEWS * VIEW_TOK < len_ref[0], 1, 0), 0)
        for v in range(VIEWS):
            inside = jnp.where(p >= v * VIEW_TOK, 1, 0) * jnp.where(p < (v + 1) * VIEW_TOK, 1, 0)
            usable = usable + inside * jnp.where(view_ref[0, v] == 1, 1, 0)
        ceiling = jnp.where(usable > 0, -NEG, NEG)
        attend(
            r, wide(kv[r, 0], kv[r, 1]), wide(kv[r, 2], kv[r, 3]),
            lambda scores: jnp.minimum(scores, ceiling), e_s.at[r], d_s.at[r],
        )

    for i in (2, 3):
        recv(f"zp{i}", kvp(3, i))
    ysend(3, 1)
    for i in (0, 1):
        recv(f"zm{i}", kvp(1, i))
    ysend(1, 0)
    ywait(0)
    attend_prefix(0)
    for i in (0, 1):
        recv(f"zf{i}", kvp(2, i))
    ysend(2, 0)
    for i in (2, 3):
        recv(f"zf{i}", kvp(2, i))
    ysend(2, 1)
    send_hidden(2)
    ywait(3)
    attend_prefix(3)
    ywait(1)
    attend_prefix(1)
    ywait(2)
    attend_prefix(2)

    blocks = ("a", 0, 1, 2, 3)
    top = block_max["a"]
    for r in (0, 1, 2, 3):
        top = jnp.maximum(top, block_max[r])
    factor = {r: jnp.exp(block_max[r] - top) for r in blocks}
    total = sum(factor[r] * block_sum[r] for r in blocks)
    inverse = 1.0 / total
    row_dot = sum(factor[r] * block_dot[r] for r in blocks) * inverse

    def half(h):
        r0, n = HALF[h]
        return pl.ds(r0, n)

    def gradients(r, h):
        p = e_s[r, half(h), :] * (factor[r] * inverse)
        d = p * (d_s[r, half(h), :] - row_dot)
        dk = dot(d.astype(BF), qs[...])
        dv = dot(p.astype(BF), gs[...])
        for k in range(4):
            columns = (dk, dv)[k // 2][:, (k % 2) * COLS : (k % 2 + 1) * COLS]
            dkv[r, k, half(h), :] = columns
            st[r, k, half(h), :] = columns.astype(BF)
        for k in (2, 1, 3):
            send(f"r{r}{k}{h}", st.at[r, at(m, k), half(h)], yb.at[r, 3 - k, half(h)], dev(km=k))

    def finish(r, h):
        piece = dkv[r, m, half(h), :]
        for k in (1, 3, 2):
            recv(f"r{r}{k}{h}", yb.at[r, 3 - k, half(h)])
            piece = piece + yb[r, 3 - k, half(h), :].astype(F32)
        return piece

    order = ((2, 0), (2, 1), (1, 1), (3, 0), (1, 0), (3, 1))
    for r, h in order:
        gradients(r, h)
    for i, (r, h) in enumerate(order[:4]):
        zst[r, half(h), :] = finish(r, h).astype(BF)
        target = (za0, za1, zb1, zb0)[i]
        send(f"z{i}", zst.at[r, half(h)], target, zm if i % 2 else zp)
        if i < 2:
            gradients(0, i)
    early = len(sent)
    for i, (r, h), arrived, target in ((4, order[4], za0, zc0), (5, order[5], za1, zc1)):
        piece = finish(r, h)
        recv(f"z{i - 4}", arrived)
        zst[r, half(h), :] = (piece + arrived[...].astype(F32)).astype(BF)
        send(f"z{i}", zst.at[r, half(h)], target, zm if i % 2 else zp)

    def wpart(part, k):
        return wg.at[at(m, k), pl.ds(pl.multiple_of(part * 1024, 1024), 1024)]

    for k in (2, 1, 3):
        send(f"w{k}", wpart(c, 0), wpart(c, 0), dev(km=k))

    for h in (0, 1):
        rr[half(h), :] = finish(0, h)
    for kx in (1, 3, 2):
        for kc in (0, 1):
            recv(f"hx{kx}{kc}", hx.at[slot(4 - kx, kc)])
    recv("hx01", hx.at[slot(0, 1)])
    hxa[...] = hx[0 : 4 * ROWS, :].T
    hxb[...] = hx[4 * ROWS : 8 * ROWS, :].T
    drain(early)

    def block(rx, rc):
        return gbuf.at[slot(rx, rc)]

    recv("z3", zb0)
    recv("z4", zc0)
    dres[half(0), :] = rr[half(0), :] + zb0[...].astype(F32) + zc0[...].astype(F32)
    recv("z2", zb1)
    recv("z5", zc1)
    dres[half(1), :] = rr[half(1), :] + zb1[...].astype(F32) + zc1[...].astype(F32)
    gbuf[slot(0, 0), :] = dres[...].astype(BF)
    for kx in (2, 1, 3):
        send(f"g{kx}", block(0, 0), block(4 - kx, 0), dev(kx=kx))
    send("gc0", block(0, 0), block(0, 1), other)

    for k in range(4):
        ds[k, 0:52, :] = dres[52 * k : 52 * k + 52, :].astype(BF)
        ds[k, 48:64, :] = jnp.where(
            lax.broadcasted_iota(jnp.int32, (16, COLS), 0) < 4, ds[k, 48:64, :].astype(F32), 0.0
        ).astype(BF)
    for k in (1, 3, 2):
        send(f"dy{k}", ds.at[at(m, k)], dr.at[m], dev(km=k))
    dr[m] = ds[m]

    for kx in (1, 3, 2):
        recv(f"g{kx}", block(4 - kx, 0))
        send(f"gc{kx}", block(4 - kx, 0), block(4 - kx, 1), other)
    tf[...] = dot(hxa[...], gbuf[0 : 4 * ROWS, :])
    for kx in (0, 1, 3, 2):
        recv(f"gc{kx}", block((4 - kx) % 4, 1))

    part = tf[...] + dot(hxb[...], gbuf[4 * ROWS : 8 * ROWS, :])
    tf[...] = part
    ts[...] = part.astype(BF)

    def rows(start, n):
        return pl.ds(pl.multiple_of(start, n), n)

    def place(ks, kz):
        return (at(s, ks) * 4 + at(zl, kz)) * 16

    for i, (ks, kz) in enumerate(along_z):
        send(f"t{ks}{kz}", ts.at[rows(place(ks, kz), 16)], zr.at[i], dev(ks=ks, kz=kz))
    for k in (1, 3, 2):
        recv(f"w{k}", wpart(c, 4 - k))
        send(f"wc{k}", wpart(c, 4 - k), wpart(c, 4 - k), other)
    late = len(sent)
    base = (x * 2 + c) * 256
    piece = tf[rows(z * 16, 16), :]
    for i, (ks, kz) in reversed(list(enumerate(along_z))):
        recv(f"t{ks}{kz}", zr.at[i])
        piece = piece + zr[i].astype(F32)
    mine = upd.at[rows(base + z * 16, 16)]
    mine[...] = piece.astype(BF)
    for ks, kz in along_z:
        send(f"u{ks}{kz}", mine, mine, dev(ks=ks, kz=kz))
    drain(late)

    for k in (1, 3, 2):
        recv(f"wc{k}", wpart(1 - c, 4 - k))
    for k in (1, 3, 2):
        recv(f"dy{k}", dr.at[at(m, 4 - k)])
    for j in range(4):
        weight = wide(*[wg[k, 512 * j : 512 * j + 512, :] for k in range(4)])
        part = dot_nt(wide(dr[0], dr[1], dr[2], dr[3]), weight)
        o_grad[0, :, 512 * j : 512 * j + 512] = part[:52].astype(BF)

    across = [(kx, kc) for kx in (2, 1, 3, 0) for kc in (1, 0) if kx or kc]

    def u64(kx, ks, kc=0):
        start = at(x, kx) * 512 + (1 - c if kc else c) * 256 + at(s, ks) * 64
        return upd.at[rows(start, 64)]

    for ks in (0, 1, 3, 2):
        for kz in (1, 2, 3, 0):
            if ks or kz:
                source = rows(base + place(4 - ks, 4 - kz), 16)
                recv(f"u{ks}{kz}", upd.at[source])
        for kx, kc in across:
            send(f"ux{kx}{kc}{ks}", u64(0, 4 - ks), u64(0, 4 - ks), dev(kx=kx, kc=kc))
    own = upd[rows(base, 256), :].astype(F32)
    sq[...] = jnp.sum((own * own).reshape(32, 8, COLS), axis=0)
    for k in (1, 3, 2):
        send(f"sy{k}", sq, ysq.at[3 - k], dev(km=k))

    for k in (1, 3, 2):
        recv(f"sy{k}", ysq.at[3 - k])
    xs[...] = sq[...] + ysq[0] + ysq[1] + ysq[2]
    for i, (kx, kc) in enumerate(across):
        send(f"sx{kx}{kc}", xs, xsq.at[i], dev(kx=kx, kc=kc))
    everything = xs[...]
    for i, (kx, kc) in enumerate(across):
        recv(f"sx{kx}{kc}", xsq.at[i])
        everything = everything + xsq[i]
    o_sq[...] = everything
    for ks in (0, 1, 3, 2):
        for kx, kc in across:
            recv(f"ux{kx}{kc}{ks}", u64(4 - kx, 4 - ks, kc))
    o_upd[...] = upd[...]
    drain(len(sent))


def write_results(grad_ref, raw_ref, sq_ref, o_grad, o_upd):
    o_grad[...] = grad_ref[...]
    scale = lax.rsqrt(jnp.sum(sq_ref[...]) / (D * 2 * HD) + 1e-06)
    o_upd[...] = (raw_ref[...].astype(F32) * scale).astype(BF)


def per_device(
    prefix_hidden, prefix_kv_weight, action_hidden, query_weight, action_kv_weight,
    out_cotangent, prompt_len, view_valid,
):
    vm = pltpu.VMEM
    scratch = [
        vm((ROWS, D), BF), vm((4, D, COLS), BF), vm((ACT, 1024), BF), vm((1024, 512), BF),
        vm((1024, 512), BF), vm((ACT, 512), BF), vm((4, 4, ROWS, COLS), BF), vm((ACTP, 512), BF),
        vm((QR, HD), BF), vm((QR, HD), BF), vm((HD, QR), BF), vm((HD, QR), BF),
        vm((4, ROWS, QR), F32), vm((4, ROWS, QR), F32),
        vm((4, 4, ROWS, COLS), F32), vm((4, 4, ROWS, COLS), BF),
        vm((4, 3, ROWS, COLS), BF),
        vm((ROWS, COLS), F32), vm((4, ROWS, COLS), BF),
        vm((112, COLS), BF), vm((96, COLS), BF), vm((112, COLS), BF), vm((96, COLS), BF),
        vm((112, COLS), BF), vm((96, COLS), BF),
        vm((ROWS, COLS), F32), vm((8 * ROWS, COLS), BF), vm((8 * ROWS, 256), BF),
        vm((256, 4 * ROWS), BF), vm((256, 4 * ROWS), BF), vm((256, COLS), F32), vm((256, COLS), BF),
        vm((15, 16, COLS), BF), vm((D, COLS), BF),
        vm((8, 128), F32), vm((3, 8, 128), F32), vm((8, 128), F32), vm((7, 8, 128), F32),
        vm((4, 64, COLS), BF), vm((4, 64, COLS), BF),
        pltpu.SMEM((1, VIEWS), jnp.int32),
        pltpu.SemaphoreType.DMA((8,)),
        pltpu.SemaphoreType.DMA((N_SEMS,)), pltpu.SemaphoreType.DMA((N_SEMS,)),
    ]
    smem = pl.BlockSpec(memory_space=pltpu.SMEM)
    hbm = pl.BlockSpec(memory_space=pltpu.HBM)
    grad, raw, squares = pl.pallas_call(
        kernel,
        out_shape=(
            jax.ShapeDtypeStruct((1, 52, D), BF),
            jax.ShapeDtypeStruct((D, COLS), BF),
            jax.ShapeDtypeStruct((8, 128), F32),
        ),
        in_specs=[smem] + [hbm] * 7,
        out_specs=(pl.BlockSpec(memory_space=pltpu.VMEM),) * 3,
        scratch_shapes=scratch,
        compiler_params=pltpu.CompilerParams(
            collective_id=0, has_side_effects=True, vmem_limit_bytes=40 * 1024 * 1024
        ),
    )(
        prompt_len, *[pltpu.with_memory_space_constraint(v, pltpu.HBM) for v in (view_valid, prefix_hidden, prefix_kv_weight, action_hidden, query_weight, action_kv_weight, out_cotangent)])
    return pl.pallas_call(
        write_results,
        out_shape=(
            jax.ShapeDtypeStruct((1, 52, D), BF),
            jax.ShapeDtypeStruct((D, COLS), BF),
        ),
        in_specs=[pl.BlockSpec(memory_space=pltpu.VMEM)] * 3,
        out_specs=(pl.BlockSpec(memory_space=pltpu.VMEM),) * 2,
        compiler_params=pltpu.CompilerParams(vmem_limit_bytes=40 * 1024 * 1024),
    )(grad, raw, squares)


def solution(mesh):
    return jax.shard_map(
        per_device,
        mesh=mesh,
        in_specs=(
            P("dp", "sample", None),
            P(None, "mp"),
            P("dp", "sample", None),
            P(None, "mp"),
            P(),
            P("dp", "sample", "mp"),
            P("dp"),
            P("dp", None),
        ),
        out_specs=(P("dp", ("sample", "mp"), None), P(None, "mp")),
        check_vma=False,
    )
```

```python
import jax
import jax.numpy as jnp
from jax import lax
from jax.experimental import pallas as pl
from jax.experimental.pallas import tpu as pltpu
from jax.sharding import PartitionSpec as P

BF = jnp.bfloat16
F32 = jnp.float32
D = 2048
HD = 256
ROWS = 208
COLS = 128
ACT = 300
ACTP = 304
QR = 2 * ACTP
VIEW_TOK = 256
VIEWS = 3
HORIZON = 50
NEG = -3.0e38
HALF = ((0, 112), (112, 96))
PART = ((0, 64), (64, 48), (112, 48), (160, 48))
N_SEMS = 160


def dot(a, b):
    return jnp.dot(a, b, preferred_element_type=F32)


def wide(*pieces):
    return jnp.concatenate(pieces, axis=1)


def dot_nt(a, b):
    return lax.dot_general(a, b, (((1,), (1,)), ((), ())), preferred_element_type=F32)


def kernel(
    len_ref, view_h, hid_h, w_h, act_h, wq_h, wakv_h, cot_h,
    o_grad, o_upd, o_sq,
    hid_v, wg, act_v, wq_v, wakv_v, cot_v, kv, akv, qs, gs, qt, gt, e_s, d_s,
    dkv, st, yb,
    rr, zst, za0, za1, zb0, zb1, zc0, zc1,
    dres, gbuf, hx, hxa, hxb, tf, ts, zr, upd,
    sq, ysq, xs, xsq, ds, dr,
    view_ref, lsem, ssem, rsem,
):
    dp = lax.axis_index("dp")
    s = lax.axis_index("sample")
    m = lax.axis_index("mp")
    x = dp // 8
    zl = lax.rem(dp, 8) // 2
    c = lax.rem(dp, 2)

    def at(a, k):
        return lax.rem(a + k, 4)

    z = s * 4 + zl

    def dev(kx=0, kz=0, ks=0, km=0, kc=0):
        cc = 1 - c if kc else c
        d = at(x, kx) * 8 + at(zl, kz) * 2 + cc
        return {"dp": d, "sample": at(s, ks), "mp": at(m, km)}

    along_z = [(ks, kz) for ks in (2, 1, 3, 0) for kz in (1, 2, 3, 0) if ks or kz]
    zp, zm = dev(ks=1), dev(ks=3)
    other = dev(kc=1)

    index = {}
    sent = []

    def number(name):
        return index.setdefault(name, len(index))

    def send(name, src, dst, device):
        i = number(name)
        copy = pltpu.make_async_remote_copy(
            src_ref=src, dst_ref=dst, send_sem=ssem.at[i], recv_sem=rsem.at[i],
            device_id=device, device_id_type=pl.DeviceIdType.MESH,
        )
        copy.start()
        sent.append(copy)

    def recv(name, dst, device=None):
        i = number(name)
        pltpu.make_async_remote_copy(
            src_ref=dst, dst_ref=dst, send_sem=ssem.at[i], recv_sem=rsem.at[i],
            device_id=other if device is None else device,
            device_id_type=pl.DeviceIdType.MESH,
        ).wait_recv()

    def drain(n):
        for copy in sent[:n]:
            copy.wait_send()
        del sent[:n]

    loads = [
        pltpu.make_async_copy(hid_h.at[0, 0:112], hid_v.at[0:112], lsem.at[0]),
        pltpu.make_async_copy(w_h, wg.at[m], lsem.at[1]),
        pltpu.make_async_copy(act_h.at[0], act_v, lsem.at[2]),
        pltpu.make_async_copy(wq_h, wq_v, lsem.at[3]),
        pltpu.make_async_copy(wakv_h, wakv_v, lsem.at[4]),
        pltpu.make_async_copy(cot_h.at[0], cot_v, lsem.at[5]),
        pltpu.make_async_copy(hid_h.at[0, 112:208], hid_v.at[112:208], lsem.at[6]),
    ]
    loads.append(pltpu.make_async_copy(view_h, view_ref, lsem.at[7]))
    for i in (1, 0, 6, 7):
        loads[i].start()

    barrier = pltpu.get_barrier_semaphore()
    peers = [dev(km=k) for k in (1, 2, 3)] + [dev(ks=ks, kz=kz) for ks, kz in along_z] + [other]
    peers += [dev(kx=k, kc=kc) for k in (1, 2, 3) for kc in (0, 1)]
    for peer in peers:
        pl.semaphore_signal(
            barrier, inc=1, device_id=peer, device_id_type=pl.DeviceIdType.MESH
        )

    def kvp(r, i):
        r0, n = PART[i]
        return kv.at[r, m, pl.ds(r0, n)]

    def ysend(r, h):
        r0, n = HALF[h]
        block = kv.at[r, m, pl.ds(r0, n)]
        for k in (2, 1, 3):
            send(f"y{r}{k}{h}", block, block, dev(km=k))

    def ywait(r, halves=(0, 1)):
        for h in halves:
            r0, n = HALF[h]
            for k in (1, 3, 2):
                recv(f"y{r}{k}{h}", kv.at[r, at(m, 4 - k), pl.ds(r0, n)])

    loads[1].wait()
    loads[0].wait()
    for i in (2, 3, 5, 4):
        loads[i].start()
    kv[0, m, 0:112, :] = dot(hid_v[0:112], wg[m]).astype(BF)
    pl.semaphore_wait(barrier, len(peers))
    for i in (0, 1):
        send(f"zp{i}", kvp(0, i), kvp(3, i), zp)
    loads[6].wait()
    kv[0, m, 112:208, :] = dot(hid_v[112:208], wg[m]).astype(BF)
    for i in (2, 3):
        send(f"zm{i}", kvp(0, i), kvp(1, i), zm)
    for i, j in ((2, 0), (3, 1)):
        send(f"zp{i}", kvp(0, i), kvp(3, i), zp)
        send(f"zm{j}", kvp(0, j), kvp(1, j), zm)
    ysend(0, 0)
    ysend(0, 1)

    def slot(rx, rc):
        return pl.ds((rc * 4 + rx) * ROWS, ROWS)

    def hidden_columns(kx, kc):
        j = at(x, kx) * 2 + (1 - c if kc else c)
        return pl.ds(pl.multiple_of(j * 256, 256), 256)

    def send_hidden(kx):
        for kc in (0, 1):
            send(f"hx{kx}{kc}", hid_v.at[:, hidden_columns(kx, kc)],
                 hx.at[slot(4 - kx, kc)], dev(kx=kx, kc=kc))

    first = len(sent)
    send_hidden(1)
    send_hidden(3)
    send("hx01", hid_v.at[:, hidden_columns(0, 1)], hx.at[slot(0, 1)], other)
    hx[slot(0, 0), :] = hid_v[:, hidden_columns(0, 0)]

    for ref in (qs, gs):
        ref[288:304, :] = jnp.zeros((16, HD), BF)
        ref[592:608, :] = jnp.zeros((16, HD), BF)
    akv[288:304, :] = jnp.zeros((16, 2 * HD), BF)
    loads[2].wait()
    loads[3].wait()
    queries = (dot(act_v[...], wq_v[...]).astype(BF).astype(F32) * (HD**-0.5)).astype(BF)
    qs[0:ACT, :] = queries[:, :HD]
    qs[ACTP : ACTP + ACT, :] = queries[:, HD:]
    loads[4].wait()
    akv[0:ACT, :] = dot(act_v[...], wakv_v[...]).astype(BF)
    loads[5].wait()
    gs[0:ACT, :] = cot_v[:, :HD]
    gs[ACTP : ACTP + ACT, :] = cot_v[:, HD:]

    qt[...] = qs[...].T
    gt[...] = gs[...].T

    def half(h):
        r0, n = HALF[h]
        return pl.ds(r0, n)

    block_max, block_sum, block_dot = {}, {}, {}

    def attend(r, keys, values, mask, e_ref, d_ref):
        scores = mask(dot(keys, qt[...]))
        top = jnp.max(scores, axis=0, keepdims=True)
        e = jnp.exp(scores - top)
        d = dot(values, gt[...])
        if e_ref is not None:
            e_ref[...] = e
            d_ref[...] = d
        block_max[r] = top
        block_sum[r] = jnp.sum(e, axis=0, keepdims=True)
        block_dot[r] = jnp.sum(e * d, axis=0, keepdims=True)

    def draw(i):
        total = jnp.zeros_like(i)
        for t in range(1, ACTP // HORIZON + 1):
            total = total + jnp.where(i >= t * HORIZON, 1, 0)
        return total

    for i, j in ((0, 2), (1, 3)):
        recv(f"zp{i}", kvp(3, i))
        send(f"zf{i}", kvp(3, i), kvp(2, i), zp)
        recv(f"zm{j}", kvp(1, j))
        send(f"zf{j}", kvp(1, j), kvp(2, j), zm)
    ysend(3, 0)
    ysend(1, 1)

    key_draw = draw(lax.broadcasted_iota(jnp.int32, (ACTP, 1), 0))
    query_index = lax.broadcasted_iota(jnp.int32, (1, QR), 1)
    query_draw = draw(query_index - jnp.where(query_index >= ACTP, ACTP, 0))
    attend(
        "a", akv[:, :HD], akv[:, HD:],
        lambda scores: jnp.where(key_draw == query_draw, scores, NEG), None, None,
    )

    loads[7].wait()

    def attend_prefix(r, part=None):
        r0, n = (0, ROWS) if part is None else HALF[part]
        p = at(s, r) * ROWS + r0 + lax.broadcasted_iota(jnp.int32, (n, 1), 0)
        usable = jnp.where(p >= VIEWS * VIEW_TOK, jnp.where(p - VIEWS * VIEW_TOK < len_ref[0], 1, 0), 0)
        for v in range(VIEWS):
            inside = jnp.where(p >= v * VIEW_TOK, 1, 0) * jnp.where(p < (v + 1) * VIEW_TOK, 1, 0)
            usable = usable + inside * jnp.where(view_ref[0, v] == 1, 1, 0)
        ceiling = jnp.where(usable > 0, -NEG, NEG)
        some = pl.ds(r0, n)
        attend(
            r if part is None else (r, part),
            wide(kv[r, 0, some, :], kv[r, 1, some, :]), wide(kv[r, 2, some, :], kv[r, 3, some, :]),
            lambda scores: jnp.minimum(scores, ceiling), e_s.at[r, some], d_s.at[r, some],
        )

    for i in (2, 3):
        recv(f"zp{i}", kvp(3, i))
    ysend(3, 1)
    for i in (0, 1):
        recv(f"zm{i}", kvp(1, i))
    ysend(1, 0)
    ywait(0)
    attend_prefix(0)
    for i in (0, 1):
        recv(f"zf{i}", kvp(2, i))
    ysend(2, 0)
    for i in (2, 3):
        recv(f"zf{i}", kvp(2, i))
    ysend(2, 1)
    send_hidden(2)
    ywait(3)
    attend_prefix(3)
    ywait(1)
    attend_prefix(1)
    drain(first)

    def merge(parts):
        top = block_max[parts[0]]
        for i in parts[1:]:
            top = jnp.maximum(top, block_max[i])
        scaled = [jnp.exp(block_max[i] - top) for i in parts]
        total = sum(f * block_sum[i] for f, i in zip(scaled, parts))
        return top, total, sum(f * block_dot[i] for f, i in zip(scaled, parts))

    block_max["m"], block_sum["m"], block_dot["m"] = merge(("a", 0, 1, 3))
    for h in (0, 1):
        ywait(2, (h,))
        attend_prefix(2, h)
    top, total, row_dot = merge(("m", (2, 0), (2, 1)))
    inverse = 1.0 / total
    row_dot = row_dot * inverse

    def gradients(r, h):
        largest = block_max[(2, h) if r == 2 else r]
        p = e_s[r, half(h), :] * (jnp.exp(largest - top) * inverse)
        d = p * (d_s[r, half(h), :] - row_dot)
        dk = dot(d.astype(BF), qs[...])
        dv = dot(p.astype(BF), gs[...])
        for k in range(4):
            columns = (dk, dv)[k // 2][:, (k % 2) * COLS : (k % 2 + 1) * COLS]
            dkv[r, k, half(h), :] = columns
            st[r, k, half(h), :] = columns.astype(BF)
        for k in (2, 1, 3):
            send(f"r{r}{k}{h}", st.at[r, at(m, k), half(h)], yb.at[r, 3 - k, half(h)], dev(km=k))

    def finish(r, h):
        piece = dkv[r, m, half(h), :]
        for k in (1, 3, 2):
            recv(f"r{r}{k}{h}", yb.at[r, 3 - k, half(h)])
            piece = piece + yb[r, 3 - k, half(h), :].astype(F32)
        return piece

    order = ((2, 0), (2, 1), (1, 1), (3, 0), (1, 0), (3, 1))
    for r, h in order:
        gradients(r, h)
    for i, (r, h) in enumerate(order[:4]):
        zst[r, half(h), :] = finish(r, h).astype(BF)
        target = (za0, za1, zb1, zb0)[i]
        send(f"z{i}", zst.at[r, half(h)], target, zm if i % 2 else zp)
        if i < 2:
            gradients(0, i)
    for i, (r, h), arrived, target in ((4, order[4], za0, zc0), (5, order[5], za1, zc1)):
        piece = finish(r, h)
        recv(f"z{i - 4}", arrived)
        zst[r, half(h), :] = (piece + arrived[...].astype(F32)).astype(BF)
        send(f"z{i}", zst.at[r, half(h)], target, zm if i % 2 else zp)

    def wpart(part, k):
        return wg.at[at(m, k), pl.ds(pl.multiple_of(part * 1024, 1024), 1024)]

    for k in (2, 1, 3):
        send(f"w{k}", wpart(c, 0), wpart(c, 0), dev(km=k))

    for h in (0, 1):
        rr[half(h), :] = finish(0, h)
    for kx in (1, 3, 2):
        for kc in (0, 1):
            recv(f"hx{kx}{kc}", hx.at[slot(4 - kx, kc)])
    recv("hx01", hx.at[slot(0, 1)])
    hxa[...] = hx[0 : 4 * ROWS, :].T
    hxb[...] = hx[4 * ROWS : 8 * ROWS, :].T

    def block(rx, rc):
        return gbuf.at[slot(rx, rc)]

    recv("z3", zb0)
    recv("z4", zc0)
    dres[half(0), :] = rr[half(0), :] + zb0[...].astype(F32) + zc0[...].astype(F32)
    recv("z2", zb1)
    recv("z5", zc1)
    dres[half(1), :] = rr[half(1), :] + zb1[...].astype(F32) + zc1[...].astype(F32)
    gbuf[slot(0, 0), :] = dres[...].astype(BF)
    for kx in (2, 1, 3):
        send(f"g{kx}", block(0, 0), block(4 - kx, 0), dev(kx=kx))
    send("gc0", block(0, 0), block(0, 1), other)

    for k in range(4):
        ds[k, 0:52, :] = dres[52 * k : 52 * k + 52, :].astype(BF)
        ds[k, 48:64, :] = jnp.where(
            lax.broadcasted_iota(jnp.int32, (16, COLS), 0) < 4, ds[k, 48:64, :].astype(F32), 0.0
        ).astype(BF)
    for k in (1, 3, 2):
        send(f"dy{k}", ds.at[at(m, k)], dr.at[m], dev(km=k))
    dr[m] = ds[m]

    for kx in (1, 3, 2):
        recv(f"g{kx}", block(4 - kx, 0))
        send(f"gc{kx}", block(4 - kx, 0), block(4 - kx, 1), other)
    tf[...] = dot(hxa[...], gbuf[0 : 4 * ROWS, :])
    for kx in (0, 1, 3, 2):
        recv(f"gc{kx}", block((4 - kx) % 4, 1))

    part = tf[...] + dot(hxb[...], gbuf[4 * ROWS : 8 * ROWS, :])
    tf[...] = part
    ts[...] = part.astype(BF)

    def rows(start, n):
        return pl.ds(pl.multiple_of(start, n), n)

    def place(ks, kz):
        return (at(s, ks) * 4 + at(zl, kz)) * 16

    for i, (ks, kz) in enumerate(along_z):
        send(f"t{ks}{kz}", ts.at[rows(place(ks, kz), 16)], zr.at[i], dev(ks=ks, kz=kz))
    for k in (1, 3, 2):
        recv(f"w{k}", wpart(c, 4 - k))
        send(f"wc{k}", wpart(c, 4 - k), wpart(c, 4 - k), other)
    late = len(sent)
    base = (x * 2 + c) * 256
    piece = tf[rows(z * 16, 16), :]
    for i, (ks, kz) in reversed(list(enumerate(along_z))):
        recv(f"t{ks}{kz}", zr.at[i])
        piece = piece + zr[i].astype(F32)
    mine = upd.at[rows(base + z * 16, 16)]
    mine[...] = piece.astype(BF)
    for ks, kz in along_z:
        send(f"u{ks}{kz}", mine, mine, dev(ks=ks, kz=kz))
    drain(late)

    for k in (1, 3, 2):
        recv(f"wc{k}", wpart(1 - c, 4 - k))
    for k in (1, 3, 2):
        recv(f"dy{k}", dr.at[at(m, 4 - k)])
    for j in range(4):
        weight = wide(*[wg[k, 512 * j : 512 * j + 512, :] for k in range(4)])
        part = dot_nt(wide(dr[0], dr[1], dr[2], dr[3]), weight)
        o_grad[0, :, 512 * j : 512 * j + 512] = part[:52].astype(BF)

    def u64(kx, ks):
        return upd.at[rows(at(x, kx) * 512 + c * 256 + at(s, ks) * 64, 64)]

    def u256(kx, kc):
        return upd.at[rows(at(x, kx) * 512 + (1 - c if kc else c) * 256, 256)]

    for ks in (0, 1, 3, 2):
        for kz in (1, 2, 3, 0):
            if ks or kz:
                source = rows(base + place(4 - ks, 4 - kz), 16)
                recv(f"u{ks}{kz}", upd.at[source])
        for kx in (2, 1, 3):
            send(f"ux{kx}{ks}", u64(0, 4 - ks), u64(0, 4 - ks), dev(kx=kx))
    send("uc0", u256(0, 0), u256(0, 0), other)
    own = upd[rows(base, 256), :].astype(F32)
    sq[...] = jnp.sum((own * own).reshape(32, 8, COLS), axis=0)
    for k in (1, 3, 2):
        send(f"sy{k}", sq, ysq.at[3 - k], dev(km=k))

    for k in (1, 3, 2):
        recv(f"sy{k}", ysq.at[3 - k])
    xs[...] = sq[...] + ysq[0] + ysq[1] + ysq[2]
    across = [(kx, kc) for kx in (2, 1, 3, 0) for kc in (1, 0) if kx or kc]
    for i, (kx, kc) in enumerate(across):
        send(f"sx{kx}{kc}", xs, xsq.at[i], dev(kx=kx, kc=kc))
    for kx in (1, 3, 2):
        for ks in (0, 1, 3, 2):
            recv(f"ux{kx}{ks}", u64(4 - kx, 4 - ks))
        send(f"uc{kx}", u256(4 - kx, 0), u256(4 - kx, 0), other)
    everything = xs[...]
    for i, (kx, kc) in enumerate(across):
        recv(f"sx{kx}{kc}", xsq.at[i])
        everything = everything + xsq[i]
    o_sq[...] = everything
    drain(len(sent) - 3)
    recv("uc0", u256(0, 1))
    for kx in (1, 3, 2):
        recv(f"uc{kx}", u256(4 - kx, 1))
    o_upd[...] = upd[...]
    drain(len(sent))


def write_results(grad_ref, raw_ref, sq_ref, o_grad, o_upd):
    o_grad[...] = grad_ref[...]
    scale = lax.rsqrt(jnp.sum(sq_ref[...]) / (D * 2 * HD) + 1e-06)
    o_upd[...] = (raw_ref[...].astype(F32) * scale).astype(BF)


def per_device(
    prefix_hidden, prefix_kv_weight, action_hidden, query_weight, action_kv_weight,
    out_cotangent, prompt_len, view_valid,
):
    vm = pltpu.VMEM
    scratch = [
        vm((ROWS, D), BF), vm((4, D, COLS), BF), vm((ACT, 1024), BF), vm((1024, 512), BF),
        vm((1024, 512), BF), vm((ACT, 512), BF), vm((4, 4, ROWS, COLS), BF), vm((ACTP, 512), BF),
        vm((QR, HD), BF), vm((QR, HD), BF), vm((HD, QR), BF), vm((HD, QR), BF),
        vm((4, ROWS, QR), F32), vm((4, ROWS, QR), F32),
        vm((4, 4, ROWS, COLS), F32), vm((4, 4, ROWS, COLS), BF),
        vm((4, 3, ROWS, COLS), BF),
        vm((ROWS, COLS), F32), vm((4, ROWS, COLS), BF),
        vm((112, COLS), BF), vm((96, COLS), BF), vm((112, COLS), BF), vm((96, COLS), BF),
        vm((112, COLS), BF), vm((96, COLS), BF),
        vm((ROWS, COLS), F32), vm((8 * ROWS, COLS), BF), vm((8 * ROWS, 256), BF),
        vm((256, 4 * ROWS), BF), vm((256, 4 * ROWS), BF), vm((256, COLS), F32), vm((256, COLS), BF),
        vm((15, 16, COLS), BF), vm((D, COLS), BF),
        vm((8, 128), F32), vm((3, 8, 128), F32), vm((8, 128), F32), vm((7, 8, 128), F32),
        vm((4, 64, COLS), BF), vm((4, 64, COLS), BF),
        pltpu.SMEM((1, VIEWS), jnp.int32),
        pltpu.SemaphoreType.DMA((8,)),
        pltpu.SemaphoreType.DMA((N_SEMS,)), pltpu.SemaphoreType.DMA((N_SEMS,)),
    ]
    smem = pl.BlockSpec(memory_space=pltpu.SMEM)
    hbm = pl.BlockSpec(memory_space=pltpu.HBM)
    grad, raw, squares = pl.pallas_call(
        kernel,
        out_shape=(
            jax.ShapeDtypeStruct((1, 52, D), BF),
            jax.ShapeDtypeStruct((D, COLS), BF),
            jax.ShapeDtypeStruct((8, 128), F32),
        ),
        in_specs=[smem] + [hbm] * 7,
        out_specs=(pl.BlockSpec(memory_space=pltpu.VMEM),) * 3,
        scratch_shapes=scratch,
        compiler_params=pltpu.CompilerParams(
            collective_id=0, has_side_effects=True, vmem_limit_bytes=40 * 1024 * 1024
        ),
    )(
        prompt_len, *[pltpu.with_memory_space_constraint(v, pltpu.HBM) for v in (view_valid, prefix_hidden, prefix_kv_weight, action_hidden, query_weight, action_kv_weight, out_cotangent)])
    return pl.pallas_call(
        write_results,
        out_shape=(
            jax.ShapeDtypeStruct((1, 52, D), BF),
            jax.ShapeDtypeStruct((D, COLS), BF),
        ),
        in_specs=[pl.BlockSpec(memory_space=pltpu.VMEM)] * 3,
        out_specs=(pl.BlockSpec(memory_space=pltpu.VMEM),) * 2,
        compiler_params=pltpu.CompilerParams(vmem_limit_bytes=40 * 1024 * 1024),
    )(grad, raw, squares)


def solution(mesh):
    return jax.shard_map(
        per_device,
        mesh=mesh,
        in_specs=(
            P("dp", "sample", None),
            P(None, "mp"),
            P("dp", "sample", None),
            P(None, "mp"),
            P(),
            P("dp", "sample", "mp"),
            P("dp"),
            P("dp", None),
        ),
        out_specs=(P("dp", ("sample", "mp"), None), P(None, "mp")),
        check_vma=False,
    )
```

```python
import jax
import jax.numpy as jnp
from jax import lax
from jax.experimental import pallas as pl
from jax.experimental.pallas import tpu as pltpu
from jax.sharding import PartitionSpec as P

BF = jnp.bfloat16
F32 = jnp.float32
D = 2048
HD = 256
ROWS = 208
COLS = 128
ACT = 300
ACTP = 304
QR = 2 * ACTP
VIEW_TOK = 256
VIEWS = 3
HORIZON = 50
NEG = -3.0e38
HALF = ((0, 112), (112, 96))
PART = ((0, 64), (64, 48), (112, 48), (160, 48))
N_SEMS = 200


def dot(a, b):
    return jnp.dot(a, b, preferred_element_type=F32)


def wide(*pieces):
    return jnp.concatenate(pieces, axis=1)


def dot_nt(a, b):
    return lax.dot_general(a, b, (((1,), (1,)), ((), ())), preferred_element_type=F32)


def kernel(
    len_ref, view_h, hid_h, w_h, act_h, wq_h, wakv_h, cot_h,
    o_grad, o_upd, o_sq,
    hid_v, wg, act_v, wq_v, wakv_v, cot_v, kv, akv, qs, gs, qt, gt, e_s, d_s,
    dkv, st, yb,
    rr, zst, za0, za1, zb0, zb1, zc0, zc1,
    dres, gbuf, hx, hxa, hxb, tf, ts, zr, upd,
    sq, ysq, xs, xsq, ds, dr,
    view_ref, lsem, ssem, rsem,
):
    dp = lax.axis_index("dp")
    s = lax.axis_index("sample")
    m = lax.axis_index("mp")
    x = dp // 8
    zl = lax.rem(dp, 8) // 2
    c = lax.rem(dp, 2)

    def at(a, k):
        return lax.rem(a + k, 4)

    z = s * 4 + zl

    def dev(kx=0, kz=0, ks=0, km=0, kc=0):
        cc = 1 - c if kc else c
        d = at(x, kx) * 8 + at(zl, kz) * 2 + cc
        return {"dp": d, "sample": at(s, ks), "mp": at(m, km)}

    along_z = [(ks, kz) for ks in (2, 1, 3, 0) for kz in (1, 2, 3, 0) if ks or kz]
    zp, zm = dev(ks=1), dev(ks=3)
    other = dev(kc=1)

    index = {}
    sent = []

    def number(name):
        return index.setdefault(name, len(index))

    def send(name, src, dst, device):
        i = number(name)
        copy = pltpu.make_async_remote_copy(
            src_ref=src, dst_ref=dst, send_sem=ssem.at[i], recv_sem=rsem.at[i],
            device_id=device, device_id_type=pl.DeviceIdType.MESH,
        )
        copy.start()
        sent.append(copy)

    def recv(name, dst, device=None):
        i = number(name)
        pltpu.make_async_remote_copy(
            src_ref=dst, dst_ref=dst, send_sem=ssem.at[i], recv_sem=rsem.at[i],
            device_id=other if device is None else device,
            device_id_type=pl.DeviceIdType.MESH,
        ).wait_recv()

    def drain(n):
        for copy in sent[:n]:
            copy.wait_send()
        del sent[:n]

    loads = [
        pltpu.make_async_copy(hid_h.at[0, 0:112], hid_v.at[0:112], lsem.at[0]),
        pltpu.make_async_copy(w_h, wg.at[m], lsem.at[1]),
        pltpu.make_async_copy(act_h.at[0], act_v, lsem.at[2]),
        pltpu.make_async_copy(wq_h, wq_v, lsem.at[3]),
        pltpu.make_async_copy(wakv_h, wakv_v, lsem.at[4]),
        pltpu.make_async_copy(cot_h.at[0], cot_v, lsem.at[5]),
        pltpu.make_async_copy(hid_h.at[0, 112:208], hid_v.at[112:208], lsem.at[6]),
    ]
    loads.append(pltpu.make_async_copy(view_h, view_ref, lsem.at[7]))
    for i in (1, 0, 6, 7):
        loads[i].start()

    barrier = pltpu.get_barrier_semaphore()
    peers = [dev(km=k) for k in (1, 2, 3)] + [dev(ks=ks, kz=kz) for ks, kz in along_z] + [other]
    peers += [dev(kx=k, kc=kc) for k in (1, 2, 3) for kc in (0, 1)]
    for peer in peers:
        pl.semaphore_signal(
            barrier, inc=1, device_id=peer, device_id_type=pl.DeviceIdType.MESH
        )

    def kvp(r, i):
        r0, n = PART[i]
        return kv.at[r, m, pl.ds(r0, n)]

    def ysend(r, h):
        r0, n = HALF[h]
        block = kv.at[r, m, pl.ds(r0, n)]
        for k in (2, 1, 3):
            send(f"y{r}{k}{h}", block, block, dev(km=k))

    def ywait(r):
        for h in (0, 1):
            r0, n = HALF[h]
            for k in (1, 3, 2):
                recv(f"y{r}{k}{h}", kv.at[r, at(m, 4 - k), pl.ds(r0, n)])

    def ylast(i):
        for k in (2, 1, 3):
            send(f"yl{k}{i}", kvp(2, i), kvp(2, i), dev(km=k))

    def ylast_wait(h):
        for i in (2 * h, 2 * h + 1):
            r0, n = PART[i]
            for k in (1, 3, 2):
                recv(f"yl{k}{i}", kv.at[2, at(m, 4 - k), pl.ds(r0, n)])

    loads[1].wait()
    loads[0].wait()
    for i in (2, 3, 5, 4):
        loads[i].start()
    kv[0, m, 0:112, :] = dot(hid_v[0:112], wg[m]).astype(BF)
    pl.semaphore_wait(barrier, len(peers))
    for i in (0, 1):
        send(f"zp{i}", kvp(0, i), kvp(3, i), zp)
    loads[6].wait()
    kv[0, m, 112:208, :] = dot(hid_v[112:208], wg[m]).astype(BF)
    for i in (2, 3):
        send(f"zm{i}", kvp(0, i), kvp(1, i), zm)
    for i, j in ((2, 0), (3, 1)):
        send(f"zp{i}", kvp(0, i), kvp(3, i), zp)
        send(f"zm{j}", kvp(0, j), kvp(1, j), zm)
    ysend(0, 0)
    ysend(0, 1)

    def slot(rx, rc):
        return pl.ds((rc * 4 + rx) * ROWS, ROWS)

    def hidden_columns(kx, kc):
        j = at(x, kx) * 2 + (1 - c if kc else c)
        return pl.ds(pl.multiple_of(j * 256, 256), 256)

    def send_hidden(kx):
        for kc in (0, 1):
            send(f"hx{kx}{kc}", hid_v.at[:, hidden_columns(kx, kc)],
                 hx.at[slot(4 - kx, kc)], dev(kx=kx, kc=kc))

    first = len(sent)
    send_hidden(1)
    send_hidden(3)
    send("hx01", hid_v.at[:, hidden_columns(0, 1)], hx.at[slot(0, 1)], other)
    hx[slot(0, 0), :] = hid_v[:, hidden_columns(0, 0)]

    for ref in (qs, gs):
        ref[288:304, :] = jnp.zeros((16, HD), BF)
        ref[592:608, :] = jnp.zeros((16, HD), BF)
    akv[288:304, :] = jnp.zeros((16, 2 * HD), BF)
    loads[2].wait()
    loads[3].wait()
    queries = (dot(act_v[...], wq_v[...]).astype(BF).astype(F32) * (HD**-0.5)).astype(BF)
    qs[0:ACT, :] = queries[:, :HD]
    qs[ACTP : ACTP + ACT, :] = queries[:, HD:]
    loads[4].wait()
    akv[0:ACT, :] = dot(act_v[...], wakv_v[...]).astype(BF)
    loads[5].wait()
    gs[0:ACT, :] = cot_v[:, :HD]
    gs[ACTP : ACTP + ACT, :] = cot_v[:, HD:]

    qt[...] = qs[...].T
    gt[...] = gs[...].T

    def half(h):
        r0, n = HALF[h]
        return pl.ds(r0, n)

    block_max, block_sum, block_dot = {}, {}, {}

    def attend(r, keys, values, mask, e_ref, d_ref):
        scores = mask(dot(keys, qt[...]))
        top = jnp.max(scores, axis=0, keepdims=True)
        e = jnp.exp(scores - top)
        d = dot(values, gt[...])
        if e_ref is not None:
            e_ref[...] = e
            d_ref[...] = d
        block_max[r] = top
        block_sum[r] = jnp.sum(e, axis=0, keepdims=True)
        block_dot[r] = jnp.sum(e * d, axis=0, keepdims=True)

    def draw(i):
        total = jnp.zeros_like(i)
        for t in range(1, ACTP // HORIZON + 1):
            total = total + jnp.where(i >= t * HORIZON, 1, 0)
        return total

    for i, j in ((0, 2), (1, 3)):
        recv(f"zp{i}", kvp(3, i))
        send(f"zf{i}", kvp(3, i), kvp(2, i), zp)
        recv(f"zm{j}", kvp(1, j))
        send(f"zf{j}", kvp(1, j), kvp(2, j), zm)
    ysend(3, 0)
    ysend(1, 1)

    key_draw = draw(lax.broadcasted_iota(jnp.int32, (ACTP, 1), 0))
    query_index = lax.broadcasted_iota(jnp.int32, (1, QR), 1)
    query_draw = draw(query_index - jnp.where(query_index >= ACTP, ACTP, 0))
    attend(
        "a", akv[:, :HD], akv[:, HD:],
        lambda scores: jnp.where(key_draw == query_draw, scores, NEG), None, None,
    )

    loads[7].wait()

    def attend_prefix(r, part=None):
        r0, n = (0, ROWS) if part is None else HALF[part]
        p = at(s, r) * ROWS + r0 + lax.broadcasted_iota(jnp.int32, (n, 1), 0)
        usable = jnp.where(p >= VIEWS * VIEW_TOK, jnp.where(p - VIEWS * VIEW_TOK < len_ref[0], 1, 0), 0)
        for v in range(VIEWS):
            inside = jnp.where(p >= v * VIEW_TOK, 1, 0) * jnp.where(p < (v + 1) * VIEW_TOK, 1, 0)
            usable = usable + inside * jnp.where(view_ref[0, v] == 1, 1, 0)
        ceiling = jnp.where(usable > 0, -NEG, NEG)
        some = pl.ds(r0, n)
        attend(
            r if part is None else (r, part),
            wide(kv[r, 0, some, :], kv[r, 1, some, :]), wide(kv[r, 2, some, :], kv[r, 3, some, :]),
            lambda scores: jnp.minimum(scores, ceiling), e_s.at[r, some], d_s.at[r, some],
        )

    for i in (2, 3):
        recv(f"zp{i}", kvp(3, i))
    ysend(3, 1)
    for i in (0, 1):
        recv(f"zm{i}", kvp(1, i))
    ysend(1, 0)
    ywait(0)
    attend_prefix(0)
    for i in (0, 2, 1, 3):
        recv(f"zf{i}", kvp(2, i))
        ylast(i)
    send_hidden(2)
    ywait(3)
    attend_prefix(3)
    ywait(1)
    attend_prefix(1)
    drain(first)

    def merge(parts):
        top = block_max[parts[0]]
        for i in parts[1:]:
            top = jnp.maximum(top, block_max[i])
        scaled = [jnp.exp(block_max[i] - top) for i in parts]
        total = sum(f * block_sum[i] for f, i in zip(scaled, parts))
        return top, total, sum(f * block_dot[i] for f, i in zip(scaled, parts))

    block_max["m"], block_sum["m"], block_dot["m"] = merge(("a", 0, 1, 3))
    for h in (0, 1):
        ylast_wait(h)
        attend_prefix(2, h)
    top, total, row_dot = merge(("m", (2, 0), (2, 1)))
    inverse = 1.0 / total
    row_dot = row_dot * inverse

    def gradients(r, h):
        largest = block_max[(2, h) if r == 2 else r]
        p = e_s[r, half(h), :] * (jnp.exp(largest - top) * inverse)
        d = p * (d_s[r, half(h), :] - row_dot)
        dk = dot(d.astype(BF), qs[...])
        dv = dot(p.astype(BF), gs[...])
        for k in range(4):
            columns = (dk, dv)[k // 2][:, (k % 2) * COLS : (k % 2 + 1) * COLS]
            dkv[r, k, half(h), :] = columns
            st[r, k, half(h), :] = columns.astype(BF)
        for k in (2, 1, 3):
            send(f"r{r}{k}{h}", st.at[r, at(m, k), half(h)], yb.at[r, 3 - k, half(h)], dev(km=k))

    def finish(r, h):
        piece = dkv[r, m, half(h), :]
        for k in (1, 3, 2):
            recv(f"r{r}{k}{h}", yb.at[r, 3 - k, half(h)])
            piece = piece + yb[r, 3 - k, half(h), :].astype(F32)
        return piece

    order = ((2, 0), (2, 1), (1, 1), (3, 0), (1, 0), (3, 1))
    for r, h in order:
        gradients(r, h)
    for i, (r, h) in enumerate(order[:4]):
        zst[r, half(h), :] = finish(r, h).astype(BF)
        target = (za0, za1, zb1, zb0)[i]
        send(f"z{i}", zst.at[r, half(h)], target, zm if i % 2 else zp)
        if i < 2:
            gradients(0, i)
    for i, (r, h), arrived, target in ((4, order[4], za0, zc0), (5, order[5], za1, zc1)):
        piece = finish(r, h)
        recv(f"z{i - 4}", arrived)
        zst[r, half(h), :] = (piece + arrived[...].astype(F32)).astype(BF)
        send(f"z{i}", zst.at[r, half(h)], target, zm if i % 2 else zp)

    def wpart(part, k):
        return wg.at[at(m, k), pl.ds(pl.multiple_of(part * 1024, 1024), 1024)]

    for k in (2, 1, 3):
        send(f"w{k}", wpart(c, 0), wpart(c, 0), dev(km=k))

    for h in (0, 1):
        rr[half(h), :] = finish(0, h)
    for kx in (1, 3, 2):
        for kc in (0, 1):
            recv(f"hx{kx}{kc}", hx.at[slot(4 - kx, kc)])
    recv("hx01", hx.at[slot(0, 1)])
    hxa[...] = hx[0 : 4 * ROWS, :].T
    hxb[...] = hx[4 * ROWS : 8 * ROWS, :].T

    def block(rx, rc):
        return gbuf.at[slot(rx, rc)]

    recv("z3", zb0)
    recv("z4", zc0)
    dres[half(0), :] = rr[half(0), :] + zb0[...].astype(F32) + zc0[...].astype(F32)
    recv("z2", zb1)
    recv("z5", zc1)
    dres[half(1), :] = rr[half(1), :] + zb1[...].astype(F32) + zc1[...].astype(F32)
    gbuf[slot(0, 0), :] = dres[...].astype(BF)
    for kx in (2, 1, 3):
        send(f"g{kx}", block(0, 0), block(4 - kx, 0), dev(kx=kx))
    send("gc0", block(0, 0), block(0, 1), other)

    for k in range(4):
        ds[k, 0:52, :] = dres[52 * k : 52 * k + 52, :].astype(BF)
        ds[k, 48:64, :] = jnp.where(
            lax.broadcasted_iota(jnp.int32, (16, COLS), 0) < 4, ds[k, 48:64, :].astype(F32), 0.0
        ).astype(BF)
    for k in (1, 3, 2):
        send(f"dy{k}", ds.at[at(m, k)], dr.at[m], dev(km=k))
    dr[m] = ds[m]

    for kx in (1, 3, 2):
        recv(f"g{kx}", block(4 - kx, 0))
        send(f"gc{kx}", block(4 - kx, 0), block(4 - kx, 1), other)
    tf[...] = dot(hxa[...], gbuf[0 : 4 * ROWS, :])
    for kx in (0, 1, 3, 2):
        recv(f"gc{kx}", block((4 - kx) % 4, 1))

    part = tf[...] + dot(hxb[...], gbuf[4 * ROWS : 8 * ROWS, :])
    tf[...] = part
    ts[...] = part.astype(BF)

    def rows(start, n):
        return pl.ds(pl.multiple_of(start, n), n)

    def place(ks, kz):
        return (at(s, ks) * 4 + at(zl, kz)) * 16

    for i, (ks, kz) in enumerate(along_z):
        send(f"t{ks}{kz}", ts.at[rows(place(ks, kz), 16)], zr.at[i], dev(ks=ks, kz=kz))
    for k in (1, 3, 2):
        recv(f"w{k}", wpart(c, 4 - k))
        send(f"wc{k}", wpart(c, 4 - k), wpart(c, 4 - k), other)
    late = len(sent)
    base = (x * 2 + c) * 256
    piece = tf[rows(z * 16, 16), :]
    for i, (ks, kz) in reversed(list(enumerate(along_z))):
        recv(f"t{ks}{kz}", zr.at[i])
        piece = piece + zr[i].astype(F32)
    mine = upd.at[rows(base + z * 16, 16)]
    mine[...] = piece.astype(BF)
    for ks, kz in along_z:
        send(f"u{ks}{kz}", mine, mine, dev(ks=ks, kz=kz))
    drain(late)

    for k in (1, 3, 2):
        recv(f"wc{k}", wpart(1 - c, 4 - k))
    for k in (1, 3, 2):
        recv(f"dy{k}", dr.at[at(m, 4 - k)])
    for j in range(4):
        weight = wide(*[wg[k, 512 * j : 512 * j + 512, :] for k in range(4)])
        part = dot_nt(wide(dr[0], dr[1], dr[2], dr[3]), weight)
        o_grad[0, :, 512 * j : 512 * j + 512] = part[:52].astype(BF)

    def u64(kx, ks):
        return upd.at[rows(at(x, kx) * 512 + c * 256 + at(s, ks) * 64, 64)]

    def u256(kx, kc):
        return upd.at[rows(at(x, kx) * 512 + (1 - c if kc else c) * 256, 256)]

    for ks in (0, 1, 3, 2):
        for kz in (1, 2, 3, 0):
            if ks or kz:
                source = rows(base + place(4 - ks, 4 - kz), 16)
                recv(f"u{ks}{kz}", upd.at[source])
        for kx in (2, 1, 3):
            send(f"ux{kx}{ks}", u64(0, 4 - ks), u64(0, 4 - ks), dev(kx=kx))
    send("uc0", u256(0, 0), u256(0, 0), other)
    own = upd[rows(base, 256), :].astype(F32)
    sq[...] = jnp.sum((own * own).reshape(32, 8, COLS), axis=0)
    for k in (1, 3, 2):
        send(f"sy{k}", sq, ysq.at[3 - k], dev(km=k))

    for k in (1, 3, 2):
        recv(f"sy{k}", ysq.at[3 - k])
    xs[...] = sq[...] + ysq[0] + ysq[1] + ysq[2]
    across = [(kx, kc) for kx in (2, 1, 3, 0) for kc in (1, 0) if kx or kc]
    for i, (kx, kc) in enumerate(across):
        send(f"sx{kx}{kc}", xs, xsq.at[i], dev(kx=kx, kc=kc))
    for kx in (1, 3, 2):
        for ks in (0, 1, 3, 2):
            recv(f"ux{kx}{ks}", u64(4 - kx, 4 - ks))
        send(f"uc{kx}", u256(4 - kx, 0), u256(4 - kx, 0), other)
    everything = xs[...]
    for i, (kx, kc) in enumerate(across):
        recv(f"sx{kx}{kc}", xsq.at[i])
        everything = everything + xsq[i]
    o_sq[...] = everything
    drain(len(sent) - 3)
    recv("uc0", u256(0, 1))
    for kx in (1, 3, 2):
        recv(f"uc{kx}", u256(4 - kx, 1))
    o_upd[...] = upd[...]
    drain(len(sent))


def write_results(grad_ref, raw_ref, sq_ref, o_grad, o_upd):
    o_grad[...] = grad_ref[...]
    scale = lax.rsqrt(jnp.sum(sq_ref[...]) / (D * 2 * HD) + 1e-06)
    o_upd[...] = (raw_ref[...].astype(F32) * scale).astype(BF)


def per_device(
    prefix_hidden, prefix_kv_weight, action_hidden, query_weight, action_kv_weight,
    out_cotangent, prompt_len, view_valid,
):
    vm = pltpu.VMEM
    scratch = [
        vm((ROWS, D), BF), vm((4, D, COLS), BF), vm((ACT, 1024), BF), vm((1024, 512), BF),
        vm((1024, 512), BF), vm((ACT, 512), BF), vm((4, 4, ROWS, COLS), BF), vm((ACTP, 512), BF),
        vm((QR, HD), BF), vm((QR, HD), BF), vm((HD, QR), BF), vm((HD, QR), BF),
        vm((4, ROWS, QR), F32), vm((4, ROWS, QR), F32),
        vm((4, 4, ROWS, COLS), F32), vm((4, 4, ROWS, COLS), BF),
        vm((4, 3, ROWS, COLS), BF),
        vm((ROWS, COLS), F32), vm((4, ROWS, COLS), BF),
        vm((112, COLS), BF), vm((96, COLS), BF), vm((112, COLS), BF), vm((96, COLS), BF),
        vm((112, COLS), BF), vm((96, COLS), BF),
        vm((ROWS, COLS), F32), vm((8 * ROWS, COLS), BF), vm((8 * ROWS, 256), BF),
        vm((256, 4 * ROWS), BF), vm((256, 4 * ROWS), BF), vm((256, COLS), F32), vm((256, COLS), BF),
        vm((15, 16, COLS), BF), vm((D, COLS), BF),
        vm((8, 128), F32), vm((3, 8, 128), F32), vm((8, 128), F32), vm((7, 8, 128), F32),
        vm((4, 64, COLS), BF), vm((4, 64, COLS), BF),
        pltpu.SMEM((1, VIEWS), jnp.int32),
        pltpu.SemaphoreType.DMA((8,)),
        pltpu.SemaphoreType.DMA((N_SEMS,)), pltpu.SemaphoreType.DMA((N_SEMS,)),
    ]
    smem = pl.BlockSpec(memory_space=pltpu.SMEM)
    hbm = pl.BlockSpec(memory_space=pltpu.HBM)
    grad, raw, squares = pl.pallas_call(
        kernel,
        out_shape=(
            jax.ShapeDtypeStruct((1, 52, D), BF),
            jax.ShapeDtypeStruct((D, COLS), BF),
            jax.ShapeDtypeStruct((8, 128), F32),
        ),
        in_specs=[smem] + [hbm] * 7,
        out_specs=(pl.BlockSpec(memory_space=pltpu.VMEM),) * 3,
        scratch_shapes=scratch,
        compiler_params=pltpu.CompilerParams(
            collective_id=0, has_side_effects=True, vmem_limit_bytes=40 * 1024 * 1024
        ),
    )(
        prompt_len, *[pltpu.with_memory_space_constraint(v, pltpu.HBM) for v in (view_valid, prefix_hidden, prefix_kv_weight, action_hidden, query_weight, action_kv_weight, out_cotangent)])
    return pl.pallas_call(
        write_results,
        out_shape=(
            jax.ShapeDtypeStruct((1, 52, D), BF),
            jax.ShapeDtypeStruct((D, COLS), BF),
        ),
        in_specs=[pl.BlockSpec(memory_space=pltpu.VMEM)] * 3,
        out_specs=(pl.BlockSpec(memory_space=pltpu.VMEM),) * 2,
        compiler_params=pltpu.CompilerParams(vmem_limit_bytes=40 * 1024 * 1024),
    )(grad, raw, squares)


def solution(mesh):
    return jax.shard_map(
        per_device,
        mesh=mesh,
        in_specs=(
            P("dp", "sample", None),
            P(None, "mp"),
            P("dp", "sample", None),
            P(None, "mp"),
            P(),
            P("dp", "sample", "mp"),
            P("dp"),
            P("dp", None),
        ),
        out_specs=(P("dp", ("sample", "mp"), None), P(None, "mp")),
        check_vma=False,
    )
```

```python
import jax
import jax.numpy as jnp
from jax import lax
from jax.experimental import pallas as pl
from jax.experimental.pallas import tpu as pltpu
from jax.sharding import PartitionSpec as P

BF = jnp.bfloat16
F32 = jnp.float32
D = 2048
HD = 256
ROWS = 208
COLS = 128
ACT = 300
ACTP = 304
QR = 2 * ACTP
VIEW_TOK = 256
VIEWS = 3
HORIZON = 50
NEG = -3.0e38
HALF = ((0, 112), (112, 96))
PART = ((0, 64), (64, 48), (112, 48), (160, 48))
N_SEMS = 200


def dot(a, b):
    return jnp.dot(a, b, preferred_element_type=F32)


def wide(*pieces):
    return jnp.concatenate(pieces, axis=1)


def dot_nt(a, b):
    return lax.dot_general(a, b, (((1,), (1,)), ((), ())), preferred_element_type=F32)


def kernel(
    len_ref, view_h, hid_h, w_h, act_h, wq_h, wakv_h, cot_h,
    o_grad, o_upd, o_sq,
    hid_v, wg, act_v, wq_v, wakv_v, cot_v, kv, akv, qs, gs, qt, gt, e_s, d_s,
    dkv, st, yb,
    rr, zst, za0, za1, zb0, zb1, zc0, zc1,
    dres, gbuf, hx, hxa, hxb, tf, ts, zr, upd,
    sq, ysq, xs, xsq, ds, dr,
    view_ref, lsem, ssem, rsem,
):
    dp = lax.axis_index("dp")
    s = lax.axis_index("sample")
    m = lax.axis_index("mp")
    x = dp // 8
    zl = lax.rem(dp, 8) // 2
    c = lax.rem(dp, 2)

    def at(a, k):
        return lax.rem(a + k, 4)

    z = s * 4 + zl

    def dev(kx=0, kz=0, ks=0, km=0, kc=0):
        cc = 1 - c if kc else c
        d = at(x, kx) * 8 + at(zl, kz) * 2 + cc
        return {"dp": d, "sample": at(s, ks), "mp": at(m, km)}

    along_z = [(ks, kz) for ks in (2, 1, 3, 0) for kz in (1, 2, 3, 0) if ks or kz]
    zp, zm = dev(ks=1), dev(ks=3)
    other = dev(kc=1)

    index = {}
    sent = []

    def number(name):
        return index.setdefault(name, len(index))

    def send(name, src, dst, device):
        i = number(name)
        copy = pltpu.make_async_remote_copy(
            src_ref=src, dst_ref=dst, send_sem=ssem.at[i], recv_sem=rsem.at[i],
            device_id=device, device_id_type=pl.DeviceIdType.MESH,
        )
        copy.start()
        sent.append(copy)

    def recv(name, dst, device=None):
        i = number(name)
        pltpu.make_async_remote_copy(
            src_ref=dst, dst_ref=dst, send_sem=ssem.at[i], recv_sem=rsem.at[i],
            device_id=other if device is None else device,
            device_id_type=pl.DeviceIdType.MESH,
        ).wait_recv()

    def drain(n):
        for copy in sent[:n]:
            copy.wait_send()
        del sent[:n]

    loads = [
        pltpu.make_async_copy(hid_h.at[0, 0:112], hid_v.at[0:112], lsem.at[0]),
        pltpu.make_async_copy(w_h, wg.at[m], lsem.at[1]),
        pltpu.make_async_copy(act_h.at[0], act_v, lsem.at[2]),
        pltpu.make_async_copy(wq_h, wq_v, lsem.at[3]),
        pltpu.make_async_copy(wakv_h, wakv_v, lsem.at[4]),
        pltpu.make_async_copy(cot_h.at[0], cot_v, lsem.at[5]),
        pltpu.make_async_copy(hid_h.at[0, 112:208], hid_v.at[112:208], lsem.at[6]),
    ]
    loads.append(pltpu.make_async_copy(view_h, view_ref, lsem.at[7]))
    for i in (1, 0, 6, 7):
        loads[i].start()

    barrier = pltpu.get_barrier_semaphore()
    peers = [dev(km=k) for k in (1, 2, 3)] + [dev(ks=ks, kz=kz) for ks, kz in along_z] + [other]
    peers += [dev(kx=k, kc=kc) for k in (1, 2, 3) for kc in (0, 1)]
    for peer in peers:
        pl.semaphore_signal(
            barrier, inc=1, device_id=peer, device_id_type=pl.DeviceIdType.MESH
        )

    def kvp(r, i):
        r0, n = PART[i]
        return kv.at[r, m, pl.ds(r0, n)]

    def ysend(r, h):
        r0, n = HALF[h]
        block = kv.at[r, m, pl.ds(r0, n)]
        for k in (2, 1, 3):
            send(f"y{r}{k}{h}", block, block, dev(km=k))

    def ywait(r):
        for h in (0, 1):
            r0, n = HALF[h]
            for k in (1, 3, 2):
                recv(f"y{r}{k}{h}", kv.at[r, at(m, 4 - k), pl.ds(r0, n)])

    def ylast(i):
        for k in (2, 1, 3):
            send(f"yl{k}{i}", kvp(2, i), kvp(2, i), dev(km=k))

    def ylast_wait(h):
        for i in (2 * h, 2 * h + 1):
            r0, n = PART[i]
            for k in (1, 3, 2):
                recv(f"yl{k}{i}", kv.at[2, at(m, 4 - k), pl.ds(r0, n)])

    loads[1].wait()
    loads[0].wait()
    for i in (2, 3, 5, 4):
        loads[i].start()
    kv[0, m, 0:112, :] = dot(hid_v[0:112], wg[m]).astype(BF)
    pl.semaphore_wait(barrier, len(peers))
    for i in (0, 1):
        send(f"zp{i}", kvp(0, i), kvp(3, i), zp)
    loads[6].wait()
    kv[0, m, 112:208, :] = dot(hid_v[112:208], wg[m]).astype(BF)
    for i in (2, 3):
        send(f"zm{i}", kvp(0, i), kvp(1, i), zm)
    for i, j in ((2, 0), (3, 1)):
        send(f"zp{i}", kvp(0, i), kvp(3, i), zp)
        send(f"zm{j}", kvp(0, j), kvp(1, j), zm)
    ysend(0, 0)
    ysend(0, 1)

    def slot(rx, rc):
        return pl.ds((rc * 4 + rx) * ROWS, ROWS)

    def hidden_columns(kx, kc):
        j = at(x, kx) * 2 + (1 - c if kc else c)
        return pl.ds(pl.multiple_of(j * 256, 256), 256)

    def send_hidden(kx):
        for kc in (0, 1):
            send(f"hx{kx}{kc}", hid_v.at[:, hidden_columns(kx, kc)],
                 hx.at[slot(4 - kx, kc)], dev(kx=kx, kc=kc))

    first = len(sent)
    send_hidden(1)
    send_hidden(3)
    send("hx01", hid_v.at[:, hidden_columns(0, 1)], hx.at[slot(0, 1)], other)
    hx[slot(0, 0), :] = hid_v[:, hidden_columns(0, 0)]

    for ref in (qs, gs):
        ref[288:304, :] = jnp.zeros((16, HD), BF)
        ref[592:608, :] = jnp.zeros((16, HD), BF)
    akv[288:304, :] = jnp.zeros((16, 2 * HD), BF)
    loads[2].wait()
    loads[3].wait()
    queries = (dot(act_v[...], wq_v[...]).astype(BF).astype(F32) * (HD**-0.5)).astype(BF)
    qs[0:ACT, :] = queries[:, :HD]
    qs[ACTP : ACTP + ACT, :] = queries[:, HD:]
    loads[4].wait()
    akv[0:ACT, :] = dot(act_v[...], wakv_v[...]).astype(BF)
    loads[5].wait()
    gs[0:ACT, :] = cot_v[:, :HD]
    gs[ACTP : ACTP + ACT, :] = cot_v[:, HD:]

    qt[...] = qs[...].T
    gt[...] = gs[...].T

    def half(h):
        r0, n = HALF[h]
        return pl.ds(r0, n)

    block_max, block_sum, block_dot = {}, {}, {}

    def attend(r, keys, values, mask, e_ref, d_ref):
        scores = mask(dot(keys, qt[...]))
        top = jnp.max(scores, axis=0, keepdims=True)
        e = jnp.exp(scores - top)
        d = dot(values, gt[...])
        if e_ref is not None:
            e_ref[...] = e
            d_ref[...] = d
        block_max[r] = top
        block_sum[r] = jnp.sum(e, axis=0, keepdims=True)
        block_dot[r] = jnp.sum(e * d, axis=0, keepdims=True)

    def draw(i):
        total = jnp.zeros_like(i)
        for t in range(1, ACTP // HORIZON + 1):
            total = total + jnp.where(i >= t * HORIZON, 1, 0)
        return total

    for i, j in ((0, 2), (1, 3)):
        recv(f"zp{i}", kvp(3, i))
        send(f"zf{i}", kvp(3, i), kvp(2, i), zp)
        recv(f"zm{j}", kvp(1, j))
        send(f"zf{j}", kvp(1, j), kvp(2, j), zm)
    ysend(3, 0)
    ysend(1, 1)

    key_draw = draw(lax.broadcasted_iota(jnp.int32, (ACTP, 1), 0))
    query_index = lax.broadcasted_iota(jnp.int32, (1, QR), 1)
    query_draw = draw(query_index - jnp.where(query_index >= ACTP, ACTP, 0))
    attend(
        "a", akv[:, :HD], akv[:, HD:],
        lambda scores: jnp.where(key_draw == query_draw, scores, NEG), None, None,
    )

    loads[7].wait()

    def attend_prefix(r, part=None):
        r0, n = (0, ROWS) if part is None else HALF[part]
        p = at(s, r) * ROWS + r0 + lax.broadcasted_iota(jnp.int32, (n, 1), 0)
        usable = jnp.where(p >= VIEWS * VIEW_TOK, jnp.where(p - VIEWS * VIEW_TOK < len_ref[0], 1, 0), 0)
        for v in range(VIEWS):
            inside = jnp.where(p >= v * VIEW_TOK, 1, 0) * jnp.where(p < (v + 1) * VIEW_TOK, 1, 0)
            usable = usable + inside * jnp.where(view_ref[0, v] == 1, 1, 0)
        ceiling = jnp.where(usable > 0, -NEG, NEG)
        some = pl.ds(r0, n)
        attend(
            r if part is None else (r, part),
            wide(kv[r, 0, some, :], kv[r, 1, some, :]), wide(kv[r, 2, some, :], kv[r, 3, some, :]),
            lambda scores: jnp.minimum(scores, ceiling), e_s.at[r, some], d_s.at[r, some],
        )

    for i in (2, 3):
        recv(f"zp{i}", kvp(3, i))
    ysend(3, 1)
    for i in (0, 1):
        recv(f"zm{i}", kvp(1, i))
    ysend(1, 0)
    ywait(0)
    attend_prefix(0)
    for i in (0, 2, 1, 3):
        recv(f"zf{i}", kvp(2, i))
        ylast(i)
    send_hidden(2)
    ywait(3)
    attend_prefix(3)
    ywait(1)
    attend_prefix(1)
    drain(first)

    def merge(parts):
        top = block_max[parts[0]]
        for i in parts[1:]:
            top = jnp.maximum(top, block_max[i])
        scaled = [jnp.exp(block_max[i] - top) for i in parts]
        total = sum(f * block_sum[i] for f, i in zip(scaled, parts))
        return top, total, sum(f * block_dot[i] for f, i in zip(scaled, parts))

    block_max["m"], block_sum["m"], block_dot["m"] = merge(("a", 0, 1, 3))
    for h in (0, 1):
        ylast_wait(h)
        attend_prefix(2, h)
    top, total, row_dot = merge(("m", (2, 0), (2, 1)))
    inverse = 1.0 / total
    row_dot = row_dot * inverse

    def gradients(r, h):
        largest = block_max[(2, h) if r == 2 else r]
        p = e_s[r, half(h), :] * (jnp.exp(largest - top) * inverse)
        d = p * (d_s[r, half(h), :] - row_dot)
        dk = dot(d.astype(BF), qs[...])
        dv = dot(p.astype(BF), gs[...])
        for k in range(4):
            columns = (dk, dv)[k // 2][:, (k % 2) * COLS : (k % 2 + 1) * COLS]
            dkv[r, k, half(h), :] = columns
            st[r, k, half(h), :] = columns.astype(BF)
        for k in (2, 1, 3):
            send(f"r{r}{k}{h}", st.at[r, at(m, k), half(h)], yb.at[r, 3 - k, half(h)], dev(km=k))

    def finish(r, h):
        piece = dkv[r, m, half(h), :]
        for k in (1, 3, 2):
            recv(f"r{r}{k}{h}", yb.at[r, 3 - k, half(h)])
            piece = piece + yb[r, 3 - k, half(h), :].astype(F32)
        return piece

    order = ((2, 0), (2, 1), (1, 1), (3, 0), (1, 0), (3, 1))
    for r, h in order:
        gradients(r, h)
    for i, (r, h) in enumerate(order[:4]):
        zst[r, half(h), :] = finish(r, h).astype(BF)
        target = (za0, za1, zb1, zb0)[i]
        send(f"z{i}", zst.at[r, half(h)], target, zm if i % 2 else zp)
        if i < 2:
            gradients(0, i)
    for i, (r, h), arrived, target in ((4, order[4], za0, zc0), (5, order[5], za1, zc1)):
        piece = finish(r, h)
        recv(f"z{i - 4}", arrived)
        zst[r, half(h), :] = (piece + arrived[...].astype(F32)).astype(BF)
        send(f"z{i}", zst.at[r, half(h)], target, zm if i % 2 else zp)

    def wpart(part, k):
        return wg.at[at(m, k), pl.ds(pl.multiple_of(part * 1024, 1024), 1024)]

    for k in (2, 1, 3):
        send(f"w{k}", wpart(c, 0), wpart(c, 0), dev(km=k))

    for h in (0, 1):
        rr[half(h), :] = finish(0, h)
    for kx in (1, 3, 2):
        for kc in (0, 1):
            recv(f"hx{kx}{kc}", hx.at[slot(4 - kx, kc)])
    recv("hx01", hx.at[slot(0, 1)])
    hxa[...] = hx[0 : 4 * ROWS, :].T
    hxb[...] = hx[4 * ROWS : 8 * ROWS, :].T

    def block(rx, rc):
        return gbuf.at[slot(rx, rc)]

    recv("z3", zb0)
    recv("z4", zc0)
    dres[half(0), :] = rr[half(0), :] + zb0[...].astype(F32) + zc0[...].astype(F32)
    recv("z2", zb1)
    recv("z5", zc1)
    dres[half(1), :] = rr[half(1), :] + zb1[...].astype(F32) + zc1[...].astype(F32)
    gbuf[slot(0, 0), :] = dres[...].astype(BF)
    for kx in (2, 1, 3):
        send(f"g{kx}", block(0, 0), block(4 - kx, 0), dev(kx=kx))
    send("gc0", block(0, 0), block(0, 1), other)

    for k in range(4):
        ds[k, 0:52, :] = dres[52 * k : 52 * k + 52, :].astype(BF)
        ds[k, 48:64, :] = jnp.where(
            lax.broadcasted_iota(jnp.int32, (16, COLS), 0) < 4, ds[k, 48:64, :].astype(F32), 0.0
        ).astype(BF)
    for k in (1, 3, 2):
        send(f"dy{k}", ds.at[at(m, k)], dr.at[m], dev(km=k))
    dr[m] = ds[m]

    for kx in (1, 3, 2):
        recv(f"g{kx}", block(4 - kx, 0))
        send(f"gc{kx}", block(4 - kx, 0), block(4 - kx, 1), other)
    tf[...] = dot(hxa[...], gbuf[0 : 4 * ROWS, :])
    for kx in (0, 1, 3, 2):
        recv(f"gc{kx}", block((4 - kx) % 4, 1))

    part = tf[...] + dot(hxb[...], gbuf[4 * ROWS : 8 * ROWS, :])
    tf[...] = part
    ts[...] = part.astype(BF)

    def rows(start, n):
        return pl.ds(pl.multiple_of(start, n), n)

    def place(ks, kz):
        return (at(s, ks) * 4 + at(zl, kz)) * 16

    for i, (ks, kz) in enumerate(along_z):
        send(f"t{ks}{kz}", ts.at[rows(place(ks, kz), 16)], zr.at[i], dev(ks=ks, kz=kz))
    late = len(sent)
    base = (x * 2 + c) * 256
    piece = tf[rows(z * 16, 16), :]
    for i, (ks, kz) in reversed(list(enumerate(along_z))):
        recv(f"t{ks}{kz}", zr.at[i])
        piece = piece + zr[i].astype(F32)
    mine = upd.at[rows(base + z * 16, 16)]
    mine[...] = piece.astype(BF)
    for ks, kz in along_z:
        send(f"u{ks}{kz}", mine, mine, dev(ks=ks, kz=kz))
    for k in (1, 3, 2):
        recv(f"w{k}", wpart(c, 4 - k))
        send(f"wc{k}", wpart(c, 4 - k), wpart(c, 4 - k), other)
    drain(late)

    def u64(kx, ks):
        return upd.at[rows(at(x, kx) * 512 + c * 256 + at(s, ks) * 64, 64)]

    def u256(kx, kc):
        return upd.at[rows(at(x, kx) * 512 + (1 - c if kc else c) * 256, 256)]

    for ks in (0, 1, 3, 2):
        for kz in (1, 2, 3, 0):
            if ks or kz:
                source = rows(base + place(4 - ks, 4 - kz), 16)
                recv(f"u{ks}{kz}", upd.at[source])
        for kx in (2, 1, 3):
            send(f"ux{kx}{ks}", u64(0, 4 - ks), u64(0, 4 - ks), dev(kx=kx))
    send("uc0", u256(0, 0), u256(0, 0), other)
    own = upd[rows(base, 256), :].astype(F32)
    sq[...] = jnp.sum((own * own).reshape(32, 8, COLS), axis=0)
    for k in (1, 3, 2):
        send(f"sy{k}", sq, ysq.at[3 - k], dev(km=k))

    for k in (1, 3, 2):
        recv(f"wc{k}", wpart(1 - c, 4 - k))
    for k in (1, 3, 2):
        recv(f"dy{k}", dr.at[at(m, 4 - k)])
    for j in range(4):
        weight = wide(*[wg[k, 512 * j : 512 * j + 512, :] for k in range(4)])
        part = dot_nt(wide(dr[0], dr[1], dr[2], dr[3]), weight)
        o_grad[0, :, 512 * j : 512 * j + 512] = part[:52].astype(BF)

    for k in (1, 3, 2):
        recv(f"sy{k}", ysq.at[3 - k])
    xs[...] = sq[...] + ysq[0] + ysq[1] + ysq[2]
    across = [(kx, kc) for kx in (2, 1, 3, 0) for kc in (1, 0) if kx or kc]
    for i, (kx, kc) in enumerate(across):
        send(f"sx{kx}{kc}", xs, xsq.at[i], dev(kx=kx, kc=kc))
    for kx in (1, 3, 2):
        for ks in (0, 1, 3, 2):
            recv(f"ux{kx}{ks}", u64(4 - kx, 4 - ks))
        send(f"uc{kx}", u256(4 - kx, 0), u256(4 - kx, 0), other)
    everything = xs[...]
    for i, (kx, kc) in enumerate(across):
        recv(f"sx{kx}{kc}", xsq.at[i])
        everything = everything + xsq[i]
    o_sq[...] = everything
    drain(len(sent) - 3)
    recv("uc0", u256(0, 1))
    for kx in (1, 3, 2):
        recv(f"uc{kx}", u256(4 - kx, 1))
    o_upd[...] = upd[...]
    drain(len(sent))


def write_results(grad_ref, raw_ref, sq_ref, o_grad, o_upd):
    o_grad[...] = grad_ref[...]
    scale = lax.rsqrt(jnp.sum(sq_ref[...]) / (D * 2 * HD) + 1e-06)
    o_upd[...] = (raw_ref[...].astype(F32) * scale).astype(BF)


def per_device(
    prefix_hidden, prefix_kv_weight, action_hidden, query_weight, action_kv_weight,
    out_cotangent, prompt_len, view_valid,
):
    vm = pltpu.VMEM
    scratch = [
        vm((ROWS, D), BF), vm((4, D, COLS), BF), vm((ACT, 1024), BF), vm((1024, 512), BF),
        vm((1024, 512), BF), vm((ACT, 512), BF), vm((4, 4, ROWS, COLS), BF), vm((ACTP, 512), BF),
        vm((QR, HD), BF), vm((QR, HD), BF), vm((HD, QR), BF), vm((HD, QR), BF),
        vm((4, ROWS, QR), F32), vm((4, ROWS, QR), F32),
        vm((4, 4, ROWS, COLS), F32), vm((4, 4, ROWS, COLS), BF),
        vm((4, 3, ROWS, COLS), BF),
        vm((ROWS, COLS), F32), vm((4, ROWS, COLS), BF),
        vm((112, COLS), BF), vm((96, COLS), BF), vm((112, COLS), BF), vm((96, COLS), BF),
        vm((112, COLS), BF), vm((96, COLS), BF),
        vm((ROWS, COLS), F32), vm((8 * ROWS, COLS), BF), vm((8 * ROWS, 256), BF),
        vm((256, 4 * ROWS), BF), vm((256, 4 * ROWS), BF), vm((256, COLS), F32), vm((256, COLS), BF),
        vm((15, 16, COLS), BF), vm((D, COLS), BF),
        vm((8, 128), F32), vm((3, 8, 128), F32), vm((8, 128), F32), vm((7, 8, 128), F32),
        vm((4, 64, COLS), BF), vm((4, 64, COLS), BF),
        pltpu.SMEM((1, VIEWS), jnp.int32),
        pltpu.SemaphoreType.DMA((8,)),
        pltpu.SemaphoreType.DMA((N_SEMS,)), pltpu.SemaphoreType.DMA((N_SEMS,)),
    ]
    smem = pl.BlockSpec(memory_space=pltpu.SMEM)
    hbm = pl.BlockSpec(memory_space=pltpu.HBM)
    grad, raw, squares = pl.pallas_call(
        kernel,
        out_shape=(
            jax.ShapeDtypeStruct((1, 52, D), BF),
            jax.ShapeDtypeStruct((D, COLS), BF),
            jax.ShapeDtypeStruct((8, 128), F32),
        ),
        in_specs=[smem] + [hbm] * 7,
        out_specs=(pl.BlockSpec(memory_space=pltpu.VMEM),) * 3,
        scratch_shapes=scratch,
        compiler_params=pltpu.CompilerParams(
            collective_id=0, has_side_effects=True, vmem_limit_bytes=40 * 1024 * 1024
        ),
    )(
        prompt_len, *[pltpu.with_memory_space_constraint(v, pltpu.HBM) for v in (view_valid, prefix_hidden, prefix_kv_weight, action_hidden, query_weight, action_kv_weight, out_cotangent)])
    return pl.pallas_call(
        write_results,
        out_shape=(
            jax.ShapeDtypeStruct((1, 52, D), BF),
            jax.ShapeDtypeStruct((D, COLS), BF),
        ),
        in_specs=[pl.BlockSpec(memory_space=pltpu.VMEM)] * 3,
        out_specs=(pl.BlockSpec(memory_space=pltpu.VMEM),) * 2,
        compiler_params=pltpu.CompilerParams(vmem_limit_bytes=40 * 1024 * 1024),
    )(grad, raw, squares)


def solution(mesh):
    return jax.shard_map(
        per_device,
        mesh=mesh,
        in_specs=(
            P("dp", "sample", None),
            P(None, "mp"),
            P("dp", "sample", None),
            P(None, "mp"),
            P(),
            P("dp", "sample", "mp"),
            P("dp"),
            P("dp", None),
        ),
        out_specs=(P("dp", ("sample", "mp"), None), P(None, "mp")),
        check_vma=False,
    )
```
